256 devices in a mesh: dp: 8 (over y_hi, x), cols: 32 (over z, y_lo, core).
Axes of the slice: x: 4, y: 4 (y_hi: 2, y_lo: 2; y = y_hi * 2 + y_lo), z: 8, core: 2. Of those that a mesh axis runs over, the one named last changes fastest.
Arguments:
- prefix_ids: int32 [8, 32, 32, 128], P('dp', 'cols'), may hold values from 0 to 65535, as said below
- suffix_ids: int32 [8, 32, 32, 128], P('dp', 'cols'), may hold values from 0 to 65535, as said below
- weights: float32 [8, 32, 32, 128], P('dp', 'cols'), may hold values from 0.25 to 36
- counts: int32 [8, 32, 32], P('dp', 'cols'), may hold values from 42 to 128, as said below
- omega: bfloat16 [65536, 512], P('cols'), may hold values from -6 to 6
Outputs:
- basis: float32 [65536, 512], P('cols')
- coefficients: float32 [512, 65536], P('dp', 'cols')
The draws below stay inside these ranges and needn't reach their ends.
Inputs may be any that keep to these rules, and one draw needn't show every extreme that they name: `prefix_ids`: the prefix ids of block (d, c, j) lie in [j * 2048, (j + 1) * 2048), on dead slots too. `suffix_ids`: the suffix ids of block (d, c, j) lie in [c * 2048, (c + 1) * 2048), on dead slots too. For every d some j has counts[d, c, j] = 128 for every c.
All inputs are finite; a program needn't handle non-finite values.
Results may differ from the reference program's by a relative error of at most 0.0028.
The reference program's roundings to bfloat16 on the way count: a program that leaves them out, or rounds other values in their place, can miss the bound.
Values may be sent and summed in bfloat16 or wider, within the bound.
A program may use at most 128 MiB of HBM per device.

```python
import math
import jax
import jax.numpy as jnp
from jax import lax

BLOCK = 2048
K = 512
SLOTS = 128
NP = 65536
NS = 65536
N_DP = 8
N_COLS = 32


def draw_prefix_ids(key, part):
    key = jax.random.fold_in(key, 11)
    shape = (N_DP, N_COLS, N_COLS, SLOTS)
    offsets = jax.random.randint(key, shape, 0, BLOCK)
    base = lax.broadcasted_iota(jnp.int32, shape, 2) * BLOCK
    return (base + offsets).astype(jnp.int32)


def draw_suffix_ids(key, part):
    key = jax.random.fold_in(key, 12)
    shape = (N_DP, N_COLS, N_COLS, SLOTS)
    offsets = jax.random.randint(key, shape, 0, BLOCK)
    base = lax.broadcasted_iota(jnp.int32, shape, 1) * BLOCK
    return (base + offsets).astype(jnp.int32)


def draw_counts(key, part):
    key = jax.random.fold_in(key, 13)
    first, second = jax.random.split(key)
    shape = (N_DP, N_COLS, N_COLS)
    base = jax.random.randint(first, shape, SLOTS // 3, SLOTS + 1)
    full_block = jax.random.randint(second, (N_DP, 1, 1), 0, N_COLS)
    column = lax.broadcasted_iota(jnp.int32, shape, 2)
    return jnp.where(column == full_block, SLOTS, base).astype(jnp.int32)


def draw_weights(key, part):
    key = jax.random.fold_in(key, 17)
    shape = (N_DP, N_COLS, N_COLS, SLOTS)
    group = lax.broadcasted_iota(jnp.int32, shape, 0)
    column = lax.broadcasted_iota(jnp.int32, shape, 1)
    place = (group * N_COLS + column).astype(jnp.float32) / float(N_DP * N_COLS - 1)
    base = jnp.exp(jax.random.uniform(key, shape, jnp.float32, math.log(0.25), math.log(4.0)))
    rise = 1.0 + 2.0 * place
    return (base * rise).astype(jnp.float32)


def level_of(rng, extent, cuts, least, high):
    def one(axis_at, blocks):
        heights = jax.random.uniform(jax.random.fold_in(jax.random.fold_in(rng, 6), axis_at), (blocks,), jnp.float32, least / len(cuts), high / len(cuts))
        return jnp.repeat(jnp.exp(heights), extent[axis_at] // blocks).reshape((-1,) + (1,) * (len(extent) - axis_at - 1))

    level = one(*cuts[0])
    for cut in cuts[1:]:
        level = level * one(*cut)
    return level


def noise(own_key, dims, scale, most, shards=(), held_as=jnp.bfloat16):
    drawn = scale * jax.random.normal(own_key, dims, jnp.float32)
    if shards:
        drawn = drawn * level_of(own_key, dims, shards, -0.22, 0.18)
    return jnp.clip(drawn, -most, most).astype(held_as)


def setup_inputs(seed: int = 0) -> dict:
    splits = jax.random.split(jax.random.key(seed), 6)
    return {
        "prefix_ids": draw_prefix_ids(jax.random.fold_in(splits[5], 71), 0),
        "suffix_ids": draw_suffix_ids(jax.random.fold_in(splits[5], 71), 0),
        "weights": draw_weights(jax.random.fold_in(splits[5], 71), 0),
        "counts": draw_counts(jax.random.fold_in(splits[5], 71), 0),
        "omega": noise(splits[4], (NS, K), 1.0, 6.0, ((0, 32),)),
    }


def gram_of(rows):
    return lax.dot_general(rows.astype(jnp.float32), rows.astype(jnp.float32), (((0,), (0,)), ((), ())), precision=lax.Precision.HIGHEST, preferred_element_type=jnp.float32)

def basis_from(rows, gram):
    lower = jnp.linalg.cholesky(gram)
    identity = jnp.eye(gram.shape[0], dtype=jnp.float32)
    inverse_factor = jax.scipy.linalg.solve_triangular(lower, identity, lower=True)
    return lax.dot_general(rows.astype(jnp.float32), inverse_factor.astype(jnp.float32), (((1,), (1,)), ((), ())), precision=lax.Precision.HIGHEST, preferred_element_type=jnp.float32)

def reference(prefix_ids, suffix_ids, weights, counts, omega):
    width = omega.shape[1]
    live = lax.broadcasted_iota(jnp.int32, prefix_ids.shape, 3) < counts[..., None]
    live_weights = jnp.where(live, weights, jnp.zeros_like(weights))
    mean_weight = jnp.sum(live_weights) / jnp.sum(live.astype(jnp.float32))
    pairs = N_DP * N_COLS
    prefix_all = prefix_ids.reshape(pairs, -1)
    suffix_all = suffix_ids.reshape(pairs, -1)
    weight_all = live_weights.reshape(pairs, -1)

    def add_sketch(total, items):
        prefix_row, suffix_row, weight_row = items
        rows = (weight_row[:, None] * omega[suffix_row].astype(jnp.float32)).astype(jnp.bfloat16)
        return (total.at[prefix_row].add(rows.astype(jnp.float32)), None)
    sketch, _ = lax.scan(add_sketch, jnp.zeros((NP, width), jnp.float32), (prefix_all, suffix_all, weight_all))
    gram = gram_of(sketch)
    q_full = basis_from(sketch, gram)
    basis = math.sqrt(NP) * q_full
    q_half = q_full.astype(jnp.bfloat16)

    def add_coef(total, items):
        prefix_row, suffix_row, weight_row = items
        terms = weight_row[:, None] * q_half[prefix_row].astype(jnp.float32)
        return (total.at[suffix_row].add(terms), None)
    coef_t, _ = lax.scan(add_coef, jnp.zeros((NS, width), jnp.float32), (prefix_all, suffix_all, weight_all))
    coefficients = math.sqrt(NP) / mean_weight * coef_t.T
    return (basis, coefficients)
```

```python
import functools
import math

import jax
import jax.numpy as jnp
from jax import lax
from jax.experimental import pallas as pl
from jax.experimental.pallas import tpu as pltpu
from jax.sharding import PartitionSpec as P

HIGHEST = lax.Precision.HIGHEST


def dot_exact(a, b, dims):
    return lax.dot_general(
        a, b, (dims, ((), ())), precision=HIGHEST, preferred_element_type=jnp.float32
    )


def one_hot(ids, size):
    rows = lax.broadcasted_iota(jnp.int32, (size, ids.shape[1]), 0)
    return jnp.where(rows == ids, 1.0, 0.0).astype(jnp.bfloat16)


def move_block(table, take, put, weight, width):
    size = table.shape[1]
    groups = table.shape[0] // width
    shift = size.bit_length() - 1
    beside = functools.partial(jnp.concatenate, axis=1)
    picked = jnp.dot(
        table,
        beside([one_hot(ids & (size - 1), size) for ids in take]),
        preferred_element_type=jnp.float32,
    )
    take_group = beside([lax.shift_right_logical(ids, shift) for ids in take])
    put_group = beside([lax.shift_right_logical(ids, shift) for ids in put])
    row = picked[:width]
    for g in range(1, groups):
        row = jnp.where(take_group == g, picked[g * width : (g + 1) * width], row)
    row = beside(weight) * row
    placed = jnp.concatenate(
        [jnp.where(put_group == g, row, 0.0).astype(jnp.bfloat16) for g in range(groups)], axis=0
    )
    spots = beside([one_hot(ids & (size - 1), size) for ids in put])
    return lax.dot_general(
        placed, spots, (((1,), (1,)), ((), ())), preferred_element_type=jnp.float32
    )


def move_kernel(width, table_ref, take_ref, put_ref, weight_ref, total_ref):
    @pl.when(pl.program_id(0) == 0)
    def _():
        total_ref[...] = jnp.zeros_like(total_ref)

    rows = range(take_ref.shape[1])
    total_ref[...] += move_block(
        table_ref[0],
        [take_ref[0, r : r + 1, :] for r in rows],
        [put_ref[0, r : r + 1, :] for r in rows],
        [weight_ref[0, r : r + 1, :] for r in rows],
        width,
    )


def move(name, tables, take, put, weight, width):
    blocks, stacked, size = tables.shape
    _, parts, slots = take.shape
    records = pl.BlockSpec((1, parts, slots), lambda i: (i, 0, 0))
    return pl.pallas_call(
        functools.partial(move_kernel, width),
        out_shape=jax.ShapeDtypeStruct((stacked, size), jnp.float32),
        grid=(blocks,),
        in_specs=[pl.BlockSpec((1, stacked, size), lambda i: (i, 0, 0)), records, records, records],
        out_specs=pl.BlockSpec((stacked, size), lambda i: (0, 0)),
        compiler_params=pltpu.CompilerParams(vmem_limit_bytes=40 * 2**20),
        name=name,
    )(tables, take, put, weight)


def shards(prefix_ids, suffix_ids, weights, counts, omega):
    ncols = lax.axis_size("cols")
    ndata = lax.axis_size("dp")
    block, width = omega.shape
    slots = prefix_ids.shape[-1]
    chunk = width // ndata
    size = block // ndata
    data_at = lax.axis_index("dp")

    live = lax.broadcasted_iota(jnp.int32, (ncols, slots), 1) < counts.reshape(ncols, 1)
    live_weights = jnp.where(live, weights.reshape(ncols, slots), 0.0)
    prefix_local = prefix_ids.reshape(ncols, slots) & (block - 1)
    suffix_local = suffix_ids.reshape(ncols, slots) & (block - 1)
    packed = prefix_local * block + suffix_local

    own = (packed, live_weights)
    here = [lax.all_to_all(x, "cols", split_axis=0, concat_axis=0, tiled=True) for x in own]
    here_ids, here_weights = [lax.all_gather(x, "dp", axis=1) for x in here]
    mine_ids, mine_weights = [lax.all_gather(x, "dp", axis=1) for x in own]
    live_rows, total_weight = lax.psum(
        (jnp.sum(live.astype(jnp.float32)), jnp.sum(live_weights)), ("dp", "cols")
    )

    part = lax.dynamic_slice_in_dim(omega, data_at * chunk, chunk, 1)
    part = part.reshape(ndata, size, chunk).swapaxes(1, 2).reshape(ndata * chunk, size)
    tables = lax.all_gather(part, "cols", axis=0)
    shift = block.bit_length() - 1
    sketch = move(
        "sketch", tables, here_ids & (block - 1), here_ids >> shift, here_weights, chunk
    )
    sketch_rows = lax.all_to_all(
        sketch.reshape(ndata, chunk, size), "dp", split_axis=0, concat_axis=0, tiled=True
    ).reshape(width, size)
    gram = lax.psum(dot_exact(sketch_rows, sketch_rows, ((1,), (1,))), ("dp", "cols"))
    lower = jnp.linalg.cholesky(gram)
    identity = jnp.eye(width, dtype=jnp.float32)
    inverse_factor = jax.scipy.linalg.solve_triangular(lower, identity, lower=True)
    q_part = dot_exact(inverse_factor, sketch_rows, ((1,), (0,)))
    scale = math.sqrt(block * ncols)
    basis = lax.all_gather(scale * q_part.T, "dp", axis=0, tiled=True)

    q_half = q_part.astype(jnp.bfloat16).reshape(ndata, chunk, size)
    q_chunk = lax.all_to_all(q_half, "dp", split_axis=0, concat_axis=0, tiled=True)
    q_tables = lax.all_gather(q_chunk.reshape(width, size), "cols", axis=0)
    sums = move(
        "project", q_tables, mine_ids >> shift, mine_ids & (block - 1), mine_weights, chunk
    )
    sums = sums.reshape(ndata, chunk, size).swapaxes(0, 1).reshape(chunk, block)
    coefficients = (scale * live_rows / total_weight) * sums
    return (basis, coefficients)


def solution(mesh):
    placed = (
        P("dp", "cols", None, None),
        P("dp", "cols", None, None),
        P("dp", "cols", None, None),
        P("dp", "cols", None),
        P("cols", None),
    )
    return jax.shard_map(
        shards,
        mesh=mesh,
        in_specs=placed,
        out_specs=(P("cols", None), P("dp", "cols")),
        check_vma=False,
    )
```

```python
import functools
import math

import jax
import jax.numpy as jnp
from jax import lax
from jax.experimental import pallas as pl
from jax.experimental.pallas import tpu as pltpu
from jax.sharding import PartitionSpec as P

HIGHEST = lax.Precision.HIGHEST


def dot_exact(a, b, dims):
    return lax.dot_general(
        a, b, (dims, ((), ())), precision=HIGHEST, preferred_element_type=jnp.float32
    )


def one_hot(ids, size):
    rows = lax.broadcasted_iota(jnp.int32, (size, ids.shape[1]), 0)
    return jnp.where(rows == ids, 1.0, 0.0).astype(jnp.bfloat16)


def move_block(table, take, put, weight, width):
    size = table.shape[1]
    groups = table.shape[0] // width
    shift = size.bit_length() - 1
    beside = functools.partial(jnp.concatenate, axis=1)
    picked = jnp.dot(
        table,
        beside([one_hot(ids & (size - 1), size) for ids in take]),
        preferred_element_type=jnp.float32,
    )
    take_group = beside([lax.shift_right_logical(ids, shift) for ids in take])
    put_group = beside([lax.shift_right_logical(ids, shift) for ids in put])
    row = picked[:width]
    for g in range(1, groups):
        row = jnp.where(take_group == g, picked[g * width : (g + 1) * width], row)
    row = beside(weight) * row
    placed = jnp.concatenate(
        [jnp.where(put_group == g, row, 0.0).astype(jnp.bfloat16) for g in range(groups)], axis=0
    )
    spots = beside([one_hot(ids & (size - 1), size) for ids in put])
    return lax.dot_general(
        placed, spots, (((1,), (1,)), ((), ())), preferred_element_type=jnp.float32
    )


def move_kernel(width, table_ref, take_ref, put_ref, weight_ref, total_ref):
    @pl.when(pl.program_id(0) == 0)
    def _():
        total_ref[...] = jnp.zeros_like(total_ref)

    rows = range(take_ref.shape[1])
    total_ref[...] += move_block(
        table_ref[0],
        [take_ref[0, r : r + 1, :] for r in rows],
        [put_ref[0, r : r + 1, :] for r in rows],
        [weight_ref[0, r : r + 1, :] for r in rows],
        width,
    )


def move(name, tables, take, put, weight, width):
    blocks, stacked, size = tables.shape
    _, parts, slots = take.shape
    records = pl.BlockSpec((1, parts, slots), lambda i: (i, 0, 0))
    return pl.pallas_call(
        functools.partial(move_kernel, width),
        out_shape=jax.ShapeDtypeStruct((stacked, size), jnp.float32),
        grid=(blocks,),
        in_specs=[pl.BlockSpec((1, stacked, size), lambda i: (i, 0, 0)), records, records, records],
        out_specs=pl.BlockSpec((stacked, size), lambda i: (0, 0)),
        compiler_params=pltpu.CompilerParams(vmem_limit_bytes=40 * 2**20),
        name=name,
    )(tables, take, put, weight)


def vmem():
    return pl.BlockSpec(memory_space=pltpu.VMEM)


def put_copy(src, dst, send, recv, axis, peer):
    return pltpu.make_async_remote_copy(
        src_ref=src,
        dst_ref=dst,
        send_sem=send,
        recv_sem=recv,
        device_id={axis: peer},
        device_id_type=pl.DeviceIdType.MESH,
    )


def over_peers(axis, act):
    count = lax.axis_size(axis)
    me = lax.axis_index(axis)

    def one(offset, carry):
        act(offset, lax.rem(me + offset, count))
        return carry

    lax.fori_loop(1, count, one, 0)


def greet(*axes):
    barrier = pltpu.get_barrier_semaphore()
    for axis in axes:
        over_peers(
            axis,
            lambda offset, peer, axis=axis: pl.semaphore_signal(
                barrier, inc=1, device_id={axis: peer}, device_id_type=pl.DeviceIdType.MESH
            ),
        )
    pl.semaphore_wait(barrier, sum(lax.axis_size(axis) - 1 for axis in axes))


def exchange(axis, make):
    over_peers(axis, lambda offset, peer: make(offset, peer).start())
    over_peers(axis, lambda offset, peer: make(offset, peer).wait())


def records_kernel(own_ref, here_ref, mine_ref, col_sems, here_sems, mine_sems):
    data_at, col_at = lax.axis_index("dp"), lax.axis_index("cols")
    greet("cols", "dp")

    def to_col(offset, peer):
        return put_copy(
            own_ref.at[peer],
            here_ref.at[data_at, col_at],
            col_sems.at[0, offset],
            col_sems.at[1, offset],
            "cols",
            peer,
        )

    def own_to_data(offset, peer):
        return put_copy(
            own_ref,
            mine_ref.at[data_at],
            mine_sems.at[0, offset],
            mine_sems.at[1, offset],
            "dp",
            peer,
        )

    def here_to_data(offset, peer):
        return put_copy(
            here_ref.at[data_at],
            here_ref.at[data_at],
            here_sems.at[0, offset],
            here_sems.at[1, offset],
            "dp",
            peer,
        )

    over_peers("cols", lambda offset, peer: to_col(offset, peer).start())
    over_peers("dp", lambda offset, peer: own_to_data(offset, peer).start())
    here_ref[data_at, col_at] = own_ref[col_at]
    mine_ref[data_at] = own_ref[...]
    over_peers("cols", lambda offset, peer: to_col(offset, peer).wait())
    exchange("dp", here_to_data)
    over_peers("dp", lambda offset, peer: own_to_data(offset, peer).wait())


def exchange_records(own):
    ndata, ncols = lax.axis_size("dp"), lax.axis_size("cols")
    gathered = jax.ShapeDtypeStruct((ndata, *own.shape), own.dtype)
    return pl.pallas_call(
        records_kernel,
        out_shape=(gathered, gathered),
        in_specs=[vmem()],
        out_specs=(vmem(), vmem()),
        scratch_shapes=[
            pltpu.SemaphoreType.DMA((2, ncols)),
            pltpu.SemaphoreType.DMA((2, ndata)),
            pltpu.SemaphoreType.DMA((2, ndata)),
        ],
        compiler_params=pltpu.CompilerParams(collective_id=0, has_side_effects=True),
        name="records",
    )(own)


def gram_kernel(
    sketch_ref,
    weight_ref,
    rows_ref,
    gram_ref,
    totals_ref,
    part_ref,
    got_ref,
    piece_ref,
    arrived_ref,
    shared_ref,
    rows_sems,
    part_sems,
    piece_sems,
    shared_sems,
    gram_sems,
):
    data_at, col_at = lax.axis_index("dp"), lax.axis_index("cols")
    ndata, chunk, size = sketch_ref.shape
    width = ndata * chunk
    lanes = piece_ref.shape[2]
    across = width // lanes
    greet("cols", "dp")

    def rows_copy(offset, peer):
        return put_copy(
            sketch_ref.at[peer],
            rows_ref.at[data_at],
            rows_sems.at[0, offset],
            rows_sems.at[1, offset],
            "dp",
            peer,
        )

    over_peers("dp", lambda offset, peer: rows_copy(offset, peer).start())
    rows_ref[data_at] = sketch_ref[data_at]
    over_peers("dp", lambda offset, peer: rows_copy(offset, peer).wait())
    rows = rows_ref[...].reshape(width, size)
    part_ref[...] = dot_exact(rows, rows, ((1,), (1,))).reshape(part_ref.shape)

    def part_copy(offset, peer):
        return put_copy(
            part_ref.at[peer],
            got_ref.at[data_at],
            part_sems.at[0, offset],
            part_sems.at[1, offset],
            "dp",
            peer,
        )

    over_peers("dp", lambda offset, peer: part_copy(offset, peer).start())
    got_ref[data_at] = part_ref[data_at]
    over_peers("dp", lambda offset, peer: part_copy(offset, peer).wait())
    summed = got_ref[0]
    for d in range(1, ndata):
        summed = summed + got_ref[d]
    for at in range(piece_ref.shape[0]):
        r, l = divmod(at, across)
        piece_ref[at] = summed[8 * r : 8 * r + 8, lanes * l : lanes * (l + 1)]

    def piece_copy(offset, peer):
        return put_copy(
            piece_ref.at[peer],
            arrived_ref.at[col_at],
            piece_sems.at[0, offset],
            piece_sems.at[1, offset],
            "cols",
            peer,
        )

    over_peers("cols", lambda offset, peer: piece_copy(offset, peer).start())
    arrived_ref[col_at] = piece_ref[col_at]
    weight = weight_ref[...]
    shared_ref[col_at, 1] = jnp.sum(weight, axis=0)
    shared_ref[col_at, 2] = jnp.sum((weight > 0.0).astype(jnp.float32), axis=0)
    over_peers("cols", lambda offset, peer: piece_copy(offset, peer).wait())
    shared_ref[col_at, 0] = jnp.sum(arrived_ref[...], axis=0)

    def shared_copy(offset, peer):
        return put_copy(
            shared_ref.at[col_at],
            shared_ref.at[col_at],
            shared_sems.at[0, offset],
            shared_sems.at[1, offset],
            "cols",
            peer,
        )

    exchange("cols", shared_copy)
    for r in range(chunk // 8):
        row = [shared_ref[r * across + l, 0] for l in range(across)]
        gram_ref[data_at, pl.ds(8 * r, 8), :] = jnp.concatenate(row, axis=1)

    def gram_copy(offset, peer):
        return put_copy(
            gram_ref.at[data_at],
            gram_ref.at[data_at],
            gram_sems.at[0, offset],
            gram_sems.at[1, offset],
            "dp",
            peer,
        )

    over_peers("dp", lambda offset, peer: gram_copy(offset, peer).start())
    totals_ref[0] = jnp.sum(shared_ref[:, 1], axis=0)
    totals_ref[1] = jnp.sum(shared_ref[:, 2], axis=0)
    over_peers("dp", lambda offset, peer: gram_copy(offset, peer).wait())


def sum_gram(sketch, weights):
    ndata, chunk, size = sketch.shape
    ncols = lax.axis_size("cols")
    width = ndata * chunk
    f32 = jnp.float32
    tile = weights.shape[1:]
    assert ncols * tile[0] * tile[1] == chunk * width
    dma = pltpu.SemaphoreType.DMA
    return pl.pallas_call(
        gram_kernel,
        out_shape=(
            jax.ShapeDtypeStruct((ndata, chunk, size), f32),
            jax.ShapeDtypeStruct((ndata, chunk, width), f32),
            jax.ShapeDtypeStruct((2, *tile), f32),
        ),
        in_specs=[vmem(), vmem()],
        out_specs=(vmem(), vmem(), vmem()),
        scratch_shapes=[
            pltpu.VMEM((ndata, chunk, width), f32),
            pltpu.VMEM((ndata, chunk, width), f32),
            pltpu.VMEM((ncols, *tile), f32),
            pltpu.VMEM((ncols, *tile), f32),
            pltpu.VMEM((ncols, 3, *tile), f32),
            dma((2, ndata)),
            dma((2, ndata)),
            dma((2, ncols)),
            dma((2, ncols)),
            dma((2, ndata)),
        ],
        compiler_params=pltpu.CompilerParams(
            collective_id=1, has_side_effects=True, vmem_limit_bytes=24 * 2**20
        ),
        name="gram",
    )(sketch, weights)


def corner_inverse(tile, pivots=8):
    n = tile.shape[0]
    blocks = n // pivots

    def full(x):
        return jnp.broadcast_to(x, (pivots, n))

    work = [tile[pivots * i : pivots * (i + 1), :] for i in range(blocks)]
    lane = lax.broadcasted_iota(jnp.int32, (pivots, n), 1)
    sub = lax.broadcasted_iota(jnp.int32, (pivots, n), 0)
    done = []
    for at in range(blocks):
        start = at * pivots
        group = (lane >= start) & (lane < start + pivots)
        cols = [full(work[at][:, start + c : start + c + 1]) for c in range(pivots)]
        left = [[full(cols[c][r : r + 1, :]) for c in range(r + 1)] for r in range(pivots)]
        rows = [
            jnp.where(group, jnp.where(lane == start + r, 1.0, 0.0), full(work[at][r : r + 1, :]))
            for r in range(pivots)
        ]
        recip = [None] * pivots
        low = [[None] * pivots for _ in range(pivots)]
        for c in range(pivots):
            recip[c] = 1.0 / left[c][c]
            for r in range(c + 1, pivots):
                low[r][c] = left[r][c] * recip[c]
                for e in range(c + 1, r + 1):
                    left[r][e] = left[r][e] - low[r][c] * left[e][c]
        for r in range(pivots):
            for c in range(r):
                rows[r] = rows[r] - low[r][c] * rows[c]
        result = jnp.zeros((pivots, n), jnp.float32)
        for r in range(pivots):
            result = jnp.where(sub == r, rows[r] * lax.rsqrt(left[r][r]), result)
        done.append(jnp.where(lane <= sub + start, result, 0.0))
        back = [rows[r] * recip[r] for r in range(pivots)]
        for r in range(pivots - 1, -1, -1):
            for c in range(r):
                back[c] = back[c] - low[r][c] * back[r]
        for i in range(at + 1, blocks):
            rest = jnp.where(group, 0.0, work[i])
            for c in range(pivots):
                rest = rest - full(work[i][:, start + c : start + c + 1]) * back[c]
            work[i] = rest
    return jnp.concatenate(done, axis=0)


def factor_kernel(scale, corner_size, gram_ref, rows_ref, basis_ref, half_ref, work_ref, inverse_ref):
    n = gram_ref.shape[0]
    work_ref[...] = gram_ref[...]
    row_at = lax.broadcasted_iota(jnp.int32, (n, n), 0)
    col_at = lax.broadcasted_iota(jnp.int32, (n, n), 1)
    inverse_ref[...] = jnp.where(row_at == col_at, 1.0, 0.0)

    def step(k, carry):
        at = pl.ds(pl.multiple_of(k * corner_size, corner_size), corner_size)
        corner = corner_inverse(work_ref[at, at])
        row = dot_exact(corner, inverse_ref[at, :], ((1,), (0,)))
        low = dot_exact(work_ref[:, at], corner, ((1,), (1,)))
        below = lax.broadcasted_iota(jnp.int32, low.shape, 0) >= (k + 1) * corner_size
        low = jnp.where(below, low, 0.0)
        work_ref[...] -= dot_exact(low, low, ((1,), (1,)))
        inverse_ref[...] -= dot_exact(low, row, ((1,), (0,)))
        inverse_ref[at, :] = row
        return carry

    lax.fori_loop(0, n // corner_size, step, 0)
    q = dot_exact(inverse_ref[...], rows_ref[...], ((1,), (0,)))
    half_ref[...] = q.astype(jnp.bfloat16)
    basis_ref[...] = scale * q.T


def factor_and_q(gram, rows, scale):
    width, size = rows.shape
    return pl.pallas_call(
        functools.partial(factor_kernel, scale, 128),
        out_shape=(
            jax.ShapeDtypeStruct((size, width), jnp.float32),
            jax.ShapeDtypeStruct((width, size), jnp.bfloat16),
        ),
        in_specs=[vmem(), vmem()],
        out_specs=(vmem(), vmem()),
        scratch_shapes=[pltpu.VMEM((width, width), jnp.float32)] * 2,
        compiler_params=pltpu.CompilerParams(vmem_limit_bytes=24 * 2**20),
        name="factor",
    )(gram, rows)


def shards(prefix_ids, suffix_ids, weights, counts, omega):
    ncols = lax.axis_size("cols")
    ndata = lax.axis_size("dp")
    block, width = omega.shape
    slots = prefix_ids.shape[-1]
    chunk = width // ndata
    size = block // ndata
    data_at = lax.axis_index("dp")

    live = lax.broadcasted_iota(jnp.int32, (ncols, slots), 1) < counts.reshape(ncols, 1)
    live_weights = jnp.where(live, weights.reshape(ncols, slots), 0.0)
    prefix_local = prefix_ids.reshape(ncols, slots) & (block - 1)
    suffix_local = suffix_ids.reshape(ncols, slots) & (block - 1)
    packed = prefix_local * block + suffix_local
    own = jnp.stack([packed.astype(jnp.float32), live_weights], axis=1)
    here, mine = exchange_records(own)
    here_ids, here_weights = here[:, :, 0].astype(jnp.int32).swapaxes(0, 1), here[:, :, 1].swapaxes(0, 1)
    mine_ids, mine_weights = mine[:, :, 0].astype(jnp.int32).swapaxes(0, 1), mine[:, :, 1].swapaxes(0, 1)

    part = lax.dynamic_slice_in_dim(omega, data_at * chunk, chunk, 1)
    part = part.reshape(ndata, size, chunk).swapaxes(1, 2).reshape(ndata * chunk, size)
    tables = lax.all_gather(part, "cols", axis=0)
    shift = block.bit_length() - 1
    sketch = move(
        "sketch", tables, here_ids & (block - 1), here_ids >> shift, here_weights, chunk
    )
    rows, gram, totals = sum_gram(sketch.reshape(ndata, chunk, size), mine_weights)
    scale = math.sqrt(block * ncols)
    basis_part, q_half = factor_and_q(gram.reshape(width, width), rows.reshape(width, size), scale)
    basis = lax.all_gather(basis_part, "dp", axis=0, tiled=True)

    q_half = q_half.reshape(ndata, chunk, size)
    q_chunk = lax.all_to_all(q_half, "dp", split_axis=0, concat_axis=0, tiled=True)
    q_tables = lax.all_gather(q_chunk.reshape(width, size), "cols", axis=0)
    sums = move(
        "project", q_tables, mine_ids >> shift, mine_ids & (block - 1), mine_weights, chunk
    )
    sums = sums.reshape(ndata, chunk, size).swapaxes(0, 1).reshape(chunk, block)
    coefficients = (scale * jnp.sum(totals[1]) / jnp.sum(totals[0])) * sums
    return (basis, coefficients)


def solution(mesh):
    placed = (
        P("dp", "cols", None, None),
        P("dp", "cols", None, None),
        P("dp", "cols", None, None),
        P("dp", "cols", None),
        P("cols", None),
    )
    return jax.shard_map(
        shards,
        mesh=mesh,
        in_specs=placed,
        out_specs=(P("cols", None), P("dp", "cols")),
        check_vma=False,
    )
```

```python
import functools
import math

import jax
import jax.numpy as jnp
from jax import lax
from jax.experimental import pallas as pl
from jax.experimental.pallas import tpu as pltpu
from jax.sharding import PartitionSpec as P

HIGHEST = lax.Precision.HIGHEST


def dot_exact(a, b, dims):
    return lax.dot_general(
        a, b, (dims, ((), ())), precision=HIGHEST, preferred_element_type=jnp.float32
    )


def one_hot(ids, size):
    rows = lax.broadcasted_iota(jnp.int32, (size, ids.shape[1]), 0)
    return jnp.where(rows == ids, 1.0, 0.0).astype(jnp.bfloat16)


def move_block(table, take, put, weight, width):
    size = table.shape[1]
    groups = table.shape[0] // width
    shift = size.bit_length() - 1
    beside = functools.partial(jnp.concatenate, axis=1)
    picked = jnp.dot(
        table,
        beside([one_hot(ids & (size - 1), size) for ids in take]),
        preferred_element_type=jnp.float32,
    )
    take_group = beside([lax.shift_right_logical(ids, shift) for ids in take])
    put_group = beside([lax.shift_right_logical(ids, shift) for ids in put])
    row = picked[:width]
    for g in range(1, groups):
        row = jnp.where(take_group == g, picked[g * width : (g + 1) * width], row)
    row = beside(weight) * row
    placed = jnp.concatenate(
        [jnp.where(put_group == g, row, 0.0).astype(jnp.bfloat16) for g in range(groups)], axis=0
    )
    spots = beside([one_hot(ids & (size - 1), size) for ids in put])
    return lax.dot_general(
        placed, spots, (((1,), (1,)), ((), ())), preferred_element_type=jnp.float32
    )


def vmem():
    return pl.BlockSpec(memory_space=pltpu.VMEM)


def put_copy(src, dst, send, recv, axis, peer):
    return pltpu.make_async_remote_copy(
        src_ref=src,
        dst_ref=dst,
        send_sem=send,
        recv_sem=recv,
        device_id={axis: peer},
        device_id_type=pl.DeviceIdType.MESH,
    )


def over_peers(axis, act):
    count = lax.axis_size(axis)
    me = lax.axis_index(axis)

    def one(offset, carry):
        act(offset, lax.rem(me + offset, count))
        return carry

    lax.fori_loop(1, count, one, 0)


def greet(*axes):
    barrier = pltpu.get_barrier_semaphore()
    for axis in axes:
        over_peers(
            axis,
            lambda offset, peer, axis=axis: pl.semaphore_signal(
                barrier, inc=1, device_id={axis: peer}, device_id_type=pl.DeviceIdType.MESH
            ),
        )
    pl.semaphore_wait(barrier, sum(lax.axis_size(axis) - 1 for axis in axes))


def exchange(axis, make):
    over_peers(axis, lambda offset, peer: make(offset, peer).start())
    over_peers(axis, lambda offset, peer: make(offset, peer).wait())


def records_kernel(own_ref, here_ref, mine_ref, col_sems, here_sems, mine_sems):
    data_at, col_at = lax.axis_index("dp"), lax.axis_index("cols")
    greet("cols", "dp")

    def to_col(offset, peer):
        return put_copy(
            own_ref.at[peer],
            here_ref.at[data_at, col_at],
            col_sems.at[0, offset],
            col_sems.at[1, offset],
            "cols",
            peer,
        )

    def own_to_data(offset, peer):
        return put_copy(
            own_ref,
            mine_ref.at[data_at],
            mine_sems.at[0, offset],
            mine_sems.at[1, offset],
            "dp",
            peer,
        )

    def here_to_data(offset, peer):
        return put_copy(
            here_ref.at[data_at],
            here_ref.at[data_at],
            here_sems.at[0, offset],
            here_sems.at[1, offset],
            "dp",
            peer,
        )

    over_peers("cols", lambda offset, peer: to_col(offset, peer).start())
    over_peers("dp", lambda offset, peer: own_to_data(offset, peer).start())
    here_ref[data_at, col_at] = own_ref[col_at]
    mine_ref[data_at] = own_ref[...]
    over_peers("cols", lambda offset, peer: to_col(offset, peer).wait())
    exchange("dp", here_to_data)
    over_peers("dp", lambda offset, peer: own_to_data(offset, peer).wait())


def exchange_records(own):
    ndata, ncols = lax.axis_size("dp"), lax.axis_size("cols")
    gathered = jax.ShapeDtypeStruct((ndata, *own.shape), own.dtype)
    return pl.pallas_call(
        records_kernel,
        out_shape=(gathered, gathered),
        in_specs=[vmem()],
        out_specs=(vmem(), vmem()),
        scratch_shapes=[
            pltpu.SemaphoreType.DMA((2, ncols)),
            pltpu.SemaphoreType.DMA((2, ndata)),
            pltpu.SemaphoreType.DMA((2, ndata)),
        ],
        compiler_params=pltpu.CompilerParams(collective_id=0, has_side_effects=True),
        name="records",
    )(own)


def gram_kernel(
    sketch_ref,
    mine_ref,
    rows_ref,
    gram_ref,
    totals_ref,
    part_ref,
    got_ref,
    piece_ref,
    arrived_ref,
    shared_ref,
    rows_sems,
    part_sems,
    piece_sems,
    shared_sems,
    gram_sems,
):
    data_at, col_at = lax.axis_index("dp"), lax.axis_index("cols")
    ndata, chunk, size = sketch_ref.shape
    width = ndata * chunk
    lanes = piece_ref.shape[2]
    across = width // lanes
    greet("cols", "dp")

    def rows_copy(offset, peer):
        return put_copy(
            sketch_ref.at[peer],
            rows_ref.at[data_at],
            rows_sems.at[0, offset],
            rows_sems.at[1, offset],
            "dp",
            peer,
        )

    over_peers("dp", lambda offset, peer: rows_copy(offset, peer).start())
    rows_ref[data_at] = sketch_ref[data_at]
    over_peers("dp", lambda offset, peer: rows_copy(offset, peer).wait())
    rows = rows_ref[...].reshape(width, size)
    part_ref[...] = dot_exact(rows, rows, ((1,), (1,))).reshape(part_ref.shape)

    def part_copy(offset, peer):
        return put_copy(
            part_ref.at[peer],
            got_ref.at[data_at],
            part_sems.at[0, offset],
            part_sems.at[1, offset],
            "dp",
            peer,
        )

    over_peers("dp", lambda offset, peer: part_copy(offset, peer).start())
    got_ref[data_at] = part_ref[data_at]
    over_peers("dp", lambda offset, peer: part_copy(offset, peer).wait())
    summed = got_ref[0]
    for d in range(1, ndata):
        summed = summed + got_ref[d]
    for at in range(piece_ref.shape[0]):
        r, l = divmod(at, across)
        piece_ref[at] = summed[8 * r : 8 * r + 8, lanes * l : lanes * (l + 1)]

    def piece_copy(offset, peer):
        return put_copy(
            piece_ref.at[peer],
            arrived_ref.at[col_at],
            piece_sems.at[0, offset],
            piece_sems.at[1, offset],
            "cols",
            peer,
        )

    over_peers("cols", lambda offset, peer: piece_copy(offset, peer).start())
    arrived_ref[col_at] = piece_ref[col_at]
    weight = mine_ref[:, :, 1, :]
    for at, term in ((1, weight), (2, (weight > 0.0).astype(jnp.float32))):
        term = jnp.sum(term, axis=0).reshape(-1, *shared_ref.shape[2:])
        shared_ref[col_at, at] = jnp.sum(term, axis=0)
    over_peers("cols", lambda offset, peer: piece_copy(offset, peer).wait())
    shared_ref[col_at, 0] = jnp.sum(arrived_ref[...], axis=0)

    def shared_copy(offset, peer):
        return put_copy(
            shared_ref.at[col_at],
            shared_ref.at[col_at],
            shared_sems.at[0, offset],
            shared_sems.at[1, offset],
            "cols",
            peer,
        )

    exchange("cols", shared_copy)
    for r in range(chunk // 8):
        row = [shared_ref[r * across + l, 0] for l in range(across)]
        gram_ref[data_at, pl.ds(8 * r, 8), :] = jnp.concatenate(row, axis=1)

    def gram_copy(offset, peer):
        return put_copy(
            gram_ref.at[data_at],
            gram_ref.at[data_at],
            gram_sems.at[0, offset],
            gram_sems.at[1, offset],
            "dp",
            peer,
        )

    over_peers("dp", lambda offset, peer: gram_copy(offset, peer).start())
    totals_ref[0] = jnp.sum(shared_ref[:, 1], axis=0)
    totals_ref[1] = jnp.sum(shared_ref[:, 2], axis=0)
    over_peers("dp", lambda offset, peer: gram_copy(offset, peer).wait())


def sum_gram(sketch, mine):
    ndata, chunk, size = sketch.shape
    ncols = lax.axis_size("cols")
    width = ndata * chunk
    f32 = jnp.float32
    tile = (8, mine.shape[-1])
    assert ncols * tile[0] * tile[1] == chunk * width
    dma = pltpu.SemaphoreType.DMA
    return pl.pallas_call(
        gram_kernel,
        out_shape=(
            jax.ShapeDtypeStruct((ndata, chunk, size), f32),
            jax.ShapeDtypeStruct((ndata, chunk, width), f32),
            jax.ShapeDtypeStruct((2, *tile), f32),
        ),
        in_specs=[vmem(), vmem()],
        out_specs=(vmem(), vmem(), vmem()),
        scratch_shapes=[
            pltpu.VMEM((ndata, chunk, width), f32),
            pltpu.VMEM((ndata, chunk, width), f32),
            pltpu.VMEM((ncols, *tile), f32),
            pltpu.VMEM((ncols, *tile), f32),
            pltpu.VMEM((ncols, 3, *tile), f32),
            dma((2, ndata)),
            dma((2, ndata)),
            dma((2, ncols)),
            dma((2, ncols)),
            dma((2, ndata)),
        ],
        compiler_params=pltpu.CompilerParams(
            collective_id=1, has_side_effects=True, vmem_limit_bytes=24 * 2**20
        ),
        name="gram",
    )(sketch, mine)


def corner_inverse(tile, pivots=8):
    n = tile.shape[0]
    blocks = n // pivots

    def full(x):
        return jnp.broadcast_to(x, (pivots, n))

    work = [tile[pivots * i : pivots * (i + 1), :] for i in range(blocks)]
    lane = lax.broadcasted_iota(jnp.int32, (pivots, n), 1)
    sub = lax.broadcasted_iota(jnp.int32, (pivots, n), 0)
    done = []
    for at in range(blocks):
        start = at * pivots
        group = (lane >= start) & (lane < start + pivots)
        cols = [full(work[at][:, start + c : start + c + 1]) for c in range(pivots)]
        left = [[full(cols[c][r : r + 1, :]) for c in range(r + 1)] for r in range(pivots)]
        rows = [
            jnp.where(group, jnp.where(lane == start + r, 1.0, 0.0), full(work[at][r : r + 1, :]))
            for r in range(pivots)
        ]
        recip = [None] * pivots
        low = [[None] * pivots for _ in range(pivots)]
        for c in range(pivots):
            recip[c] = 1.0 / left[c][c]
            for r in range(c + 1, pivots):
                low[r][c] = left[r][c] * recip[c]
                for e in range(c + 1, r + 1):
                    left[r][e] = left[r][e] - low[r][c] * left[e][c]
        for r in range(pivots):
            for c in range(r):
                rows[r] = rows[r] - low[r][c] * rows[c]
        result = jnp.zeros((pivots, n), jnp.float32)
        for r in range(pivots):
            result = jnp.where(sub == r, rows[r] * lax.rsqrt(left[r][r]), result)
        done.append(jnp.where(lane <= sub + start, result, 0.0))
        back = [rows[r] * recip[r] for r in range(pivots)]
        for r in range(pivots - 1, -1, -1):
            for c in range(r):
                back[c] = back[c] - low[r][c] * back[r]
        for i in range(at + 1, blocks):
            rest = jnp.where(group, 0.0, work[i])
            for c in range(pivots):
                rest = rest - full(work[i][:, start + c : start + c + 1]) * back[c]
            work[i] = rest
    return jnp.concatenate(done, axis=0)


def factor_kernel(corner_size, gram_ref, rows_ref, basis_ref, half_ref, work_ref, inverse_ref):
    n = gram_ref.shape[0]
    work_ref[...] = gram_ref[...]
    row_at = lax.broadcasted_iota(jnp.int32, (n, n), 0)
    col_at = lax.broadcasted_iota(jnp.int32, (n, n), 1)
    inverse_ref[...] = jnp.where(row_at == col_at, 1.0, 0.0)

    def step(k, carry):
        at = pl.ds(pl.multiple_of(k * corner_size, corner_size), corner_size)
        corner = corner_inverse(work_ref[at, at])
        row = dot_exact(corner, inverse_ref[at, :], ((1,), (0,)))
        low = dot_exact(work_ref[:, at], corner, ((1,), (1,)))
        below = lax.broadcasted_iota(jnp.int32, low.shape, 0) >= (k + 1) * corner_size
        low = jnp.where(below, low, 0.0)
        work_ref[...] -= dot_exact(low, low, ((1,), (1,)))
        inverse_ref[...] -= dot_exact(low, row, ((1,), (0,)))
        inverse_ref[at, :] = row
        return carry

    lax.fori_loop(0, n // corner_size, step, 0)
    q = dot_exact(inverse_ref[...], rows_ref[...], ((1,), (0,)))
    half_ref[...] = q.astype(jnp.bfloat16)
    basis_ref[...] = q.T.astype(jnp.bfloat16)


def factor_and_q(gram, rows):
    width, size = rows.shape
    return pl.pallas_call(
        functools.partial(factor_kernel, 128),
        out_shape=(
            jax.ShapeDtypeStruct((size, width), jnp.bfloat16),
            jax.ShapeDtypeStruct((width, size), jnp.bfloat16),
        ),
        in_specs=[vmem(), vmem()],
        out_specs=(vmem(), vmem()),
        scratch_shapes=[pltpu.VMEM((width, width), jnp.float32)] * 2,
        compiler_params=pltpu.CompilerParams(vmem_limit_bytes=24 * 2**20),
        name="factor",
    )(gram, rows)


class Ring:
    def __init__(self, all_ref, got_sems, ring_sems, pair_sems, across_sem):
        self.all_ref, self.got_sems = all_ref, got_sems
        self.ring_sems, self.pair_sems, self.across_sem = ring_sems, pair_sems, across_sem
        at = lax.axis_index("cols")
        self.length = lax.axis_size("cols") // 4
        self.z, quad = at // 4, lax.rem(at, 4)
        self.y, self.core = quad // 2, lax.rem(quad, 2)
        self.way = 1 - 2 * self.core
        self.pair = self.device(self.z, self.y, 1 - self.core)
        self.across = self.device(self.z, 1 - self.y, self.core)
        self.after = self.device(self.z + self.way, self.y, self.core)
        self.before = self.device(self.z - self.way, self.y, self.core)

    def device(self, z, y, core):
        z = lax.rem(z + self.length, self.length)
        return z * 4 + y * 2 + core

    def quad_slot(self, z, turn, core):
        y = lax.rem(self.y + lax.rem(turn, 2), 2)
        return self.device(z, y, lax.rem(core + turn // 2, 2))

    def greet(self, others=()):
        barrier = pltpu.get_barrier_semaphore()
        for peer in (self.pair, self.across, self.after, self.before):
            pl.semaphore_signal(
                barrier, inc=1, device_id={"cols": peer}, device_id_type=pl.DeviceIdType.MESH
            )
        for axis in others:
            over_peers(
                axis,
                lambda offset, peer, axis=axis: pl.semaphore_signal(
                    barrier, inc=1, device_id={axis: peer}, device_id_type=pl.DeviceIdType.MESH
                ),
            )
        pl.semaphore_wait(barrier, 4 + sum(lax.axis_size(axis) - 1 for axis in others))

    def copy(self, slot, send, peer):
        part = self.all_ref.at[slot]
        return put_copy(part, part, send, self.got_sems.at[slot], "cols", peer)

    def arrived(self, slot):
        self.copy(slot, self.across_sem.at[0], self.pair).wait_recv()

    def run(self, work, begun=None):
        steps = 4 * (self.length // 2) - 2

        def near(turn, carry):
            slot = self.quad_slot(self.z, turn, self.core)

            @pl.when(turn > 0)
            def _():
                self.arrived(slot)

            self.copy(slot, self.ring_sems.at[turn], self.after).start()

            @pl.when(turn < 2)
            def _():
                self.copy(slot, self.pair_sems.at[turn], self.pair).start()

            @pl.when(turn == 0)
            def _():
                self.copy(slot, self.across_sem.at[0], self.across).start()

            work(slot)
            return carry

        lax.fori_loop(0, 4, near, 0)
        if begun is not None:
            begun()

        def far(step, carry):
            turn, away = lax.rem(step, 4), step // 4 + 1
            slot = self.quad_slot(self.z - self.way * away, turn, self.core)
            self.arrived(slot)

            @pl.when(step < steps - 4)
            def _():
                self.copy(slot, self.ring_sems.at[step + 4], self.after).start()

            self.copy(slot, self.pair_sems.at[step + 2], self.pair).start()
            work(slot)
            slot = self.quad_slot(self.z + self.way * away, turn, 1 - self.core)
            self.arrived(slot)
            work(slot)
            return carry

        lax.fori_loop(0, steps, far, 0)
        own = self.device(self.z, self.y, self.core)

        def sent(sems):
            def one(at, carry):
                self.copy(own, sems.at[at], self.pair).wait_send()
                return carry

            lax.fori_loop(0, sems.shape[0], one, 0)

        sent(self.ring_sems)
        sent(self.pair_sems)
        sent(self.across_sem)


def ring_scratch(table):
    ncols = lax.axis_size("cols")
    moved = 4 * (ncols // 8) - 2
    dma = pltpu.SemaphoreType.DMA
    return [
        pltpu.VMEM((ncols, *table), jnp.bfloat16),
        dma((ncols,)),
        dma((moved,)),
        dma((moved + 2,)),
        dma((1,)),
    ]


def block_sums(table, records_ref, slot, block, width, by_prefix):
    shift = block.bit_length() - 1
    rows = range(records_ref.shape[0])
    packed = [records_ref[d, slot, 0:1, :].astype(jnp.int32) for d in rows]
    weight = [records_ref[d, slot, 1:2, :] for d in rows]
    prefix = [lax.shift_right_logical(ids, shift) for ids in packed]
    suffix = [ids & (block - 1) for ids in packed]
    take, put = (prefix, suffix) if by_prefix else (suffix, prefix)
    return move_block(table, take, put, weight, width)


def sketch_kernel(block, width, part_ref, here_ref, total_ref, all_ref, *sems):
    ring = Ring(all_ref, *sems)
    ring.greet()
    all_ref[lax.axis_index("cols")] = part_ref[...]
    total_ref[...] = jnp.zeros_like(total_ref)

    def work(slot):
        total_ref[...] += block_sums(all_ref[slot], here_ref, slot, block, width, False)

    ring.run(work)


def sketch_sums(part, here, block, width):
    return pl.pallas_call(
        functools.partial(sketch_kernel, block, width),
        out_shape=jax.ShapeDtypeStruct(part.shape, jnp.float32),
        in_specs=[vmem(), vmem()],
        out_specs=vmem(),
        scratch_shapes=ring_scratch(part.shape),
        compiler_params=pltpu.CompilerParams(
            collective_id=2, has_side_effects=True, vmem_limit_bytes=40 * 2**20
        ),
        name="sketch",
    )(part, here)


def project_kernel(
    scale,
    block,
    width,
    half_ref,
    basis_ref,
    mine_ref,
    totals_ref,
    coef_ref,
    whole_ref,
    total_ref,
    half_sems,
    basis_sems,
    own_sem,
    all_ref,
    *sems,
):
    ring = Ring(all_ref, *sems)
    ring.greet(["dp"])
    data_at, col_at = lax.axis_index("dp"), lax.axis_index("cols")
    size = basis_ref.shape[0]
    own_rows = pl.ds(pl.multiple_of(data_at * width, width), width)

    def half_copy(offset, peer):
        return put_copy(
            half_ref.at[pl.ds(pl.multiple_of(peer * width, width), width), :],
            all_ref.at[col_at, own_rows, :],
            half_sems.at[0, offset],
            half_sems.at[1, offset],
            "dp",
            peer,
        )

    own_basis = whole_ref.at[pl.ds(pl.multiple_of(data_at * size, size), size), :]

    def basis_copy(offset, peer):
        return put_copy(
            basis_ref, own_basis, basis_sems.at[0, offset], basis_sems.at[1, offset], "dp", peer
        )

    own_copy = pltpu.make_async_copy(basis_ref, own_basis, own_sem)

    def begun():
        over_peers("dp", lambda offset, peer: basis_copy(offset, peer).start())
        own_copy.start()

    def work(slot):
        total_ref[...] += block_sums(all_ref[slot], mine_ref, slot, block, width, True)

    over_peers("dp", lambda offset, peer: half_copy(offset, peer).start())
    all_ref[col_at, own_rows, :] = half_ref[own_rows, :]
    total_ref[...] = jnp.zeros_like(total_ref)
    over_peers("dp", lambda offset, peer: half_copy(offset, peer).wait())
    ring.run(work, begun)
    factor = scale * jnp.sum(totals_ref[1]) / jnp.sum(totals_ref[0])
    for g in range(total_ref.shape[0] // width):
        coef_ref[:, g * size : (g + 1) * size] = factor * total_ref[g * width : (g + 1) * width, :]
    over_peers("dp", lambda offset, peer: basis_copy(offset, peer).wait())
    own_copy.wait()


def project(half, basis_part, mine, totals, scale, block, width):
    ndata = lax.axis_size("dp")
    size, whole = basis_part.shape
    dma = pltpu.SemaphoreType.DMA
    anywhere = pl.BlockSpec(memory_space=pl.ANY)
    return pl.pallas_call(
        functools.partial(project_kernel, scale, block, width),
        out_shape=(
            jax.ShapeDtypeStruct((width, block), jnp.float32),
            jax.ShapeDtypeStruct((size * ndata, whole), jnp.bfloat16),
        ),
        in_specs=[vmem(), anywhere, vmem(), vmem()],
        out_specs=(vmem(), anywhere),
        scratch_shapes=[
            pltpu.VMEM(half.shape, jnp.float32),
            dma((2, ndata)),
            dma((2, ndata)),
            dma,
            *ring_scratch(half.shape),
        ],
        compiler_params=pltpu.CompilerParams(
            collective_id=3, has_side_effects=True, vmem_limit_bytes=40 * 2**20
        ),
        name="project",
    )(half, basis_part, mine, totals)


def shards(prefix_ids, suffix_ids, weights, counts, omega):
    ncols = lax.axis_size("cols")
    ndata = lax.axis_size("dp")
    block, width = omega.shape
    slots = prefix_ids.shape[-1]
    chunk = width // ndata
    size = block // ndata
    data_at = lax.axis_index("dp")

    live = lax.broadcasted_iota(jnp.int32, (ncols, slots), 1) < counts.reshape(ncols, 1)
    live_weights = jnp.where(live, weights.reshape(ncols, slots), 0.0)
    prefix_local = prefix_ids.reshape(ncols, slots) & (block - 1)
    suffix_local = suffix_ids.reshape(ncols, slots) & (block - 1)
    packed = prefix_local * block + suffix_local
    own = jnp.stack([packed.astype(jnp.float32), live_weights], axis=1)
    here, mine = exchange_records(own)
    part = lax.dynamic_slice_in_dim(omega, data_at * chunk, chunk, 1)
    part = part.reshape(ndata, size, chunk).swapaxes(1, 2).reshape(ndata * chunk, size)
    sketch = sketch_sums(part, here, block, chunk)
    rows, gram, totals = sum_gram(sketch.reshape(ndata, chunk, size), mine)
    basis_part, q_half = factor_and_q(gram.reshape(width, width), rows.reshape(width, size))
    scale = math.sqrt(block * ncols)
    coefficients, q_block = project(q_half, basis_part, mine, totals, scale, block, chunk)
    basis = scale * q_block.astype(jnp.float32)
    return (basis, coefficients)


def solution(mesh):
    placed = (
        P("dp", "cols", None, None),
        P("dp", "cols", None, None),
        P("dp", "cols", None, None),
        P("dp", "cols", None),
        P("cols", None),
    )
    return jax.shard_map(
        shards,
        mesh=mesh,
        in_specs=placed,
        out_specs=(P("cols", None), P("dp", "cols")),
        check_vma=False,
    )
```

```python
import functools
import math

import jax
import jax.numpy as jnp
from jax import lax
from jax.experimental import pallas as pl
from jax.experimental.pallas import tpu as pltpu
from jax.sharding import PartitionSpec as P

HIGHEST = lax.Precision.HIGHEST


def dot_exact(a, b, dims):
    return lax.dot_general(
        a, b, (dims, ((), ())), precision=HIGHEST, preferred_element_type=jnp.float32
    )


def one_hot(ids, size):
    rows = lax.broadcasted_iota(jnp.int32, (size, ids.shape[1]), 0)
    return jnp.where(rows == ids, 1.0, 0.0).astype(jnp.bfloat16)


def move_block(table, take, put, weight, width):
    size = table.shape[1]
    groups = table.shape[0] // width
    shift = size.bit_length() - 1
    beside = functools.partial(jnp.concatenate, axis=1)
    picked = jnp.dot(
        table,
        beside([one_hot(ids & (size - 1), size) for ids in take]),
        preferred_element_type=jnp.float32,
    )
    take_group = beside([lax.shift_right_logical(ids, shift) for ids in take])
    put_group = beside([lax.shift_right_logical(ids, shift) for ids in put])
    row = picked[:width]
    for g in range(1, groups):
        row = jnp.where(take_group == g, picked[g * width : (g + 1) * width], row)
    row = beside(weight) * row
    placed = jnp.concatenate(
        [jnp.where(put_group == g, row, 0.0).astype(jnp.bfloat16) for g in range(groups)], axis=0
    )
    spots = beside([one_hot(ids & (size - 1), size) for ids in put])
    return lax.dot_general(
        placed, spots, (((1,), (1,)), ((), ())), preferred_element_type=jnp.float32
    )


def vmem():
    return pl.BlockSpec(memory_space=pltpu.VMEM)


def put_copy(src, dst, send, recv, axis, peer):
    return pltpu.make_async_remote_copy(
        src_ref=src,
        dst_ref=dst,
        send_sem=send,
        recv_sem=recv,
        device_id={axis: peer},
        device_id_type=pl.DeviceIdType.MESH,
    )


def over_peers(axis, act, stride=1):
    count = lax.axis_size(axis)
    me = lax.axis_index(axis)

    def one(offset, carry):
        act(offset, lax.rem(me + stride * offset, count))
        return carry

    lax.fori_loop(1, count // stride, one, 0)


def signal(barrier, axis, peer):
    pl.semaphore_signal(
        barrier, inc=1, device_id={axis: peer}, device_id_type=pl.DeviceIdType.MESH
    )


def greet(*groups, near=()):
    barrier = pltpu.get_barrier_semaphore()
    for peer in near:
        signal(barrier, "cols", peer)
    for axis, stride in groups:
        over_peers(axis, lambda offset, peer, axis=axis: signal(barrier, axis, peer), stride)
    count = sum(lax.axis_size(axis) // stride - 1 for axis, stride in groups)
    pl.semaphore_wait(barrier, count + len(near))


def exchange(axis, make):
    over_peers(axis, lambda offset, peer: make(offset, peer).start())
    over_peers(axis, lambda offset, peer: make(offset, peer).wait())


def records_kernel(own_ref, here_ref, mine_ref, col_sems, here_sems, mine_sems):
    data_at, col_at = lax.axis_index("dp"), lax.axis_index("cols")
    greet(("cols", 1), ("dp", 1))

    def to_col(offset, peer):
        return put_copy(
            own_ref.at[peer],
            here_ref.at[data_at, col_at],
            col_sems.at[0, offset],
            col_sems.at[1, offset],
            "cols",
            peer,
        )

    def own_to_data(offset, peer):
        return put_copy(
            own_ref,
            mine_ref.at[data_at],
            mine_sems.at[0, offset],
            mine_sems.at[1, offset],
            "dp",
            peer,
        )

    def here_to_data(offset, peer):
        return put_copy(
            here_ref.at[data_at],
            here_ref.at[data_at],
            here_sems.at[0, offset],
            here_sems.at[1, offset],
            "dp",
            peer,
        )

    over_peers("cols", lambda offset, peer: to_col(offset, peer).start())
    over_peers("dp", lambda offset, peer: own_to_data(offset, peer).start())
    here_ref[data_at, col_at] = own_ref[col_at]
    mine_ref[data_at] = own_ref[...]
    over_peers("cols", lambda offset, peer: to_col(offset, peer).wait())
    exchange("dp", here_to_data)
    over_peers("dp", lambda offset, peer: own_to_data(offset, peer).wait())


def exchange_records(own):
    ndata, ncols = lax.axis_size("dp"), lax.axis_size("cols")
    gathered = jax.ShapeDtypeStruct((ndata, *own.shape), own.dtype)
    return pl.pallas_call(
        records_kernel,
        out_shape=(gathered, gathered),
        in_specs=[vmem()],
        out_specs=(vmem(), vmem()),
        scratch_shapes=[
            pltpu.SemaphoreType.DMA((2, ncols)),
            pltpu.SemaphoreType.DMA((2, ndata)),
            pltpu.SemaphoreType.DMA((2, ndata)),
        ],
        compiler_params=pltpu.CompilerParams(collective_id=0, has_side_effects=True),
        name="records",
    )(own)


def lower_blocks(width, lanes):
    return [(i, j) for i in range(width // lanes) for j in range(i + 1)]


def gram_kernel(
    sketch_ref,
    mine_ref,
    rows_ref,
    gram_ref,
    totals_ref,
    part_ref,
    half_ref,
    other_ref,
    got_ref,
    piece_ref,
    arrived_ref,
    shared_ref,
    own_ref,
    sum_ref,
    rows_sems,
    pair_sems,
    part_sems,
    piece_sems,
    shared_sems,
    gram_sems,
):
    data_at, col_at = lax.axis_index("dp"), lax.axis_index("cols")
    core, chip = lax.rem(col_at, 2), col_at // 2
    pair = col_at + 1 - 2 * core
    ndata, chunk, size = sketch_ref.shape
    width = ndata * chunk
    lanes = part_ref.shape[1]
    half = half_ref.shape[0]
    share = half // ndata
    chips = piece_ref.shape[0]
    few = share // chips

    def rows_at(start, count):
        return pl.ds(pl.multiple_of(start, 8), count)

    greet(("dp", 1), ("cols", 2), near=(pair,))

    def rows_copy(offset, peer):
        return put_copy(
            sketch_ref.at[peer],
            rows_ref.at[data_at],
            rows_sems.at[0, offset],
            rows_sems.at[1, offset],
            "dp",
            peer,
        )

    over_peers("dp", lambda offset, peer: rows_copy(offset, peer).start())
    rows_ref[data_at] = sketch_ref[data_at]
    weight = mine_ref[:, :, 1, :]
    for at, term in ((0, weight), (1, (weight > 0.0).astype(jnp.float32))):
        term = jnp.sum(term, axis=0).reshape(-1, *totals_ref.shape[1:])
        sum_ref[0, at] = jnp.sum(term, axis=0)
    sums_copy = put_copy(
        sum_ref.at[0], sum_ref.at[1], pair_sems.at[0, 0], pair_sems.at[1, 0], "cols", pair
    )
    sums_copy.start()
    piece_ref[...] = jnp.zeros_like(piece_ref)
    over_peers("dp", lambda offset, peer: rows_copy(offset, peer).wait())
    rows = rows_ref[...].reshape(width, size)
    gram = dot_exact(rows, rows, ((1,), (1,)))
    for at, (i, j) in enumerate(lower_blocks(width, lanes)):
        part_ref[lanes * at : lanes * (at + 1), :] = gram[
            lanes * i : lanes * (i + 1), lanes * j : lanes * (j + 1)
        ]

    pair_copy = put_copy(
        part_ref.at[rows_at((1 - core) * half, half), :],
        other_ref,
        pair_sems.at[0, 1],
        pair_sems.at[1, 1],
        "cols",
        pair,
    )
    pair_copy.start()
    sums_copy.wait()
    shared_ref[chip, 1] = sum_ref[0, 0] + sum_ref[1, 0]
    shared_ref[chip, 2] = sum_ref[0, 1] + sum_ref[1, 1]
    pair_copy.wait()
    half_ref[...] = part_ref[rows_at(core * half, half), :] + other_ref[...]

    def part_copy(offset, peer):
        return put_copy(
            half_ref.at[rows_at(peer * share, share), :],
            got_ref.at[data_at],
            part_sems.at[0, offset],
            part_sems.at[1, offset],
            "dp",
            peer,
        )

    over_peers("dp", lambda offset, peer: part_copy(offset, peer).start())
    got_ref[data_at] = half_ref[rows_at(data_at * share, share), :]
    over_peers("dp", lambda offset, peer: part_copy(offset, peer).wait())
    summed = jnp.sum(got_ref[...], axis=0)
    for at in range(chips):
        piece_ref[at, :few] = summed[few * at : few * (at + 1)]

    def piece_copy(offset, peer):
        return put_copy(
            piece_ref.at[peer // 2],
            arrived_ref.at[chip],
            piece_sems.at[0, offset],
            piece_sems.at[1, offset],
            "cols",
            peer,
        )

    over_peers("cols", lambda offset, peer: piece_copy(offset, peer).start(), 2)
    arrived_ref[chip] = piece_ref[chip]
    over_peers("cols", lambda offset, peer: piece_copy(offset, peer).wait(), 2)
    shared_ref[chip, 0] = jnp.sum(arrived_ref[...], axis=0)

    def shared_copy(offset, peer):
        return put_copy(
            shared_ref.at[chip],
            shared_ref.at[chip],
            shared_sems.at[0, offset],
            shared_sems.at[1, offset],
            "cols",
            peer,
        )

    over_peers("cols", lambda offset, peer: shared_copy(offset, peer).start(), 2)
    over_peers("cols", lambda offset, peer: shared_copy(offset, peer).wait(), 2)
    for at in range(chips):
        own_ref[few * at : few * (at + 1), :] = shared_ref[at, 0, :few, :]
    own_rows = rows_at((core * ndata + data_at) * share, share)

    def gram_copy(offset, peer):
        return put_copy(
            own_ref,
            gram_ref.at[own_rows, :],
            gram_sems.at[0, offset],
            gram_sems.at[1, offset],
            "dp",
            peer,
        )

    over_peers("dp", lambda offset, peer: gram_copy(offset, peer).start())
    gram_ref[own_rows, :] = own_ref[...]
    totals_ref[0] = jnp.sum(shared_ref[:, 1], axis=0)
    totals_ref[1] = jnp.sum(shared_ref[:, 2], axis=0)
    over_peers("dp", lambda offset, peer: gram_copy(offset, peer).wait())
    own_half = gram_ref.at[rows_at(core * half, half), :]
    last_copy = put_copy(
        own_half, own_half, pair_sems.at[0, 2], pair_sems.at[1, 2], "cols", pair
    )
    last_copy.start()
    last_copy.wait()


def sum_gram(sketch, mine):
    ndata, chunk, size = sketch.shape
    chips = lax.axis_size("cols") // 2
    width = ndata * chunk
    lanes = mine.shape[-1]
    f32 = jnp.float32
    packed = len(lower_blocks(width, lanes)) * lanes
    half = packed // 2
    share = half // ndata
    tile = (8, lanes)
    assert share % 8 == 0 and share % chips == 0 and share // chips <= 8
    dma = pltpu.SemaphoreType.DMA
    return pl.pallas_call(
        gram_kernel,
        out_shape=(
            jax.ShapeDtypeStruct((ndata, chunk, size), f32),
            jax.ShapeDtypeStruct((packed, lanes), f32),
            jax.ShapeDtypeStruct((2, *tile), f32),
        ),
        in_specs=[vmem(), vmem()],
        out_specs=(vmem(), vmem(), vmem()),
        scratch_shapes=[
            pltpu.VMEM((packed, lanes), f32),
            pltpu.VMEM((half, lanes), f32),
            pltpu.VMEM((half, lanes), f32),
            pltpu.VMEM((ndata, share, lanes), f32),
            pltpu.VMEM((chips, *tile), f32),
            pltpu.VMEM((chips, *tile), f32),
            pltpu.VMEM((chips, 3, *tile), f32),
            pltpu.VMEM((share, lanes), f32),
            pltpu.VMEM((2, 2, *tile), f32),
            dma((2, ndata)),
            dma((2, 3)),
            dma((2, ndata)),
            dma((2, chips)),
            dma((2, chips)),
            dma((2, ndata)),
        ],
        compiler_params=pltpu.CompilerParams(
            collective_id=1, has_side_effects=True, vmem_limit_bytes=24 * 2**20
        ),
        name="gram",
    )(sketch, mine)


def corner_inverse(tile, pivots=8):
    n = tile.shape[0]
    blocks = n // pivots

    def full(x):
        return jnp.broadcast_to(x, (pivots, n))

    work = [tile[pivots * i : pivots * (i + 1), :] for i in range(blocks)]
    lane = lax.broadcasted_iota(jnp.int32, (pivots, n), 1)
    sub = lax.broadcasted_iota(jnp.int32, (pivots, n), 0)
    done = []
    for at in range(blocks):
        start = at * pivots
        group = (lane >= start) & (lane < start + pivots)
        cols = [full(work[at][:, start + c : start + c + 1]) for c in range(pivots)]
        left = [[full(cols[c][r : r + 1, :]) for c in range(r + 1)] for r in range(pivots)]
        rows = [
            jnp.where(group, jnp.where(lane == start + r, 1.0, 0.0), full(work[at][r : r + 1, :]))
            for r in range(pivots)
        ]
        recip = [None] * pivots
        low = [[None] * pivots for _ in range(pivots)]
        for c in range(pivots):
            recip[c] = 1.0 / left[c][c]
            for r in range(c + 1, pivots):
                low[r][c] = left[r][c] * recip[c]
                for e in range(c + 1, r + 1):
                    left[r][e] = left[r][e] - low[r][c] * left[e][c]
        for r in range(pivots):
            for c in range(r):
                rows[r] = rows[r] - low[r][c] * rows[c]
        result = jnp.zeros((pivots, n), jnp.float32)
        for r in range(pivots):
            result = jnp.where(sub == r, rows[r] * lax.rsqrt(left[r][r]), result)
        done.append(jnp.where(lane <= sub + start, result, 0.0))
        back = [rows[r] * recip[r] for r in range(pivots)]
        for r in range(pivots - 1, -1, -1):
            for c in range(r):
                back[c] = back[c] - low[r][c] * back[r]
        for i in range(at + 1, blocks):
            rest = jnp.where(group, 0.0, work[i])
            for c in range(pivots):
                rest = rest - full(work[i][:, start + c : start + c + 1]) * back[c]
            work[i] = rest
    return jnp.concatenate(done, axis=0)


def factor_kernel(gram_ref, rows_ref, basis_ref, half_ref, work_ref, inverse_ref):
    n = work_ref.shape[0]
    size = gram_ref.shape[1]
    for at, (i, j) in enumerate(lower_blocks(n, size)):
        work_ref[size * i : size * (i + 1), size * j : size * (j + 1)] = gram_ref[
            size * at : size * (at + 1), :
        ]
    for start in range(0, n, size):
        end = start + size
        corner = corner_inverse(work_ref[start:end, start:end])
        if start:
            inverse_ref[start:end, :start] = dot_exact(
                corner, inverse_ref[start:end, :start], ((1,), (0,))
            )
        inverse_ref[start:end, start:end] = corner
        if end < n:
            low = dot_exact(work_ref[end:, start:end], corner, ((1,), (1,)))
            work_ref[end:, end:] -= dot_exact(low, low, ((1,), (1,)))
            if start:
                inverse_ref[end:, :start] -= dot_exact(
                    low, inverse_ref[start:end, :start], ((1,), (0,))
                )
            inverse_ref[end:, start:end] = -dot_exact(low, corner, ((1,), (0,)))
    for start in range(0, n, size):
        end = start + size
        q = dot_exact(inverse_ref[start:end, :end], rows_ref[:end, :], ((1,), (0,)))
        half_ref[start:end, :] = q.astype(jnp.bfloat16)
        basis_ref[:, start:end] = q.T.astype(jnp.bfloat16)


def factor_and_q(gram, rows):
    width, size = rows.shape
    return pl.pallas_call(
        factor_kernel,
        out_shape=(
            jax.ShapeDtypeStruct((size, width), jnp.bfloat16),
            jax.ShapeDtypeStruct((width, size), jnp.bfloat16),
        ),
        in_specs=[vmem(), vmem()],
        out_specs=(vmem(), vmem()),
        scratch_shapes=[pltpu.VMEM((width, width), jnp.float32)] * 2,
        compiler_params=pltpu.CompilerParams(vmem_limit_bytes=24 * 2**20),
        name="factor",
    )(gram, rows)


class Ring:
    def __init__(self, all_ref, got_sems, ring_sems, pair_sems, across_sem):
        self.all_ref, self.got_sems = all_ref, got_sems
        self.ring_sems, self.pair_sems, self.across_sem = ring_sems, pair_sems, across_sem
        at = lax.axis_index("cols")
        self.length = lax.axis_size("cols") // 4
        self.z, quad = at // 4, lax.rem(at, 4)
        self.y, self.core = quad // 2, lax.rem(quad, 2)
        self.way = 1 - 2 * self.core
        self.pair = self.device(self.z, self.y, 1 - self.core)
        self.across = self.device(self.z, 1 - self.y, self.core)
        self.after = self.device(self.z + self.way, self.y, self.core)
        self.before = self.device(self.z - self.way, self.y, self.core)

    def device(self, z, y, core):
        z = lax.rem(z + self.length, self.length)
        return z * 4 + y * 2 + core

    def quad_slot(self, z, turn, core):
        y = lax.rem(self.y + lax.rem(turn, 2), 2)
        return self.device(z, y, lax.rem(core + turn // 2, 2))

    def greet(self, *groups):
        greet(*groups, near=(self.pair, self.across, self.after, self.before))

    def copy(self, slot, send, peer):
        part = self.all_ref.at[slot]
        return put_copy(part, part, send, self.got_sems.at[slot], "cols", peer)

    def arrived(self, slot):
        self.copy(slot, self.across_sem.at[0], self.pair).wait_recv()

    def run(self, work, begun=None):
        steps = 4 * (self.length // 2) - 2

        def near(turn, carry):
            slot = self.quad_slot(self.z, turn, self.core)

            @pl.when(turn > 0)
            def _():
                self.arrived(slot)

            self.copy(slot, self.ring_sems.at[turn], self.after).start()

            @pl.when(turn < 2)
            def _():
                self.copy(slot, self.pair_sems.at[turn], self.pair).start()

            @pl.when(turn == 0)
            def _():
                self.copy(slot, self.across_sem.at[0], self.across).start()

            work(slot)
            return carry

        lax.fori_loop(0, 4, near, 0)
        if begun is not None:
            begun()

        def far(step, carry):
            turn, away = lax.rem(step, 4), step // 4 + 1
            slot = self.quad_slot(self.z - self.way * away, turn, self.core)
            self.arrived(slot)

            @pl.when(step < steps - 4)
            def _():
                self.copy(slot, self.ring_sems.at[step + 4], self.after).start()

            self.copy(slot, self.pair_sems.at[step + 2], self.pair).start()
            work(slot)
            slot = self.quad_slot(self.z + self.way * away, turn, 1 - self.core)
            self.arrived(slot)
            work(slot)
            return carry

        lax.fori_loop(0, steps, far, 0)
        own = self.device(self.z, self.y, self.core)

        def sent(sems):
            def one(at, carry):
                self.copy(own, sems.at[at], self.pair).wait_send()
                return carry

            lax.fori_loop(0, sems.shape[0], one, 0)

        sent(self.ring_sems)
        sent(self.pair_sems)
        sent(self.across_sem)


def ring_scratch(table):
    ncols = lax.axis_size("cols")
    moved = 4 * (ncols // 8) - 2
    dma = pltpu.SemaphoreType.DMA
    return [
        pltpu.VMEM((ncols, *table), jnp.bfloat16),
        dma((ncols,)),
        dma((moved,)),
        dma((moved + 2,)),
        dma((1,)),
    ]


def block_sums(table, records_ref, slot, block, width, by_prefix):
    shift = block.bit_length() - 1
    rows = range(records_ref.shape[0])
    packed = [records_ref[d, slot, 0:1, :].astype(jnp.int32) for d in rows]
    weight = [records_ref[d, slot, 1:2, :] for d in rows]
    prefix = [lax.shift_right_logical(ids, shift) for ids in packed]
    suffix = [ids & (block - 1) for ids in packed]
    take, put = (prefix, suffix) if by_prefix else (suffix, prefix)
    return move_block(table, take, put, weight, width)


def sketch_kernel(block, width, part_ref, here_ref, total_ref, all_ref, *sems):
    ring = Ring(all_ref, *sems)
    ring.greet()
    all_ref[lax.axis_index("cols")] = part_ref[...]
    total_ref[...] = jnp.zeros_like(total_ref)

    def work(slot):
        total_ref[...] += block_sums(all_ref[slot], here_ref, slot, block, width, False)

    ring.run(work)


def sketch_sums(part, here, block, width):
    return pl.pallas_call(
        functools.partial(sketch_kernel, block, width),
        out_shape=jax.ShapeDtypeStruct(part.shape, jnp.float32),
        in_specs=[vmem(), vmem()],
        out_specs=vmem(),
        scratch_shapes=ring_scratch(part.shape),
        compiler_params=pltpu.CompilerParams(
            collective_id=2, has_side_effects=True, vmem_limit_bytes=40 * 2**20
        ),
        name="sketch",
    )(part, here)


def project_kernel(
    scale,
    block,
    width,
    half_ref,
    basis_ref,
    mine_ref,
    totals_ref,
    coef_ref,
    whole_ref,
    total_ref,
    half_sems,
    basis_sems,
    own_sem,
    all_ref,
    *sems,
):
    ring = Ring(all_ref, *sems)
    ring.greet(("dp", 1))
    data_at, col_at = lax.axis_index("dp"), lax.axis_index("cols")
    size = basis_ref.shape[0]
    own_rows = pl.ds(pl.multiple_of(data_at * width, width), width)

    def half_copy(offset, peer):
        return put_copy(
            half_ref.at[pl.ds(pl.multiple_of(peer * width, width), width), :],
            all_ref.at[col_at, own_rows, :],
            half_sems.at[0, offset],
            half_sems.at[1, offset],
            "dp",
            peer,
        )

    own_basis = whole_ref.at[pl.ds(pl.multiple_of(data_at * size, size), size), :]

    def basis_copy(offset, peer):
        return put_copy(
            basis_ref, own_basis, basis_sems.at[0, offset], basis_sems.at[1, offset], "dp", peer
        )

    own_copy = pltpu.make_async_copy(basis_ref, own_basis, own_sem)

    def begun():
        over_peers("dp", lambda offset, peer: basis_copy(offset, peer).start())
        own_copy.start()

    def work(slot):
        total_ref[...] += block_sums(all_ref[slot], mine_ref, slot, block, width, True)

    over_peers("dp", lambda offset, peer: half_copy(offset, peer).start())
    all_ref[col_at, own_rows, :] = half_ref[own_rows, :]
    total_ref[...] = jnp.zeros_like(total_ref)
    over_peers("dp", lambda offset, peer: half_copy(offset, peer).wait())
    ring.run(work, begun)
    factor = scale * jnp.sum(totals_ref[1]) / jnp.sum(totals_ref[0])
    for g in range(total_ref.shape[0] // width):
        coef_ref[:, g * size : (g + 1) * size] = factor * total_ref[g * width : (g + 1) * width, :]
    over_peers("dp", lambda offset, peer: basis_copy(offset, peer).wait())
    own_copy.wait()


def project(half, basis_part, mine, totals, scale, block, width):
    ndata = lax.axis_size("dp")
    size, whole = basis_part.shape
    dma = pltpu.SemaphoreType.DMA
    anywhere = pl.BlockSpec(memory_space=pl.ANY)
    return pl.pallas_call(
        functools.partial(project_kernel, scale, block, width),
        out_shape=(
            jax.ShapeDtypeStruct((width, block), jnp.float32),
            jax.ShapeDtypeStruct((size * ndata, whole), jnp.bfloat16),
        ),
        in_specs=[vmem(), anywhere, vmem(), vmem()],
        out_specs=(vmem(), anywhere),
        scratch_shapes=[
            pltpu.VMEM(half.shape, jnp.float32),
            dma((2, ndata)),
            dma((2, ndata)),
            dma,
            *ring_scratch(half.shape),
        ],
        compiler_params=pltpu.CompilerParams(
            collective_id=3, has_side_effects=True, vmem_limit_bytes=40 * 2**20
        ),
        name="project",
    )(half, basis_part, mine, totals)


def shards(prefix_ids, suffix_ids, weights, counts, omega):
    ncols = lax.axis_size("cols")
    ndata = lax.axis_size("dp")
    block, width = omega.shape
    slots = prefix_ids.shape[-1]
    chunk = width // ndata
    size = block // ndata
    data_at = lax.axis_index("dp")

    live = lax.broadcasted_iota(jnp.int32, (ncols, slots), 1) < counts.reshape(ncols, 1)
    live_weights = jnp.where(live, weights.reshape(ncols, slots), 0.0)
    prefix_local = prefix_ids.reshape(ncols, slots) & (block - 1)
    suffix_local = suffix_ids.reshape(ncols, slots) & (block - 1)
    packed = prefix_local * block + suffix_local
    own = jnp.stack([packed.astype(jnp.float32), live_weights], axis=1)
    here, mine = exchange_records(own)
    part = lax.dynamic_slice_in_dim(omega, data_at * chunk, chunk, 1)
    part = part.reshape(ndata, size, chunk).swapaxes(1, 2).reshape(ndata * chunk, size)
    sketch = sketch_sums(part, here, block, chunk)
    rows, gram, totals = sum_gram(sketch.reshape(ndata, chunk, size), mine)
    basis_part, q_half = factor_and_q(gram, rows.reshape(width, size))
    scale = math.sqrt(block * ncols)
    coefficients, q_block = project(q_half, basis_part, mine, totals, scale, block, chunk)
    basis = scale * q_block.astype(jnp.float32)
    return (basis, coefficients)


def solution(mesh):
    placed = (
        P("dp", "cols", None, None),
        P("dp", "cols", None, None),
        P("dp", "cols", None, None),
        P("dp", "cols", None),
        P("cols", None),
    )
    return jax.shard_map(
        shards,
        mesh=mesh,
        in_specs=placed,
        out_specs=(P("cols", None), P("dp", "cols")),
        check_vma=False,
    )
```

```python
import functools
import math

import jax
import jax.numpy as jnp
from jax import lax
from jax.experimental import pallas as pl
from jax.experimental.pallas import tpu as pltpu
from jax.sharding import PartitionSpec as P

HIGHEST = lax.Precision.HIGHEST


def dot_exact(a, b, dims):
    return lax.dot_general(
        a, b, (dims, ((), ())), precision=HIGHEST, preferred_element_type=jnp.float32
    )


def one_hot(ids, size):
    rows = lax.broadcasted_iota(jnp.int32, (size, ids.shape[1]), 0)
    return jnp.where(rows == ids, 1.0, 0.0).astype(jnp.bfloat16)


def weighted_rows(table, take, put, weight, width):
    size = table.shape[1]
    groups = table.shape[0] // width
    shift = size.bit_length() - 1
    beside = functools.partial(jnp.concatenate, axis=1)
    picked = jnp.dot(
        table,
        beside([one_hot(ids & (size - 1), size) for ids in take]),
        preferred_element_type=jnp.float32,
    )
    take_group = beside([lax.shift_right_logical(ids, shift) for ids in take])
    put_group = beside([lax.shift_right_logical(ids, shift) for ids in put])
    row = picked[:width]
    for g in range(1, groups):
        row = jnp.where(take_group == g, picked[g * width : (g + 1) * width], row)
    row = beside(weight) * row
    placed = jnp.concatenate(
        [jnp.where(put_group == g, row, 0.0).astype(jnp.bfloat16) for g in range(groups)], axis=0
    )
    return placed, beside([one_hot(ids & (size - 1), size) for ids in put])


def vmem():
    return pl.BlockSpec(memory_space=pltpu.VMEM)


def put_copy(src, dst, send, recv, axis, peer):
    return pltpu.make_async_remote_copy(
        src_ref=src,
        dst_ref=dst,
        send_sem=send,
        recv_sem=recv,
        device_id={axis: peer},
        device_id_type=pl.DeviceIdType.MESH,
    )


def over_peers(axis, act, stride=1):
    count = lax.axis_size(axis)
    me = lax.axis_index(axis)

    def one(offset, carry):
        act(offset, lax.rem(me + stride * offset, count))
        return carry

    lax.fori_loop(1, count // stride, one, 0)


def signal(barrier, axis, peer):
    pl.semaphore_signal(
        barrier, inc=1, device_id={axis: peer}, device_id_type=pl.DeviceIdType.MESH
    )


def greet(*groups, near=()):
    barrier = pltpu.get_barrier_semaphore()
    for peer in near:
        signal(barrier, "cols", peer)
    for axis, stride in groups:
        over_peers(axis, lambda offset, peer, axis=axis: signal(barrier, axis, peer), stride)
    count = sum(lax.axis_size(axis) // stride - 1 for axis, stride in groups)
    pl.semaphore_wait(barrier, count + len(near))


def exchange(axis, make):
    over_peers(axis, lambda offset, peer: make(offset, peer).start())
    over_peers(axis, lambda offset, peer: make(offset, peer).wait())


def records_kernel(own_ref, here_ref, mine_ref, col_sems, here_sems, mine_sems):
    data_at, col_at = lax.axis_index("dp"), lax.axis_index("cols")
    greet(("cols", 1), ("dp", 1))

    def to_col(offset, peer):
        return put_copy(
            own_ref.at[peer],
            here_ref.at[data_at, col_at],
            col_sems.at[0, offset],
            col_sems.at[1, offset],
            "cols",
            peer,
        )

    def own_to_data(offset, peer):
        return put_copy(
            own_ref,
            mine_ref.at[data_at],
            mine_sems.at[0, offset],
            mine_sems.at[1, offset],
            "dp",
            peer,
        )

    def here_to_data(offset, peer):
        return put_copy(
            here_ref.at[data_at],
            here_ref.at[data_at],
            here_sems.at[0, offset],
            here_sems.at[1, offset],
            "dp",
            peer,
        )

    over_peers("cols", lambda offset, peer: to_col(offset, peer).start())
    over_peers("dp", lambda offset, peer: own_to_data(offset, peer).start())
    here_ref[data_at, col_at] = own_ref[col_at]
    mine_ref[data_at] = own_ref[...]
    over_peers("cols", lambda offset, peer: to_col(offset, peer).wait())
    exchange("dp", here_to_data)
    over_peers("dp", lambda offset, peer: own_to_data(offset, peer).wait())


def exchange_records(own):
    ndata, ncols = lax.axis_size("dp"), lax.axis_size("cols")
    gathered = jax.ShapeDtypeStruct((ndata, *own.shape), own.dtype)
    return pl.pallas_call(
        records_kernel,
        out_shape=(gathered, gathered),
        in_specs=[vmem()],
        out_specs=(vmem(), vmem()),
        scratch_shapes=[
            pltpu.SemaphoreType.DMA((2, ncols)),
            pltpu.SemaphoreType.DMA((2, ndata)),
            pltpu.SemaphoreType.DMA((2, ndata)),
        ],
        compiler_params=pltpu.CompilerParams(collective_id=0, has_side_effects=True),
        name="records",
    )(own)


def lower_blocks(width, lanes):
    return [(i, j) for i in range(width // lanes) for j in range(i + 1)]


def gram_kernel(
    sketch_ref,
    mine_ref,
    rows_ref,
    gram_ref,
    totals_ref,
    part_ref,
    half_ref,
    other_ref,
    got_ref,
    piece_ref,
    arrived_ref,
    shared_ref,
    own_ref,
    sum_ref,
    rows_sems,
    pair_sems,
    part_sems,
    piece_sems,
    shared_sems,
    gram_sems,
):
    data_at, col_at = lax.axis_index("dp"), lax.axis_index("cols")
    core, chip = lax.rem(col_at, 2), col_at // 2
    pair = col_at + 1 - 2 * core
    ndata, chunk, size = sketch_ref.shape
    width = ndata * chunk
    lanes = part_ref.shape[1]
    half = half_ref.shape[0]
    share = half // ndata
    chips = piece_ref.shape[0]
    few = share // chips

    def rows_at(start, count):
        return pl.ds(pl.multiple_of(start, 8), count)

    greet(("dp", 1), ("cols", 2), near=(pair,))

    def rows_copy(offset, peer):
        return put_copy(
            sketch_ref.at[peer],
            rows_ref.at[data_at],
            rows_sems.at[0, offset],
            rows_sems.at[1, offset],
            "dp",
            peer,
        )

    over_peers("dp", lambda offset, peer: rows_copy(offset, peer).start())
    rows_ref[data_at] = sketch_ref[data_at]
    weight = mine_ref[:, :, 1, :]
    for at, term in ((0, weight), (1, (weight > 0.0).astype(jnp.float32))):
        term = jnp.sum(term, axis=0).reshape(-1, *totals_ref.shape[1:])
        sum_ref[0, at] = jnp.sum(term, axis=0)
    sums_copy = put_copy(
        sum_ref.at[0], sum_ref.at[1], pair_sems.at[0, 0], pair_sems.at[1, 0], "cols", pair
    )
    sums_copy.start()
    piece_ref[...] = jnp.zeros_like(piece_ref)
    over_peers("dp", lambda offset, peer: rows_copy(offset, peer).wait())
    rows = rows_ref[...].reshape(width, size)
    gram = dot_exact(rows, rows, ((1,), (1,)))
    for at, (i, j) in enumerate(lower_blocks(width, lanes)):
        part_ref[lanes * at : lanes * (at + 1), :] = gram[
            lanes * i : lanes * (i + 1), lanes * j : lanes * (j + 1)
        ]

    pair_copy = put_copy(
        part_ref.at[rows_at((1 - core) * half, half), :],
        other_ref,
        pair_sems.at[0, 1],
        pair_sems.at[1, 1],
        "cols",
        pair,
    )
    pair_copy.start()
    sums_copy.wait()
    shared_ref[chip, 1] = sum_ref[0, 0] + sum_ref[1, 0]
    shared_ref[chip, 2] = sum_ref[0, 1] + sum_ref[1, 1]
    pair_copy.wait()
    half_ref[...] = part_ref[rows_at(core * half, half), :] + other_ref[...]

    def part_copy(offset, peer):
        return put_copy(
            half_ref.at[rows_at(peer * share, share), :],
            got_ref.at[data_at],
            part_sems.at[0, offset],
            part_sems.at[1, offset],
            "dp",
            peer,
        )

    over_peers("dp", lambda offset, peer: part_copy(offset, peer).start())
    got_ref[data_at] = half_ref[rows_at(data_at * share, share), :]
    over_peers("dp", lambda offset, peer: part_copy(offset, peer).wait())
    summed = jnp.sum(got_ref[...], axis=0)
    for at in range(chips):
        piece_ref[at, :few] = summed[few * at : few * (at + 1)]

    def piece_copy(offset, peer):
        return put_copy(
            piece_ref.at[peer // 2],
            arrived_ref.at[chip],
            piece_sems.at[0, offset],
            piece_sems.at[1, offset],
            "cols",
            peer,
        )

    over_peers("cols", lambda offset, peer: piece_copy(offset, peer).start(), 2)
    arrived_ref[chip] = piece_ref[chip]
    over_peers("cols", lambda offset, peer: piece_copy(offset, peer).wait(), 2)
    shared_ref[chip, 0] = jnp.sum(arrived_ref[...], axis=0)

    def shared_copy(offset, peer):
        return put_copy(
            shared_ref.at[chip],
            shared_ref.at[chip],
            shared_sems.at[0, offset],
            shared_sems.at[1, offset],
            "cols",
            peer,
        )

    over_peers("cols", lambda offset, peer: shared_copy(offset, peer).start(), 2)
    over_peers("cols", lambda offset, peer: shared_copy(offset, peer).wait(), 2)
    for at in range(chips):
        own_ref[few * at : few * (at + 1), :] = shared_ref[at, 0, :few, :]
    own_rows = rows_at((core * ndata + data_at) * share, share)

    def gram_copy(offset, peer):
        return put_copy(
            own_ref,
            gram_ref.at[own_rows, :],
            gram_sems.at[0, offset],
            gram_sems.at[1, offset],
            "dp",
            peer,
        )

    over_peers("dp", lambda offset, peer: gram_copy(offset, peer).start())
    gram_ref[own_rows, :] = own_ref[...]
    totals_ref[0] = jnp.sum(shared_ref[:, 1], axis=0)
    totals_ref[1] = jnp.sum(shared_ref[:, 2], axis=0)
    over_peers("dp", lambda offset, peer: gram_copy(offset, peer).wait())
    own_half = gram_ref.at[rows_at(core * half, half), :]
    last_copy = put_copy(
        own_half, own_half, pair_sems.at[0, 2], pair_sems.at[1, 2], "cols", pair
    )
    last_copy.start()
    last_copy.wait()


def sum_gram(sketch, mine):
    ndata, chunk, size = sketch.shape
    chips = lax.axis_size("cols") // 2
    width = ndata * chunk
    lanes = mine.shape[-1]
    f32 = jnp.float32
    packed = len(lower_blocks(width, lanes)) * lanes
    half = packed // 2
    share = half // ndata
    tile = (8, lanes)
    assert share % 8 == 0 and share % chips == 0 and share // chips <= 8
    dma = pltpu.SemaphoreType.DMA
    return pl.pallas_call(
        gram_kernel,
        out_shape=(
            jax.ShapeDtypeStruct((ndata, chunk, size), f32),
            jax.ShapeDtypeStruct((packed, lanes), f32),
            jax.ShapeDtypeStruct((2, *tile), f32),
        ),
        in_specs=[vmem(), vmem()],
        out_specs=(vmem(), vmem(), vmem()),
        scratch_shapes=[
            pltpu.VMEM((packed, lanes), f32),
            pltpu.VMEM((half, lanes), f32),
            pltpu.VMEM((half, lanes), f32),
            pltpu.VMEM((ndata, share, lanes), f32),
            pltpu.VMEM((chips, *tile), f32),
            pltpu.VMEM((chips, *tile), f32),
            pltpu.VMEM((chips, 3, *tile), f32),
            pltpu.VMEM((share, lanes), f32),
            pltpu.VMEM((2, 2, *tile), f32),
            dma((2, ndata)),
            dma((2, 3)),
            dma((2, ndata)),
            dma((2, chips)),
            dma((2, chips)),
            dma((2, ndata)),
        ],
        compiler_params=pltpu.CompilerParams(
            collective_id=1, has_side_effects=True, vmem_limit_bytes=24 * 2**20
        ),
        name="gram",
    )(sketch, mine)


def corner_inverse(tile, pivots=8):
    n = tile.shape[0]
    blocks = n // pivots

    def full(x):
        return jnp.broadcast_to(x, (pivots, n))

    work = [tile[pivots * i : pivots * (i + 1), :] for i in range(blocks)]
    lane = lax.broadcasted_iota(jnp.int32, (pivots, n), 1)
    sub = lax.broadcasted_iota(jnp.int32, (pivots, n), 0)
    done = []
    for at in range(blocks):
        start = at * pivots
        group = (lane >= start) & (lane < start + pivots)
        cols = [full(work[at][:, start + c : start + c + 1]) for c in range(pivots)]
        left = [[full(cols[c][r : r + 1, :]) for c in range(r + 1)] for r in range(pivots)]
        rows = [
            jnp.where(group, jnp.where(lane == start + r, 1.0, 0.0), full(work[at][r : r + 1, :]))
            for r in range(pivots)
        ]
        recip = [None] * pivots
        low = [[None] * pivots for _ in range(pivots)]
        for c in range(pivots):
            recip[c] = 1.0 / left[c][c]
            for r in range(c + 1, pivots):
                low[r][c] = left[r][c] * recip[c]
                for e in range(c + 1, r + 1):
                    left[r][e] = left[r][e] - low[r][c] * left[e][c]
        for r in range(pivots):
            for c in range(r):
                rows[r] = rows[r] - low[r][c] * rows[c]
        result = jnp.zeros((pivots, n), jnp.float32)
        for r in range(pivots):
            result = jnp.where(sub == r, rows[r] * lax.rsqrt(left[r][r]), result)
        done.append(jnp.where(lane <= sub + start, result, 0.0))
        back = [rows[r] * recip[r] for r in range(pivots)]
        for r in range(pivots - 1, -1, -1):
            for c in range(r):
                back[c] = back[c] - low[r][c] * back[r]
        for i in range(at + 1, blocks):
            rest = jnp.where(group, 0.0, work[i])
            for c in range(pivots):
                rest = rest - full(work[i][:, start + c : start + c + 1]) * back[c]
            work[i] = rest
    return jnp.concatenate(done, axis=0)


def factor_kernel(gram_ref, rows_ref, basis_ref, half_ref, work_ref, inverse_ref):
    n = work_ref.shape[0]
    size = gram_ref.shape[1]
    for at, (i, j) in enumerate(lower_blocks(n, size)):
        work_ref[size * i : size * (i + 1), size * j : size * (j + 1)] = gram_ref[
            size * at : size * (at + 1), :
        ]
    for start in range(0, n, size):
        end = start + size
        corner = corner_inverse(work_ref[start:end, start:end])
        if start:
            inverse_ref[start:end, :start] = dot_exact(
                corner, inverse_ref[start:end, :start], ((1,), (0,))
            )
        inverse_ref[start:end, start:end] = corner
        if end < n:
            low = dot_exact(work_ref[end:, start:end], corner, ((1,), (1,)))
            work_ref[end:, end:] -= dot_exact(low, low, ((1,), (1,)))
            if start:
                inverse_ref[end:, :start] -= dot_exact(
                    low, inverse_ref[start:end, :start], ((1,), (0,))
                )
            inverse_ref[end:, start:end] = -dot_exact(low, corner, ((1,), (0,)))
    for start in range(0, n, size):
        end = start + size
        q = dot_exact(inverse_ref[start:end, :end], rows_ref[:end, :], ((1,), (0,)))
        half_ref[start:end, :] = q.astype(jnp.bfloat16)
        basis_ref[:, start:end] = q.T.astype(jnp.bfloat16)


def factor_and_q(gram, rows):
    width, size = rows.shape
    return pl.pallas_call(
        factor_kernel,
        out_shape=(
            jax.ShapeDtypeStruct((size, width), jnp.bfloat16),
            jax.ShapeDtypeStruct((width, size), jnp.bfloat16),
        ),
        in_specs=[vmem(), vmem()],
        out_specs=(vmem(), vmem()),
        scratch_shapes=[pltpu.VMEM((width, width), jnp.float32)] * 2,
        compiler_params=pltpu.CompilerParams(vmem_limit_bytes=24 * 2**20),
        name="factor",
    )(gram, rows)


class Ring:
    ARRIVALS = 15
    RING = (0, 1, 3, 4, 5, 7, 8)
    CROSS = (1, 5, 9, 12)

    def __init__(self, all_ref, got_sems, ring_sems, pair_sems, cross_sems):
        self.all_ref, self.got_sems = all_ref, got_sems
        self.ring_sems, self.pair_sems, self.cross_sems = ring_sems, pair_sems, cross_sems
        at = lax.axis_index("cols")
        self.length = lax.axis_size("cols") // 4
        assert self.length == 8
        self.z, quad = at // 4, lax.rem(at, 4)
        self.y, self.core = quad // 2, lax.rem(quad, 2)
        self.way = 1 - 2 * self.core
        self.own = at
        self.pair = self.device(0, 0, 1)
        self.across = self.device(0, 1, 0)
        self.after = self.device(-1, 0, 0)
        self.before = self.device(1, 0, 0)
        self.diagonal = self.device(0, 1, 1)

    def device(self, away, row, core, mirror=False):
        way = -self.way if mirror else self.way
        z = lax.rem(self.z - way * away + self.length, self.length)
        y = lax.rem(self.y + row, 2)
        core = lax.rem(self.core + core + (1 if mirror else 0), 2)
        return z * 4 + y * 2 + core

    def place(self, n):
        return n + n // 13

    def slot(self, m, mirror=False):
        turn = lax.rem(m, 4)
        away = m // 4 + 1 - (turn // 2 - turn // 3)
        return self.device(away, turn // 2, lax.rem((turn + 1) // 2, 2), mirror)

    def greet(self, *groups):
        greet(*groups, near=(self.pair, self.across, self.after, self.before))

    def copy(self, slot, send, peer):
        part = self.all_ref.at[slot]
        return put_copy(part, part, send, self.got_sems.at[slot], "cols", peer)

    def arrived(self, slot):
        self.copy(slot, self.cross_sems.at[0], self.pair).wait_recv()

    def to_ring(self, slot, at):
        self.copy(slot, self.ring_sems.at[at], self.after).start()

    def to_pair(self, slot, at):
        self.copy(slot, self.pair_sems.at[at], self.pair).start()

    def to_across(self, slot, at):
        self.copy(slot, self.cross_sems.at[at], self.across).start()

    def hand_on(self, n):
        m = self.place(n)
        slot = self.slot(m)
        self.arrived(slot)
        turn, step = lax.rem(m, 4), m // 4 + 1

        @pl.when((turn == 0) & (step < 4))
        def _():
            self.to_ring(slot, m + 3)

        @pl.when((turn == 1) & (step < 3))
        def _():
            self.to_ring(slot, m + 3)

        @pl.when(m == 3)
        def _():
            self.to_ring(slot, m + 3)

        @pl.when(m == 8)
        def _():
            self.to_ring(self.slot(7), 7 + 3)

        @pl.when((turn == 1) | (m == 12))
        def _():
            self.to_across(slot, m)

        @pl.when(m != 2)
        def _():
            self.to_pair(slot, n + 1)

    def begin(self):
        self.to_pair(self.own, 0)
        self.to_ring(self.own, 0)
        self.to_across(self.own, 0)
        self.arrived(self.pair)
        self.to_ring(self.pair, 1)
        self.arrived(self.across)
        self.to_ring(self.across, 2)
        self.to_pair(self.across, 3)
        self.hand_on(0)

    def run(self, work, also):
        work([self.own, self.pair])
        last = self.ARRIVALS - 1

        def one(n, carry):
            for at, act in also.items():
                pl.when(n == at)(act)

            @pl.when(n < last)
            def _():
                ahead = n + 1
                swap = ahead // 11 - 2 * (ahead // 12) + ahead // 13
                self.hand_on(ahead + swap)

            m = self.place(n)
            mirrored = self.slot(m, mirror=True)

            @pl.when(m != 2)
            def _():
                self.arrived(mirrored)

            work([self.slot(m), mirrored])
            return carry

        lax.fori_loop(0, self.ARRIVALS, one, 0)
        for at in [0, 1, 2, *(m + 3 for m in self.RING)]:
            self.copy(self.own, self.ring_sems.at[at], self.after).wait_send()
        for at in [0, *self.CROSS]:
            self.copy(self.own, self.cross_sems.at[at], self.across).wait_send()

        def sent(at, carry):
            self.copy(self.own, self.pair_sems.at[at], self.pair).wait_send()
            return carry

        lax.fori_loop(0, self.ARRIVALS + 1, sent, 0)


def ring_scratch(table):
    dma = pltpu.SemaphoreType.DMA
    ncols = lax.axis_size("cols")
    return [
        pltpu.VMEM((ncols, *table), jnp.bfloat16),
        dma((ncols,)),
        dma((Ring.RING[-1] + 4,)),
        dma((Ring.ARRIVALS + 1,)),
        dma((Ring.CROSS[-1] + 1,)),
    ]


def block_sums(all_ref, records_ref, slots, block, width, by_prefix):
    shift = block.bit_length() - 1
    rows = range(records_ref.shape[0])
    placed, spots = [], []
    for slot in slots:
        packed = [records_ref[d, slot, 0:1, :].astype(jnp.int32) for d in rows]
        weight = [records_ref[d, slot, 1:2, :] for d in rows]
        prefix = [lax.shift_right_logical(ids, shift) for ids in packed]
        suffix = [ids & (block - 1) for ids in packed]
        take, put = (prefix, suffix) if by_prefix else (suffix, prefix)
        one, spot = weighted_rows(all_ref[slot], take, put, weight, width)
        placed.append(one)
        spots.append(spot)
    return lax.dot_general(
        jnp.concatenate(placed, axis=1),
        jnp.concatenate(spots, axis=1),
        (((1,), (1,)), ((), ())),
        preferred_element_type=jnp.float32,
    )


def sketch_kernel(block, width, part_ref, here_ref, total_ref, all_ref, *sems):
    ring = Ring(all_ref, *sems)
    ring.greet()
    all_ref[ring.own] = part_ref[...]
    ring.begin()
    total_ref[...] = jnp.zeros_like(total_ref)

    def work(slots):
        total_ref[...] += block_sums(all_ref, here_ref, slots, block, width, False)

    ring.run(work, {})


def sketch_sums(part, here, block, width):
    return pl.pallas_call(
        functools.partial(sketch_kernel, block, width),
        out_shape=jax.ShapeDtypeStruct(part.shape, jnp.float32),
        in_specs=[vmem(), vmem()],
        out_specs=vmem(),
        scratch_shapes=ring_scratch(part.shape),
        compiler_params=pltpu.CompilerParams(
            collective_id=2, has_side_effects=True, vmem_limit_bytes=40 * 2**20
        ),
        name="sketch",
    )(part, here)


def project_kernel(
    scale,
    block,
    width,
    half_ref,
    basis_ref,
    mine_ref,
    totals_ref,
    coef_ref,
    whole_ref,
    total_ref,
    half_sems,
    basis_sems,
    own_sem,
    all_ref,
    *sems,
):
    ring = Ring(all_ref, *sems)
    ring.greet(("dp", 1))
    data_at, col_at = lax.axis_index("dp"), lax.axis_index("cols")
    size = basis_ref.shape[0]
    ndata = whole_ref.shape[0] // size
    own_rows = pl.ds(pl.multiple_of(data_at * width, width), width)

    def half_copy(offset, peer):
        return put_copy(
            half_ref.at[pl.ds(pl.multiple_of(peer * width, width), width), :],
            all_ref.at[col_at, own_rows, :],
            half_sems.at[0, offset],
            half_sems.at[1, offset],
            "dp",
            peer,
        )

    along = ndata // 2
    other = lax.rem(data_at + along, ndata)

    def basis_rows(owner):
        return whole_ref.at[pl.ds(pl.multiple_of(owner * size, size), size), :]

    def basis_copy(offset, rows, source, peer):
        return put_copy(
            source, rows, basis_sems.at[0, offset], basis_sems.at[1, offset], "dp", peer
        )

    def x_copy(offset, owner, source):
        peer = data_at // along * along + lax.rem(data_at + offset, along)
        at = offset if source is basis_ref else along + offset
        return basis_copy(at, basis_rows(owner), source, peer)

    def own_x_copy(offset):
        return x_copy(offset, data_at, basis_ref)

    def other_x_copy(offset):
        return x_copy(offset, other, basis_rows(other))

    own_copy = pltpu.make_async_copy(basis_ref, basis_rows(data_at), own_sem)
    other_copy = basis_copy(0, basis_rows(data_at), basis_ref, other)

    def begun():
        other_copy.start()
        for offset in range(1, along):
            own_x_copy(offset).start()
        own_copy.start()

    def later():
        other_copy.wait_recv()
        for offset in range(1, along):
            other_x_copy(offset).start()

    def work(slots):
        total_ref[...] += block_sums(all_ref, mine_ref, slots, block, width, True)

    over_peers("dp", lambda offset, peer: half_copy(offset, peer).start())
    all_ref[col_at, own_rows, :] = half_ref[own_rows, :]
    total_ref[...] = jnp.zeros_like(total_ref)
    over_peers("dp", lambda offset, peer: half_copy(offset, peer).wait())
    ring.begin()
    ring.run(work, {0: begun, 6: later})
    factor = scale * jnp.sum(totals_ref[1]) / jnp.sum(totals_ref[0])
    for g in range(total_ref.shape[0] // width):
        coef_ref[:, g * size : (g + 1) * size] = factor * total_ref[g * width : (g + 1) * width, :]
    other_copy.wait_send()
    for offset in range(1, along):
        own_x_copy(offset).wait()
        other_x_copy(offset).wait()
    own_copy.wait()


def project(half, basis_part, mine, totals, scale, block, width):
    ndata = lax.axis_size("dp")
    size, whole = basis_part.shape
    dma = pltpu.SemaphoreType.DMA
    anywhere = pl.BlockSpec(memory_space=pl.ANY)
    return pl.pallas_call(
        functools.partial(project_kernel, scale, block, width),
        out_shape=(
            jax.ShapeDtypeStruct((width, block), jnp.float32),
            jax.ShapeDtypeStruct((size * ndata, whole), jnp.bfloat16),
        ),
        in_specs=[vmem(), anywhere, vmem(), vmem()],
        out_specs=(vmem(), anywhere),
        scratch_shapes=[
            pltpu.VMEM(half.shape, jnp.float32),
            dma((2, ndata)),
            dma((2, ndata)),
            dma,
            *ring_scratch(half.shape),
        ],
        compiler_params=pltpu.CompilerParams(
            collective_id=3, has_side_effects=True, vmem_limit_bytes=40 * 2**20
        ),
        name="project",
    )(half, basis_part, mine, totals)


def shards(prefix_ids, suffix_ids, weights, counts, omega):
    ncols = lax.axis_size("cols")
    ndata = lax.axis_size("dp")
    block, width = omega.shape
    slots = prefix_ids.shape[-1]
    chunk = width // ndata
    size = block // ndata
    data_at = lax.axis_index("dp")

    live = lax.broadcasted_iota(jnp.int32, (ncols, slots), 1) < counts.reshape(ncols, 1)
    live_weights = jnp.where(live, weights.reshape(ncols, slots), 0.0)
    prefix_local = prefix_ids.reshape(ncols, slots) & (block - 1)
    suffix_local = suffix_ids.reshape(ncols, slots) & (block - 1)
    packed = prefix_local * block + suffix_local
    own = jnp.stack([packed.astype(jnp.float32), live_weights], axis=1)
    here, mine = exchange_records(own)
    part = lax.dynamic_slice_in_dim(omega, data_at * chunk, chunk, 1)
    part = part.reshape(ndata, size, chunk).swapaxes(1, 2).reshape(ndata * chunk, size)
    sketch = sketch_sums(part, here, block, chunk)
    rows, gram, totals = sum_gram(sketch.reshape(ndata, chunk, size), mine)
    basis_part, q_half = factor_and_q(gram, rows.reshape(width, size))
    scale = math.sqrt(block * ncols)
    coefficients, q_block = project(q_half, basis_part, mine, totals, scale, block, chunk)
    basis = scale * q_block.astype(jnp.float32)
    return (basis, coefficients)


def solution(mesh):
    placed = (
        P("dp", "cols", None, None),
        P("dp", "cols", None, None),
        P("dp", "cols", None, None),
        P("dp", "cols", None),
        P("cols", None),
    )
    return jax.shard_map(
        shards,
        mesh=mesh,
        in_specs=placed,
        out_specs=(P("cols", None), P("dp", "cols")),
        check_vma=False,
    )
```

```python
import functools
import math

import jax
import jax.numpy as jnp
from jax import lax
from jax.experimental import pallas as pl
from jax.experimental.pallas import tpu as pltpu
from jax.sharding import PartitionSpec as P

HIGHEST = lax.Precision.HIGHEST


def dot_exact(a, b, dims):
    return lax.dot_general(
        a, b, (dims, ((), ())), precision=HIGHEST, preferred_element_type=jnp.float32
    )


def one_hot(ids, size):
    rows = lax.broadcasted_iota(jnp.int32, (size, ids.shape[1]), 0)
    return jnp.where(rows == ids, 1.0, 0.0).astype(jnp.bfloat16)


def weighted_rows(table, take, put, weight, width):
    size = table.shape[1]
    groups = table.shape[0] // width
    shift = size.bit_length() - 1
    beside = functools.partial(jnp.concatenate, axis=1)
    picked = jnp.dot(
        table,
        beside([one_hot(ids & (size - 1), size) for ids in take]),
        preferred_element_type=jnp.float32,
    )
    take_group = beside([lax.shift_right_logical(ids, shift) for ids in take])
    put_group = beside([lax.shift_right_logical(ids, shift) for ids in put])
    row = picked[:width]
    for g in range(1, groups):
        row = jnp.where(take_group == g, picked[g * width : (g + 1) * width], row)
    row = beside(weight) * row
    placed = jnp.concatenate(
        [jnp.where(put_group == g, row, 0.0).astype(jnp.bfloat16) for g in range(groups)], axis=0
    )
    return placed, beside([one_hot(ids & (size - 1), size) for ids in put])


def vmem():
    return pl.BlockSpec(memory_space=pltpu.VMEM)


def put_copy(src, dst, send, recv, axis, peer):
    return pltpu.make_async_remote_copy(
        src_ref=src,
        dst_ref=dst,
        send_sem=send,
        recv_sem=recv,
        device_id={axis: peer},
        device_id_type=pl.DeviceIdType.MESH,
    )


def over_peers(axis, act, stride=1):
    count = lax.axis_size(axis)
    me = lax.axis_index(axis)

    def one(offset, carry):
        act(offset, lax.rem(me + stride * offset, count))
        return carry

    lax.fori_loop(1, count // stride, one, 0)


def signal(barrier, axis, peer):
    pl.semaphore_signal(
        barrier, inc=1, device_id={axis: peer}, device_id_type=pl.DeviceIdType.MESH
    )


def greet(*groups, near=()):
    barrier = pltpu.get_barrier_semaphore()
    for peer in near:
        signal(barrier, "cols", peer)
    for axis, stride in groups:
        over_peers(axis, lambda offset, peer, axis=axis: signal(barrier, axis, peer), stride)
    count = sum(lax.axis_size(axis) // stride - 1 for axis, stride in groups)
    pl.semaphore_wait(barrier, count + len(near))


def lower_blocks(width, lanes):
    return [(i, j) for i in range(width // lanes) for j in range(i + 1)]


def rows_at(start, count):
    return pl.ds(pl.multiple_of(start, 8), count)


def gram_steps(
    total_ref,
    mine_ref,
    rows_ref,
    gram_ref,
    totals_ref,
    part_ref,
    half_ref,
    other_ref,
    got_ref,
    piece_ref,
    arrived_ref,
    shared_ref,
    own_ref,
    sum_ref,
    rows_sems,
    pair_sems,
    part_sems,
    piece_sems,
    shared_sems,
    gram_sems,
):
    data_at, col_at = lax.axis_index("dp"), lax.axis_index("cols")
    core, chip = lax.rem(col_at, 2), col_at // 2
    pair = col_at + 1 - 2 * core
    ndata, chunk, size = rows_ref.shape
    width = ndata * chunk
    lanes = part_ref.shape[1]
    half = half_ref.shape[0]
    share = half // ndata
    chips = piece_ref.shape[0]
    few = share // chips

    def rows_copy(offset, peer):
        return put_copy(
            total_ref.at[rows_at(peer * chunk, chunk), :],
            rows_ref.at[data_at],
            rows_sems.at[0, offset],
            rows_sems.at[1, offset],
            "dp",
            peer,
        )

    over_peers("dp", lambda offset, peer: rows_copy(offset, peer).start())
    rows_ref[data_at] = total_ref[rows_at(data_at * chunk, chunk), :]
    weight = mine_ref[:, :, 1, :]
    for at, term in ((0, weight), (1, (weight > 0.0).astype(jnp.float32))):
        term = jnp.sum(term, axis=0).reshape(-1, *totals_ref.shape[1:])
        sum_ref[0, at] = jnp.sum(term, axis=0)
    sums_copy = put_copy(
        sum_ref.at[0], sum_ref.at[1], pair_sems.at[0, 0], pair_sems.at[1, 0], "cols", pair
    )
    sums_copy.start()
    piece_ref[...] = jnp.zeros_like(piece_ref)
    over_peers("dp", lambda offset, peer: rows_copy(offset, peer).wait())
    rows = rows_ref[...].reshape(width, size)
    gram = dot_exact(rows, rows, ((1,), (1,)))
    for at, (i, j) in enumerate(lower_blocks(width, lanes)):
        part_ref[lanes * at : lanes * (at + 1), :] = gram[
            lanes * i : lanes * (i + 1), lanes * j : lanes * (j + 1)
        ]

    pair_copy = put_copy(
        part_ref.at[rows_at((1 - core) * half, half), :],
        other_ref,
        pair_sems.at[0, 1],
        pair_sems.at[1, 1],
        "cols",
        pair,
    )
    pair_copy.start()
    sums_copy.wait()
    shared_ref[chip, 1] = sum_ref[0, 0] + sum_ref[1, 0]
    shared_ref[chip, 2] = sum_ref[0, 1] + sum_ref[1, 1]
    pair_copy.wait()
    half_ref[...] = part_ref[rows_at(core * half, half), :] + other_ref[...]

    def part_copy(offset, peer):
        return put_copy(
            half_ref.at[rows_at(peer * share, share), :],
            got_ref.at[data_at],
            part_sems.at[0, offset],
            part_sems.at[1, offset],
            "dp",
            peer,
        )

    over_peers("dp", lambda offset, peer: part_copy(offset, peer).start())
    got_ref[data_at] = half_ref[rows_at(data_at * share, share), :]
    over_peers("dp", lambda offset, peer: part_copy(offset, peer).wait())
    summed = jnp.sum(got_ref[...], axis=0)
    for at in range(chips):
        piece_ref[at, :few] = summed[few * at : few * (at + 1)]

    def piece_copy(offset, peer):
        return put_copy(
            piece_ref.at[peer // 2],
            arrived_ref.at[chip],
            piece_sems.at[0, offset],
            piece_sems.at[1, offset],
            "cols",
            peer,
        )

    over_peers("cols", lambda offset, peer: piece_copy(offset, peer).start(), 2)
    arrived_ref[chip] = piece_ref[chip]
    over_peers("cols", lambda offset, peer: piece_copy(offset, peer).wait(), 2)
    shared_ref[chip, 0] = jnp.sum(arrived_ref[...], axis=0)

    def shared_copy(offset, peer):
        return put_copy(
            shared_ref.at[chip],
            shared_ref.at[chip],
            shared_sems.at[0, offset],
            shared_sems.at[1, offset],
            "cols",
            peer,
        )

    over_peers("cols", lambda offset, peer: shared_copy(offset, peer).start(), 2)
    over_peers("cols", lambda offset, peer: shared_copy(offset, peer).wait(), 2)
    for at in range(chips):
        own_ref[few * at : few * (at + 1), :] = shared_ref[at, 0, :few, :]
    own_rows = rows_at((core * ndata + data_at) * share, share)

    def gram_copy(offset, peer):
        return put_copy(
            own_ref,
            gram_ref.at[own_rows, :],
            gram_sems.at[0, offset],
            gram_sems.at[1, offset],
            "dp",
            peer,
        )

    over_peers("dp", lambda offset, peer: gram_copy(offset, peer).start())
    gram_ref[own_rows, :] = own_ref[...]
    totals_ref[0] = jnp.sum(shared_ref[:, 1], axis=0)
    totals_ref[1] = jnp.sum(shared_ref[:, 2], axis=0)
    over_peers("dp", lambda offset, peer: gram_copy(offset, peer).wait())
    own_half = gram_ref.at[rows_at(core * half, half), :]
    last_copy = put_copy(
        own_half, own_half, pair_sems.at[0, 2], pair_sems.at[1, 2], "cols", pair
    )
    last_copy.start()
    last_copy.wait()


def corner_inverse(tile, pivots=8):
    n = tile.shape[0]
    blocks = n // pivots

    def full(x):
        return jnp.broadcast_to(x, (pivots, n))

    work = [tile[pivots * i : pivots * (i + 1), :] for i in range(blocks)]
    lane = lax.broadcasted_iota(jnp.int32, (pivots, n), 1)
    sub = lax.broadcasted_iota(jnp.int32, (pivots, n), 0)
    done = []
    for at in range(blocks):
        start = at * pivots
        group = (lane >= start) & (lane < start + pivots)
        cols = [full(work[at][:, start + c : start + c + 1]) for c in range(pivots)]
        left = [[full(cols[c][r : r + 1, :]) for c in range(r + 1)] for r in range(pivots)]
        rows = [
            jnp.where(group, jnp.where(lane == start + r, 1.0, 0.0), full(work[at][r : r + 1, :]))
            for r in range(pivots)
        ]
        recip = [None] * pivots
        low = [[None] * pivots for _ in range(pivots)]
        for c in range(pivots):
            recip[c] = 1.0 / left[c][c]
            for r in range(c + 1, pivots):
                low[r][c] = left[r][c] * recip[c]
                for e in range(c + 1, r + 1):
                    left[r][e] = left[r][e] - low[r][c] * left[e][c]
        for r in range(pivots):
            for c in range(r):
                rows[r] = rows[r] - low[r][c] * rows[c]
        result = jnp.zeros((pivots, n), jnp.float32)
        for r in range(pivots):
            result = jnp.where(sub == r, rows[r] * lax.rsqrt(left[r][r]), result)
        done.append(jnp.where(lane <= sub + start, result, 0.0))
        back = [rows[r] * recip[r] for r in range(pivots)]
        for r in range(pivots - 1, -1, -1):
            for c in range(r):
                back[c] = back[c] - low[r][c] * back[r]
        for i in range(at + 1, blocks):
            rest = jnp.where(group, 0.0, work[i])
            for c in range(pivots):
                rest = rest - full(work[i][:, start + c : start + c + 1]) * back[c]
            work[i] = rest
    return jnp.concatenate(done, axis=0)


def factor_kernel(gram_ref, rows_ref, basis_ref, half_ref, work_ref, inverse_ref):
    n = work_ref.shape[0]
    size = gram_ref.shape[1]
    for at, (i, j) in enumerate(lower_blocks(n, size)):
        work_ref[size * i : size * (i + 1), size * j : size * (j + 1)] = gram_ref[
            size * at : size * (at + 1), :
        ]
    for start in range(0, n, size):
        end = start + size
        corner = corner_inverse(work_ref[start:end, start:end])
        if start:
            inverse_ref[start:end, :start] = dot_exact(
                corner, inverse_ref[start:end, :start], ((1,), (0,))
            )
        inverse_ref[start:end, start:end] = corner
        if end < n:
            low = dot_exact(work_ref[end:, start:end], corner, ((1,), (1,)))
            work_ref[end:, end:] -= dot_exact(low, low, ((1,), (1,)))
            if start:
                inverse_ref[end:, :start] -= dot_exact(
                    low, inverse_ref[start:end, :start], ((1,), (0,))
                )
            inverse_ref[end:, start:end] = -dot_exact(low, corner, ((1,), (0,)))
    for start in range(0, n, size):
        end = start + size
        q = dot_exact(inverse_ref[start:end, :end], rows_ref[:end, :], ((1,), (0,)))
        half_ref[start:end, :] = q.astype(jnp.bfloat16)
        basis_ref[:, start:end] = q.T.astype(jnp.bfloat16)


def factor_and_q(gram, rows):
    width, size = rows.shape
    return pl.pallas_call(
        factor_kernel,
        out_shape=(
            jax.ShapeDtypeStruct((size, width), jnp.bfloat16),
            jax.ShapeDtypeStruct((width, size), jnp.bfloat16),
        ),
        in_specs=[vmem(), vmem()],
        out_specs=(vmem(), vmem()),
        scratch_shapes=[pltpu.VMEM((width, width), jnp.float32)] * 2,
        compiler_params=pltpu.CompilerParams(vmem_limit_bytes=24 * 2**20),
        name="factor",
    )(gram, rows)


class Ring:
    ARRIVALS = 15
    RING = (0, 1, 3, 4, 5, 7, 8)
    CROSS = (1, 5, 9, 12)

    def __init__(self, lead, all_ref, got_sems, ring_sems, pair_sems, cross_sems):
        self.lead = lead
        self.all_ref, self.got_sems = all_ref, got_sems
        self.ring_sems, self.pair_sems, self.cross_sems = ring_sems, pair_sems, cross_sems
        at = lax.axis_index("cols")
        self.length = lax.axis_size("cols") // 4
        assert self.length == 8
        self.z, quad = at // 4, lax.rem(at, 4)
        self.y, self.core = quad // 2, lax.rem(quad, 2)
        self.way = 1 - 2 * self.core
        self.own = at
        self.pair = self.device(0, 0, 1)
        self.across = self.device(0, 1, 0)
        self.after = self.device(-1, 0, 0)
        self.before = self.device(1, 0, 0)
        self.diagonal = self.device(0, 1, 1)

    def device(self, away, row, core, mirror=False):
        way = -self.way if mirror else self.way
        z = lax.rem(self.z - way * away + self.length, self.length)
        y = lax.rem(self.y + row, 2)
        core = lax.rem(self.core + core + (1 if mirror else 0), 2)
        return z * 4 + y * 2 + core

    def place(self, n):
        return n + n // 13

    def slot(self, m, mirror=False):
        turn = lax.rem(m, 4)
        away = m // 4 + 1 - (turn // 2 - turn // 3)
        return self.device(away, turn // 2, lax.rem((turn + 1) // 2, 2), mirror)

    def greet(self, *groups):
        greet(*groups, near=(self.pair, self.across, self.after, self.before))

    def copy(self, slot, send, peer):
        part = self.all_ref.at[slot]
        return put_copy(part, part, send, self.got_sems.at[slot], "cols", peer)

    def arrived(self, slot):
        self.copy(slot, self.cross_sems.at[0], self.pair).wait_recv()

    def to_ring(self, slot, at):
        self.copy(slot, self.ring_sems.at[at], self.after).start()

    def to_pair(self, slot, at):
        self.copy(slot, self.pair_sems.at[at], self.pair).start()

    def to_across(self, slot, at):
        self.copy(slot, self.cross_sems.at[at], self.across).start()

    def hand_on(self, n):
        m = self.place(n)
        slot = self.slot(m)
        self.arrived(slot)
        turn, step = lax.rem(m, 4), m // 4 + 1

        @pl.when((turn == 0) & (step < 4))
        def _():
            self.to_ring(slot, m + 3)

        @pl.when((turn == 1) & (step < 3))
        def _():
            self.to_ring(slot, m + 3)

        @pl.when(m == 3)
        def _():
            self.to_ring(slot, m + 3)

        @pl.when(m == 8)
        def _():
            self.to_ring(self.slot(7), 7 + 3)

        @pl.when((turn == 1) | (m == 12))
        def _():
            self.to_across(slot, m)

        @pl.when(m != 2)
        def _():
            self.to_pair(slot, n + 1)

    def begin(self, first=None, second=None):
        self.to_pair(self.own, 0)
        self.to_ring(self.own, 0)
        self.to_across(self.own, 0)
        if first is not None:
            first()
        self.arrived(self.pair)
        self.to_ring(self.pair, 1)
        self.arrived(self.across)
        self.to_ring(self.across, 2)
        self.to_pair(self.across, 3)
        self.hand_on(0)
        if second is not None:
            second()

        def early(n, carry):
            self.hand_on(n)
            return carry

        lax.fori_loop(1, self.lead, early, 0)

    def run(self, work, also):
        work([self.own, self.pair])
        last = self.ARRIVALS - 1

        def one(n, carry):
            for at, act in also.items():
                pl.when(n == at)(act)

            @pl.when(n + self.lead <= last)
            def _():
                ahead = n + self.lead
                swap = ahead // 11 - 2 * (ahead // 12) + ahead // 13
                self.hand_on(ahead + swap)

            m = self.place(n)
            mirrored = self.slot(m, mirror=True)

            @pl.when(m != 2)
            def _():
                self.arrived(mirrored)

            work([self.slot(m), mirrored])
            return carry

        lax.fori_loop(0, self.ARRIVALS, one, 0)
        for at in [0, 1, 2, *(m + 3 for m in self.RING)]:
            self.copy(self.own, self.ring_sems.at[at], self.after).wait_send()
        for at in [0, *self.CROSS]:
            self.copy(self.own, self.cross_sems.at[at], self.across).wait_send()

        def sent(at, carry):
            self.copy(self.own, self.pair_sems.at[at], self.pair).wait_send()
            return carry

        lax.fori_loop(0, self.ARRIVALS + 1, sent, 0)


def ring_scratch(table):
    dma = pltpu.SemaphoreType.DMA
    ncols = lax.axis_size("cols")
    return [
        pltpu.VMEM((ncols, *table), jnp.bfloat16),
        dma((ncols,)),
        dma((Ring.RING[-1] + 4,)),
        dma((Ring.ARRIVALS + 1,)),
        dma((Ring.CROSS[-1] + 1,)),
    ]


def block_sums(all_ref, records_ref, slots, block, width, by_prefix):
    shift = block.bit_length() - 1
    rows = range(records_ref.shape[0])
    placed, spots = [], []
    for slot in slots:
        packed = [records_ref[d, slot, 0:1, :].astype(jnp.int32) for d in rows]
        weight = [records_ref[d, slot, 1:2, :] for d in rows]
        prefix = [lax.shift_right_logical(ids, shift) for ids in packed]
        suffix = [ids & (block - 1) for ids in packed]
        take, put = (prefix, suffix) if by_prefix else (suffix, prefix)
        one, spot = weighted_rows(all_ref[slot], take, put, weight, width)
        placed.append(one)
        spots.append(spot)
    return lax.dot_general(
        jnp.concatenate(placed, axis=1),
        jnp.concatenate(spots, axis=1),
        (((1,), (1,)), ((), ())),
        preferred_element_type=jnp.float32,
    )


def sketch_kernel(block, width, own_ref, part_ref, mine_ref, rows_ref, gram_ref, totals_ref, *scratch):
    here_ref, total_ref, col_sems, here_sems, mine_sems, *scratch = scratch
    ring = Ring(5, *scratch[:5])
    data_at, col_at = lax.axis_index("dp"), lax.axis_index("cols")
    greet(("cols", 1), ("dp", 1))

    def to_col(offset, peer):
        return put_copy(
            own_ref.at[peer],
            here_ref.at[data_at, col_at],
            col_sems.at[0, offset],
            col_sems.at[1, offset],
            "cols",
            peer,
        )

    def mine_to_data(offset, peer):
        return put_copy(
            own_ref,
            mine_ref.at[data_at],
            mine_sems.at[0, offset],
            mine_sems.at[1, offset],
            "dp",
            peer,
        )

    def here_to_data(offset, peer):
        return put_copy(
            here_ref.at[data_at],
            here_ref.at[data_at],
            here_sems.at[0, offset],
            here_sems.at[1, offset],
            "dp",
            peer,
        )

    def first():
        over_peers("cols", lambda offset, peer: to_col(offset, peer).start())
        here_ref[data_at, col_at] = own_ref[col_at]
        mine_ref[data_at] = own_ref[...]

    def second():
        over_peers("cols", lambda offset, peer: to_col(offset, peer).wait())
        over_peers("dp", lambda offset, peer: here_to_data(offset, peer).start())
        over_peers("dp", lambda offset, peer: mine_to_data(offset, peer).start())

    all_ref = scratch[0]
    all_ref[ring.own] = part_ref[...]
    ring.begin(first, second)
    total_ref[...] = jnp.zeros_like(total_ref)
    over_peers("dp", lambda offset, peer: here_to_data(offset, peer).wait())

    def work(slots):
        total_ref[...] += block_sums(all_ref, here_ref, slots, block, width, False)

    ring.run(work, {})
    over_peers("dp", lambda offset, peer: mine_to_data(offset, peer).wait())
    gram_steps(total_ref, mine_ref, rows_ref, gram_ref, totals_ref, *scratch[5:])


def sketch_and_gram(own, part, block, width):
    ndata, ncols = lax.axis_size("dp"), lax.axis_size("cols")
    whole, size = part.shape
    chips = ncols // 2
    lanes = own.shape[-1]
    f32 = jnp.float32
    packed = len(lower_blocks(whole, lanes)) * lanes
    half = packed // 2
    share = half // ndata
    tile = (8, lanes)
    assert share % 8 == 0 and share % chips == 0 and share // chips <= 8
    dma = pltpu.SemaphoreType.DMA
    return pl.pallas_call(
        functools.partial(sketch_kernel, block, width),
        out_shape=(
            jax.ShapeDtypeStruct((ndata, *own.shape), f32),
            jax.ShapeDtypeStruct((ndata, width, size), f32),
            jax.ShapeDtypeStruct((packed, lanes), f32),
            jax.ShapeDtypeStruct((2, *tile), f32),
        ),
        in_specs=[vmem(), vmem()],
        out_specs=(vmem(), vmem(), vmem(), vmem()),
        scratch_shapes=[
            pltpu.VMEM((ndata, *own.shape), f32),
            pltpu.VMEM((whole, size), f32),
            dma((2, ncols)),
            dma((2, ndata)),
            dma((2, ndata)),
            *ring_scratch(part.shape),
            pltpu.VMEM((packed, lanes), f32),
            pltpu.VMEM((half, lanes), f32),
            pltpu.VMEM((half, lanes), f32),
            pltpu.VMEM((ndata, share, lanes), f32),
            pltpu.VMEM((chips, *tile), f32),
            pltpu.VMEM((chips, *tile), f32),
            pltpu.VMEM((chips, 3, *tile), f32),
            pltpu.VMEM((share, lanes), f32),
            pltpu.VMEM((2, 2, *tile), f32),
            dma((2, ndata)),
            dma((2, 3)),
            dma((2, ndata)),
            dma((2, chips)),
            dma((2, chips)),
            dma((2, ndata)),
        ],
        compiler_params=pltpu.CompilerParams(
            collective_id=0, has_side_effects=True, vmem_limit_bytes=40 * 2**20
        ),
        name="sketch",
    )(own, part)


def project_kernel(
    scale,
    block,
    width,
    half_ref,
    basis_ref,
    mine_ref,
    totals_ref,
    coef_ref,
    whole_ref,
    total_ref,
    half_sems,
    basis_sems,
    own_sem,
    all_ref,
    *sems,
):
    ring = Ring(1, all_ref, *sems)
    ring.greet(("dp", 1))
    data_at, col_at = lax.axis_index("dp"), lax.axis_index("cols")
    size = basis_ref.shape[0]
    ndata = whole_ref.shape[0] // size
    own_rows = pl.ds(pl.multiple_of(data_at * width, width), width)

    def half_copy(offset, peer):
        return put_copy(
            half_ref.at[pl.ds(pl.multiple_of(peer * width, width), width), :],
            all_ref.at[col_at, own_rows, :],
            half_sems.at[0, offset],
            half_sems.at[1, offset],
            "dp",
            peer,
        )

    along = ndata // 2
    other = lax.rem(data_at + along, ndata)

    def basis_rows(owner):
        return whole_ref.at[pl.ds(pl.multiple_of(owner * size, size), size), :]

    def basis_copy(offset, rows, source, peer):
        return put_copy(
            source, rows, basis_sems.at[0, offset], basis_sems.at[1, offset], "dp", peer
        )

    def x_copy(offset, owner, source):
        peer = data_at // along * along + lax.rem(data_at + offset, along)
        at = offset if source is basis_ref else along + offset
        return basis_copy(at, basis_rows(owner), source, peer)

    def own_x_copy(offset):
        return x_copy(offset, data_at, basis_ref)

    def other_x_copy(offset):
        return x_copy(offset, other, basis_rows(other))

    own_copy = pltpu.make_async_copy(basis_ref, basis_rows(data_at), own_sem)
    other_copy = basis_copy(0, basis_rows(data_at), basis_ref, other)

    def begun():
        other_copy.start()
        for offset in range(1, along):
            own_x_copy(offset).start()
        own_copy.start()

    def later():
        other_copy.wait_recv()
        for offset in range(1, along):
            other_x_copy(offset).start()

    def work(slots):
        total_ref[...] += block_sums(all_ref, mine_ref, slots, block, width, True)

    over_peers("dp", lambda offset, peer: half_copy(offset, peer).start())
    all_ref[col_at, own_rows, :] = half_ref[own_rows, :]
    total_ref[...] = jnp.zeros_like(total_ref)
    over_peers("dp", lambda offset, peer: half_copy(offset, peer).wait())
    ring.begin()
    ring.run(work, {0: begun, 6: later})
    factor = scale * jnp.sum(totals_ref[1]) / jnp.sum(totals_ref[0])
    for g in range(total_ref.shape[0] // width):
        coef_ref[:, g * size : (g + 1) * size] = factor * total_ref[g * width : (g + 1) * width, :]
    other_copy.wait_send()
    for offset in range(1, along):
        own_x_copy(offset).wait()
        other_x_copy(offset).wait()
    own_copy.wait()


def project(half, basis_part, mine, totals, scale, block, width):
    ndata = lax.axis_size("dp")
    size, whole = basis_part.shape
    dma = pltpu.SemaphoreType.DMA
    anywhere = pl.BlockSpec(memory_space=pl.ANY)
    return pl.pallas_call(
        functools.partial(project_kernel, scale, block, width),
        out_shape=(
            jax.ShapeDtypeStruct((width, block), jnp.float32),
            jax.ShapeDtypeStruct((size * ndata, whole), jnp.bfloat16),
        ),
        in_specs=[vmem(), anywhere, vmem(), vmem()],
        out_specs=(vmem(), anywhere),
        scratch_shapes=[
            pltpu.VMEM(half.shape, jnp.float32),
            dma((2, ndata)),
            dma((2, ndata)),
            dma,
            *ring_scratch(half.shape),
        ],
        compiler_params=pltpu.CompilerParams(
            collective_id=1, has_side_effects=True, vmem_limit_bytes=40 * 2**20
        ),
        name="project",
    )(half, basis_part, mine, totals)


def shards(prefix_ids, suffix_ids, weights, counts, omega):
    ncols = lax.axis_size("cols")
    ndata = lax.axis_size("dp")
    block, width = omega.shape
    slots = prefix_ids.shape[-1]
    chunk = width // ndata
    size = block // ndata
    data_at = lax.axis_index("dp")

    live = lax.broadcasted_iota(jnp.int32, (ncols, slots), 1) < counts.reshape(ncols, 1)
    live_weights = jnp.where(live, weights.reshape(ncols, slots), 0.0)
    prefix_local = prefix_ids.reshape(ncols, slots) & (block - 1)
    suffix_local = suffix_ids.reshape(ncols, slots) & (block - 1)
    packed = prefix_local * block + suffix_local
    own = jnp.stack([packed.astype(jnp.float32), live_weights], axis=1)
    part = lax.dynamic_slice_in_dim(omega, data_at * chunk, chunk, 1)
    part = part.reshape(ndata, size, chunk).swapaxes(1, 2).reshape(ndata * chunk, size)
    mine, rows, gram, totals = sketch_and_gram(own, part, block, chunk)
    basis_part, q_half = factor_and_q(gram, rows.reshape(width, size))
    scale = math.sqrt(block * ncols)
    coefficients, q_block = project(q_half, basis_part, mine, totals, scale, block, chunk)
    basis = scale * q_block.astype(jnp.float32)
    return (basis, coefficients)


def solution(mesh):
    placed = (
        P("dp", "cols", None, None),
        P("dp", "cols", None, None),
        P("dp", "cols", None, None),
        P("dp", "cols", None),
        P("cols", None),
    )
    return jax.shard_map(
        shards,
        mesh=mesh,
        in_specs=placed,
        out_specs=(P("cols", None), P("dp", "cols")),
        check_vma=False,
    )
```

```python
import functools
import math

import jax
import jax.numpy as jnp
from jax import lax
from jax.experimental import pallas as pl
from jax.experimental.pallas import tpu as pltpu
from jax.sharding import PartitionSpec as P

HIGHEST = lax.Precision.HIGHEST


def dot_exact(a, b, dims):
    return lax.dot_general(
        a, b, (dims, ((), ())), precision=HIGHEST, preferred_element_type=jnp.float32
    )


def one_hot(ids, size):
    rows = lax.broadcasted_iota(jnp.int32, (size, ids.shape[1]), 0)
    return jnp.where(rows == ids, 1.0, 0.0).astype(jnp.bfloat16)


def weighted_rows(table, take, put, weight, width):
    size = table.shape[1]
    groups = table.shape[0] // width
    shift = size.bit_length() - 1
    beside = functools.partial(jnp.concatenate, axis=1)
    picked = jnp.dot(
        table,
        beside([one_hot(ids & (size - 1), size) for ids in take]),
        preferred_element_type=jnp.float32,
    )
    take_group = beside([lax.shift_right_logical(ids, shift) for ids in take])
    put_group = beside([lax.shift_right_logical(ids, shift) for ids in put])
    row = picked[:width]
    for g in range(1, groups):
        row = jnp.where(take_group == g, picked[g * width : (g + 1) * width], row)
    row = beside(weight) * row
    placed = jnp.concatenate(
        [jnp.where(put_group == g, row, 0.0).astype(jnp.bfloat16) for g in range(groups)], axis=0
    )
    return placed, beside([one_hot(ids & (size - 1), size) for ids in put])


def vmem():
    return pl.BlockSpec(memory_space=pltpu.VMEM)


def put_copy(src, dst, send, recv, axis, peer):
    return pltpu.make_async_remote_copy(
        src_ref=src,
        dst_ref=dst,
        send_sem=send,
        recv_sem=recv,
        device_id={axis: peer},
        device_id_type=pl.DeviceIdType.MESH,
    )


def over_peers(axis, act, stride=1):
    count = lax.axis_size(axis)
    me = lax.axis_index(axis)

    def one(offset, carry):
        act(offset, lax.rem(me + stride * offset, count))
        return carry

    lax.fori_loop(1, count // stride, one, 0)


def signal(barrier, axis, peer):
    pl.semaphore_signal(
        barrier, inc=1, device_id={axis: peer}, device_id_type=pl.DeviceIdType.MESH
    )


def greet(*groups, near=()):
    barrier = pltpu.get_barrier_semaphore()
    for peer in near:
        signal(barrier, "cols", peer)
    for axis, stride in groups:
        over_peers(axis, lambda offset, peer, axis=axis: signal(barrier, axis, peer), stride)
    count = sum(lax.axis_size(axis) // stride - 1 for axis, stride in groups)
    pl.semaphore_wait(barrier, count + len(near))


def lower_blocks(width, lanes):
    return [(i, j) for i in range(width // lanes) for j in range(i + 1)]


def rows_at(start, count):
    return pl.ds(pl.multiple_of(start, 8), count)


def gram_steps(
    total_ref,
    mine_ref,
    rows_ref,
    gram_ref,
    totals_ref,
    part_ref,
    half_ref,
    other_ref,
    got_ref,
    piece_ref,
    arrived_ref,
    shared_ref,
    own_ref,
    sum_ref,
    rows_sems,
    pair_sems,
    part_sems,
    piece_sems,
    shared_sems,
    gram_sems,
):
    data_at, col_at = lax.axis_index("dp"), lax.axis_index("cols")
    core, chip = lax.rem(col_at, 2), col_at // 2
    pair = col_at + 1 - 2 * core
    ndata, chunk, size = rows_ref.shape
    width = ndata * chunk
    lanes = part_ref.shape[1]
    half = half_ref.shape[0]
    share = half // ndata
    chips = piece_ref.shape[0]
    few = share // chips

    def rows_copy(offset, peer):
        return put_copy(
            total_ref.at[rows_at(peer * chunk, chunk), :],
            rows_ref.at[data_at],
            rows_sems.at[0, offset],
            rows_sems.at[1, offset],
            "dp",
            peer,
        )

    over_peers("dp", lambda offset, peer: rows_copy(offset, peer).start())
    rows_ref[data_at] = total_ref[rows_at(data_at * chunk, chunk), :]
    weight = mine_ref[:, :, 1, :]
    for at, term in ((0, weight), (1, (weight > 0.0).astype(jnp.float32))):
        term = jnp.sum(term, axis=0).reshape(-1, *totals_ref.shape[1:])
        sum_ref[0, at] = jnp.sum(term, axis=0)
    sums_copy = put_copy(
        sum_ref.at[0], sum_ref.at[1], pair_sems.at[0, 0], pair_sems.at[1, 0], "cols", pair
    )
    sums_copy.start()
    piece_ref[...] = jnp.zeros_like(piece_ref)
    over_peers("dp", lambda offset, peer: rows_copy(offset, peer).wait())
    rows = rows_ref[...].reshape(width, size)
    gram = dot_exact(rows, rows, ((1,), (1,)))
    for at, (i, j) in enumerate(lower_blocks(width, lanes)):
        part_ref[lanes * at : lanes * (at + 1), :] = gram[
            lanes * i : lanes * (i + 1), lanes * j : lanes * (j + 1)
        ]

    pair_copy = put_copy(
        part_ref.at[rows_at((1 - core) * half, half), :],
        other_ref,
        pair_sems.at[0, 1],
        pair_sems.at[1, 1],
        "cols",
        pair,
    )
    pair_copy.start()
    sums_copy.wait()
    shared_ref[chip, 1] = sum_ref[0, 0] + sum_ref[1, 0]
    shared_ref[chip, 2] = sum_ref[0, 1] + sum_ref[1, 1]
    pair_copy.wait()
    half_ref[...] = part_ref[rows_at(core * half, half), :] + other_ref[...]

    def part_copy(offset, peer):
        return put_copy(
            half_ref.at[rows_at(peer * share, share), :],
            got_ref.at[data_at],
            part_sems.at[0, offset],
            part_sems.at[1, offset],
            "dp",
            peer,
        )

    over_peers("dp", lambda offset, peer: part_copy(offset, peer).start())
    got_ref[data_at] = half_ref[rows_at(data_at * share, share), :]
    over_peers("dp", lambda offset, peer: part_copy(offset, peer).wait())
    summed = jnp.sum(got_ref[...], axis=0)
    for at in range(chips):
        piece_ref[at, :few] = summed[few * at : few * (at + 1)]

    def piece_copy(offset, peer):
        return put_copy(
            piece_ref.at[peer // 2],
            arrived_ref.at[chip],
            piece_sems.at[0, offset],
            piece_sems.at[1, offset],
            "cols",
            peer,
        )

    over_peers("cols", lambda offset, peer: piece_copy(offset, peer).start(), 2)
    arrived_ref[chip] = piece_ref[chip]
    over_peers("cols", lambda offset, peer: piece_copy(offset, peer).wait(), 2)
    shared_ref[chip, 0] = jnp.sum(arrived_ref[...], axis=0)

    def shared_copy(offset, peer):
        return put_copy(
            shared_ref.at[chip],
            shared_ref.at[chip],
            shared_sems.at[0, offset],
            shared_sems.at[1, offset],
            "cols",
            peer,
        )

    over_peers("cols", lambda offset, peer: shared_copy(offset, peer).start(), 2)
    over_peers("cols", lambda offset, peer: shared_copy(offset, peer).wait(), 2)
    for at in range(chips):
        own_ref[few * at : few * (at + 1), :] = shared_ref[at, 0, :few, :]
    own_rows = rows_at((core * ndata + data_at) * share, share)

    def gram_copy(offset, peer):
        return put_copy(
            own_ref,
            gram_ref.at[own_rows, :],
            gram_sems.at[0, offset],
            gram_sems.at[1, offset],
            "dp",
            peer,
        )

    over_peers("dp", lambda offset, peer: gram_copy(offset, peer).start())
    gram_ref[own_rows, :] = own_ref[...]
    totals_ref[0] = jnp.sum(shared_ref[:, 1], axis=0)
    totals_ref[1] = jnp.sum(shared_ref[:, 2], axis=0)
    over_peers("dp", lambda offset, peer: gram_copy(offset, peer).wait())
    own_half = gram_ref.at[rows_at(core * half, half), :]
    last_copy = put_copy(
        own_half, own_half, pair_sems.at[0, 2], pair_sems.at[1, 2], "cols", pair
    )
    last_copy.start()
    last_copy.wait()


def corner_inverse(tile, pivots=8):
    n = tile.shape[0]
    blocks = n // pivots

    def full(x):
        return jnp.broadcast_to(x, (pivots, n))

    work = [tile[pivots * i : pivots * (i + 1), :] for i in range(blocks)]
    lane = lax.broadcasted_iota(jnp.int32, (pivots, n), 1)
    sub = lax.broadcasted_iota(jnp.int32, (pivots, n), 0)
    done = []
    for at in range(blocks):
        start = at * pivots
        group = (lane >= start) & (lane < start + pivots)
        cols = [full(work[at][:, start + c : start + c + 1]) for c in range(pivots)]
        left = [[full(cols[c][r : r + 1, :]) for c in range(r + 1)] for r in range(pivots)]
        rows = [
            jnp.where(group, jnp.where(lane == start + r, 1.0, 0.0), full(work[at][r : r + 1, :]))
            for r in range(pivots)
        ]
        recip = [None] * pivots
        low = [[None] * pivots for _ in range(pivots)]
        for c in range(pivots):
            recip[c] = 1.0 / left[c][c]
            for r in range(c + 1, pivots):
                low[r][c] = left[r][c] * recip[c]
                for e in range(c + 1, r + 1):
                    left[r][e] = left[r][e] - low[r][c] * left[e][c]
        for r in range(pivots):
            for c in range(r):
                rows[r] = rows[r] - low[r][c] * rows[c]
        result = jnp.zeros((pivots, n), jnp.float32)
        for r in range(pivots):
            result = jnp.where(sub == r, rows[r] * lax.rsqrt(left[r][r]), result)
        done.append(jnp.where(lane <= sub + start, result, 0.0))
        back = [rows[r] * recip[r] for r in range(pivots)]
        for r in range(pivots - 1, -1, -1):
            for c in range(r):
                back[c] = back[c] - low[r][c] * back[r]
        for i in range(at + 1, blocks):
            rest = jnp.where(group, 0.0, work[i])
            for c in range(pivots):
                rest = rest - full(work[i][:, start + c : start + c + 1]) * back[c]
            work[i] = rest
    return jnp.concatenate(done, axis=0)


def factor_kernel(gram_ref, rows_ref, basis_ref, half_ref, work_ref, inverse_ref):
    n = work_ref.shape[0]
    size = gram_ref.shape[1]
    for at, (i, j) in enumerate(lower_blocks(n, size)):
        work_ref[size * i : size * (i + 1), size * j : size * (j + 1)] = gram_ref[
            size * at : size * (at + 1), :
        ]
    for start in range(0, n, size):
        end = start + size
        corner = corner_inverse(work_ref[start:end, start:end])
        if start:
            inverse_ref[start:end, :start] = dot_exact(
                corner, inverse_ref[start:end, :start], ((1,), (0,))
            )
        inverse_ref[start:end, start:end] = corner
        if end < n:
            low = dot_exact(work_ref[end:, start:end], corner, ((1,), (1,)))
            work_ref[end:, end:] -= dot_exact(low, low, ((1,), (1,)))
            if start:
                inverse_ref[end:, :start] -= dot_exact(
                    low, inverse_ref[start:end, :start], ((1,), (0,))
                )
            inverse_ref[end:, start:end] = -dot_exact(low, corner, ((1,), (0,)))
    for start in range(0, n, size):
        end = start + size
        q = dot_exact(inverse_ref[start:end, :end], rows_ref[:end, :], ((1,), (0,)))
        half_ref[start:end, :] = q.astype(jnp.bfloat16)
        basis_ref[:, start:end] = q.T.astype(jnp.bfloat16)


def factor_and_q(gram, rows):
    width, size = rows.shape
    return pl.pallas_call(
        factor_kernel,
        out_shape=(
            jax.ShapeDtypeStruct((size, width), jnp.bfloat16),
            jax.ShapeDtypeStruct((width, size), jnp.bfloat16),
        ),
        in_specs=[vmem(), vmem()],
        out_specs=(vmem(), vmem()),
        scratch_shapes=[pltpu.VMEM((width, width), jnp.float32)] * 2,
        compiler_params=pltpu.CompilerParams(vmem_limit_bytes=24 * 2**20),
        name="factor",
    )(gram, rows)


class Ring:
    ARRIVALS = 15
    RING = (0, 1, 3, 4, 5, 7, 8, 11)
    CROSS = (1, 5, 9)

    def __init__(self, lead, all_ref, got_sems, ring_sems, pair_sems, cross_sems):
        self.lead = lead
        self.all_ref, self.got_sems = all_ref, got_sems
        self.ring_sems, self.pair_sems, self.cross_sems = ring_sems, pair_sems, cross_sems
        at = lax.axis_index("cols")
        self.length = lax.axis_size("cols") // 4
        assert self.length == 8
        self.z, quad = at // 4, lax.rem(at, 4)
        self.y, self.core = quad // 2, lax.rem(quad, 2)
        self.way = 1 - 2 * self.core
        self.own = at
        self.pair = self.device(0, 0, 1)
        self.across = self.device(0, 1, 0)
        self.after = self.device(-1, 0, 0)
        self.before = self.device(1, 0, 0)
        self.diagonal = self.device(0, 1, 1)

    def device(self, away, row, core, mirror=False):
        way = -self.way if mirror else self.way
        z = lax.rem(self.z - way * away + self.length, self.length)
        y = lax.rem(self.y + row, 2)
        core = lax.rem(self.core + core + (1 if mirror else 0), 2)
        return z * 4 + y * 2 + core

    def place(self, n):
        return n + n // 13

    def slot(self, m, mirror=False):
        turn = lax.rem(m, 4)
        away = m // 4 + 1 - (turn // 2 - turn // 3)
        return self.device(away, turn // 2, lax.rem((turn + 1) // 2, 2), mirror)

    def greet(self, *groups):
        greet(*groups, near=(self.pair, self.across, self.after, self.before))

    def copy(self, slot, send, peer):
        part = self.all_ref.at[slot]
        return put_copy(part, part, send, self.got_sems.at[slot], "cols", peer)

    def arrived(self, slot):
        self.copy(slot, self.cross_sems.at[0], self.pair).wait_recv()

    def to_ring(self, slot, at):
        self.copy(slot, self.ring_sems.at[at], self.after).start()

    def to_pair(self, slot, at):
        self.copy(slot, self.pair_sems.at[at], self.pair).start()

    def to_across(self, slot, at):
        self.copy(slot, self.cross_sems.at[at], self.across).start()

    def hand_on(self, n):
        m = self.place(n)
        slot = self.slot(m)
        self.arrived(slot)
        turn, step = lax.rem(m, 4), m // 4 + 1

        @pl.when(((turn == 1) & (step < 3)) | ((turn != 1) & (turn != 2) & (step < 4)))
        def _():
            self.to_ring(slot, m + 3)

        @pl.when(turn == 1)
        def _():
            self.to_across(slot, m)

        @pl.when(m != 2)
        def _():
            self.to_pair(slot, n + 1)

    def begin(self, *between):
        first, second, third = between or [lambda: None] * 3
        self.to_pair(self.own, 0)
        self.to_ring(self.own, 0)
        self.to_across(self.own, 0)
        first()
        self.arrived(self.pair)
        self.to_ring(self.pair, 1)
        second()
        self.arrived(self.across)
        self.to_ring(self.across, 2)
        self.to_pair(self.across, 3)
        self.hand_on(0)
        third()

        def early(n, carry):
            self.hand_on(n)
            return carry

        lax.fori_loop(1, self.lead, early, 0)

    def run(self, work, also):
        work([self.own, self.pair])
        last = self.ARRIVALS - 1

        def one(n, carry):
            for at, act in also.items():
                pl.when(n == at)(act)

            @pl.when(n + self.lead <= last)
            def _():
                self.hand_on(n + self.lead)

            m = self.place(n)
            mirrored = self.slot(m, mirror=True)

            @pl.when(m != 2)
            def _():
                self.arrived(mirrored)

            work([self.slot(m), mirrored])
            return carry

        lax.fori_loop(0, self.ARRIVALS, one, 0)
        for at in [0, 1, 2, *(m + 3 for m in self.RING)]:
            self.copy(self.own, self.ring_sems.at[at], self.after).wait_send()
        for at in [0, *self.CROSS]:
            self.copy(self.own, self.cross_sems.at[at], self.across).wait_send()

        def sent(at, carry):
            self.copy(self.own, self.pair_sems.at[at], self.pair).wait_send()
            return carry

        lax.fori_loop(0, self.ARRIVALS + 1, sent, 0)


def ring_scratch(table):
    dma = pltpu.SemaphoreType.DMA
    ncols = lax.axis_size("cols")
    return [
        pltpu.VMEM((ncols, *table), jnp.bfloat16),
        dma((ncols,)),
        dma((Ring.RING[-1] + 4,)),
        dma((Ring.ARRIVALS + 1,)),
        dma((Ring.CROSS[-1] + 1,)),
    ]


def block_sums(all_ref, records_ref, slots, places, block, width, by_prefix):
    shift = block.bit_length() - 1
    rows = range(records_ref.shape[0])
    placed, spots = [], []
    for slot, place in zip(slots, places):
        packed = [records_ref[d, place, 0:1, :].astype(jnp.int32) for d in rows]
        weight = [records_ref[d, place, 1:2, :] for d in rows]
        prefix = [lax.shift_right_logical(ids, shift) for ids in packed]
        suffix = [ids & (block - 1) for ids in packed]
        take, put = (prefix, suffix) if by_prefix else (suffix, prefix)
        one, spot = weighted_rows(all_ref[slot], take, put, weight, width)
        placed.append(one)
        spots.append(spot)
    return lax.dot_general(
        jnp.concatenate(placed, axis=1),
        jnp.concatenate(spots, axis=1),
        (((1,), (1,)), ((), ())),
        preferred_element_type=jnp.float32,
    )


def sketch_kernel(block, width, own_ref, part_ref, mine_ref, rows_ref, gram_ref, totals_ref, *scratch):
    here_ref, total_ref, col_sems, here_sems, mine_sems, *scratch = scratch
    ring = Ring(2, *scratch[:5])
    data_at, col_at = lax.axis_index("dp"), lax.axis_index("cols")
    greet(("cols", 1), ("dp", 1))

    ncols = lax.axis_size("cols")
    near = 12

    def place_at(slot, device):
        return lax.rem(slot - device // 4 * 4 + 4 + ncols, ncols)

    own_place = place_at(col_at, col_at)

    def peer_at(place):
        return lax.rem(col_at // 4 * 4 - 4 + place + ncols, ncols)

    def to_col(place):
        peer = peer_at(place)
        there = place_at(col_at, peer)
        return put_copy(
            own_ref.at[peer],
            here_ref.at[data_at, there],
            col_sems.at[0, place],
            col_sems.at[1, there],
            "cols",
            peer,
        )

    def from_col(place):
        return put_copy(
            own_ref.at[peer_at(place)],
            here_ref.at[data_at, place],
            col_sems.at[0, place],
            col_sems.at[1, place],
            "cols",
            peer_at(place),
        )

    def others(start, end, act):
        def one(place, carry):
            pl.when(place != own_place)(lambda: act(place))
            return carry

        lax.fori_loop(start, end, one, 0)

    def mine_to_data(offset, peer):
        return put_copy(
            own_ref,
            mine_ref.at[data_at],
            mine_sems.at[0, offset],
            mine_sems.at[1, offset],
            "dp",
            peer,
        )

    def here_to_data(group):
        places = pl.ds(0, near) if group == 0 else pl.ds(near, ncols - near)

        def make(offset, peer):
            return put_copy(
                here_ref.at[data_at, places],
                here_ref.at[data_at, places],
                here_sems.at[0, group, offset],
                here_sems.at[1, group, offset],
                "dp",
                peer,
            )

        return make

    def begin_data(group):
        over_peers("dp", lambda offset, peer: here_to_data(group)(offset, peer).start())

    def end_data(group):
        over_peers("dp", lambda offset, peer: here_to_data(group)(offset, peer).wait())

    def first():
        others(0, ncols, lambda place: to_col(place).start())
        here_ref[data_at, own_place] = own_ref[col_at]

    def second():
        others(0, near, lambda place: from_col(place).wait())
        begin_data(0)
        mine_ref[data_at] = own_ref[...]

    def third():
        others(near, ncols, lambda place: from_col(place).wait())
        begin_data(1)

    all_ref = scratch[0]
    all_ref[ring.own] = part_ref[...]
    ring.begin(first, second, third)
    total_ref[...] = jnp.zeros_like(total_ref)
    end_data(0)

    def work(slots):
        places = [place_at(slot, col_at) for slot in slots]
        total_ref[...] += block_sums(all_ref, here_ref, slots, places, block, width, False)

    def begin_mine():
        over_peers("dp", lambda offset, peer: mine_to_data(offset, peer).start())

    ring.run(work, {0: begin_mine, 4: lambda: end_data(1)})
    over_peers("dp", lambda offset, peer: mine_to_data(offset, peer).wait())
    gram_steps(total_ref, mine_ref, rows_ref, gram_ref, totals_ref, *scratch[5:])


def sketch_and_gram(own, part, block, width):
    ndata, ncols = lax.axis_size("dp"), lax.axis_size("cols")
    whole, size = part.shape
    chips = ncols // 2
    lanes = own.shape[-1]
    f32 = jnp.float32
    packed = len(lower_blocks(whole, lanes)) * lanes
    half = packed // 2
    share = half // ndata
    tile = (8, lanes)
    assert share % 8 == 0 and share % chips == 0 and share // chips <= 8
    dma = pltpu.SemaphoreType.DMA
    return pl.pallas_call(
        functools.partial(sketch_kernel, block, width),
        out_shape=(
            jax.ShapeDtypeStruct((ndata, *own.shape), f32),
            jax.ShapeDtypeStruct((ndata, width, size), f32),
            jax.ShapeDtypeStruct((packed, lanes), f32),
            jax.ShapeDtypeStruct((2, *tile), f32),
        ),
        in_specs=[vmem(), vmem()],
        out_specs=(vmem(), vmem(), vmem(), vmem()),
        scratch_shapes=[
            pltpu.VMEM((ndata, *own.shape), f32),
            pltpu.VMEM((whole, size), f32),
            dma((2, ncols)),
            dma((2, 2, ndata)),
            dma((2, ndata)),
            *ring_scratch(part.shape),
            pltpu.VMEM((packed, lanes), f32),
            pltpu.VMEM((half, lanes), f32),
            pltpu.VMEM((half, lanes), f32),
            pltpu.VMEM((ndata, share, lanes), f32),
            pltpu.VMEM((chips, *tile), f32),
            pltpu.VMEM((chips, *tile), f32),
            pltpu.VMEM((chips, 3, *tile), f32),
            pltpu.VMEM((share, lanes), f32),
            pltpu.VMEM((2, 2, *tile), f32),
            dma((2, ndata)),
            dma((2, 3)),
            dma((2, ndata)),
            dma((2, chips)),
            dma((2, chips)),
            dma((2, ndata)),
        ],
        compiler_params=pltpu.CompilerParams(
            collective_id=0, has_side_effects=True, vmem_limit_bytes=40 * 2**20
        ),
        name="sketch",
    )(own, part)


def project_kernel(
    scale,
    block,
    width,
    half_ref,
    basis_ref,
    mine_ref,
    totals_ref,
    coef_ref,
    whole_ref,
    total_ref,
    half_sems,
    basis_sems,
    own_sem,
    all_ref,
    *sems,
):
    ring = Ring(1, all_ref, *sems)
    ring.greet(("dp", 1))
    data_at, col_at = lax.axis_index("dp"), lax.axis_index("cols")
    size = basis_ref.shape[0]
    ndata = whole_ref.shape[0] // size
    own_rows = pl.ds(pl.multiple_of(data_at * width, width), width)

    def half_copy(offset, peer):
        return put_copy(
            half_ref.at[pl.ds(pl.multiple_of(peer * width, width), width), :],
            all_ref.at[col_at, own_rows, :],
            half_sems.at[0, offset],
            half_sems.at[1, offset],
            "dp",
            peer,
        )

    along = ndata // 2
    other = lax.rem(data_at + along, ndata)

    def basis_rows(owner):
        return whole_ref.at[pl.ds(pl.multiple_of(owner * size, size), size), :]

    def basis_copy(offset, rows, source, peer):
        return put_copy(
            source, rows, basis_sems.at[0, offset], basis_sems.at[1, offset], "dp", peer
        )

    def x_copy(offset, owner, source):
        peer = data_at // along * along + lax.rem(data_at + offset, along)
        at = offset if source is basis_ref else along + offset
        return basis_copy(at, basis_rows(owner), source, peer)

    def own_x_copy(offset):
        return x_copy(offset, data_at, basis_ref)

    def other_x_copy(offset):
        return x_copy(offset, other, basis_rows(other))

    own_copy = pltpu.make_async_copy(basis_ref, basis_rows(data_at), own_sem)
    other_copy = basis_copy(0, basis_rows(data_at), basis_ref, other)

    def begun():
        other_copy.start()
        for offset in range(1, along):
            own_x_copy(offset).start()
        own_copy.start()

    def later():
        other_copy.wait_recv()
        for offset in range(1, along):
            other_x_copy(offset).start()

    def work(slots):
        total_ref[...] += block_sums(all_ref, mine_ref, slots, slots, block, width, True)

    over_peers("dp", lambda offset, peer: half_copy(offset, peer).start())
    all_ref[col_at, own_rows, :] = half_ref[own_rows, :]
    total_ref[...] = jnp.zeros_like(total_ref)
    over_peers("dp", lambda offset, peer: half_copy(offset, peer).wait())
    ring.begin()
    ring.run(work, {0: begun, 6: later})
    factor = scale * jnp.sum(totals_ref[1]) / jnp.sum(totals_ref[0])
    for g in range(total_ref.shape[0] // width):
        coef_ref[:, g * size : (g + 1) * size] = factor * total_ref[g * width : (g + 1) * width, :]
    other_copy.wait_send()
    for offset in range(1, along):
        own_x_copy(offset).wait()
        other_x_copy(offset).wait()
    own_copy.wait()


def project(half, basis_part, mine, totals, scale, block, width):
    ndata = lax.axis_size("dp")
    size, whole = basis_part.shape
    dma = pltpu.SemaphoreType.DMA
    anywhere = pl.BlockSpec(memory_space=pl.ANY)
    return pl.pallas_call(
        functools.partial(project_kernel, scale, block, width),
        out_shape=(
            jax.ShapeDtypeStruct((width, block), jnp.float32),
            jax.ShapeDtypeStruct((size * ndata, whole), jnp.bfloat16),
        ),
        in_specs=[vmem(), anywhere, vmem(), vmem()],
        out_specs=(vmem(), anywhere),
        scratch_shapes=[
            pltpu.VMEM(half.shape, jnp.float32),
            dma((2, ndata)),
            dma((2, ndata)),
            dma,
            *ring_scratch(half.shape),
        ],
        compiler_params=pltpu.CompilerParams(
            collective_id=1, has_side_effects=True, vmem_limit_bytes=40 * 2**20
        ),
        name="project",
    )(half, basis_part, mine, totals)


def shards(prefix_ids, suffix_ids, weights, counts, omega):
    ncols = lax.axis_size("cols")
    ndata = lax.axis_size("dp")
    block, width = omega.shape
    slots = prefix_ids.shape[-1]
    chunk = width // ndata
    size = block // ndata
    data_at = lax.axis_index("dp")

    live = lax.broadcasted_iota(jnp.int32, (ncols, slots), 1) < counts.reshape(ncols, 1)
    live_weights = jnp.where(live, weights.reshape(ncols, slots), 0.0)
    prefix_local = prefix_ids.reshape(ncols, slots) & (block - 1)
    suffix_local = suffix_ids.reshape(ncols, slots) & (block - 1)
    packed = prefix_local * block + suffix_local
    own = jnp.stack([packed.astype(jnp.float32), live_weights], axis=1)
    part = lax.dynamic_slice_in_dim(omega, data_at * chunk, chunk, 1)
    part = part.reshape(ndata, size, chunk).swapaxes(1, 2).reshape(ndata * chunk, size)
    mine, rows, gram, totals = sketch_and_gram(own, part, block, chunk)
    basis_part, q_half = factor_and_q(gram, rows.reshape(width, size))
    scale = math.sqrt(block * ncols)
    coefficients, q_block = project(q_half, basis_part, mine, totals, scale, block, chunk)
    basis = scale * q_block.astype(jnp.float32)
    return (basis, coefficients)


def solution(mesh):
    placed = (
        P("dp", "cols", None, None),
        P("dp", "cols", None, None),
        P("dp", "cols", None, None),
        P("dp", "cols", None),
        P("cols", None),
    )
    return jax.shard_map(
        shards,
        mesh=mesh,
        in_specs=placed,
        out_specs=(P("cols", None), P("dp", "cols")),
        check_vma=False,
    )
```

```python
import functools
import math

import jax
import jax.numpy as jnp
from jax import lax
from jax.experimental import pallas as pl
from jax.experimental.pallas import tpu as pltpu
from jax.sharding import PartitionSpec as P

HIGHEST = lax.Precision.HIGHEST


def dot_exact(a, b, dims):
    return lax.dot_general(
        a, b, (dims, ((), ())), precision=HIGHEST, preferred_element_type=jnp.float32
    )


def one_hot(ids, size):
    rows = lax.broadcasted_iota(jnp.int32, (size, ids.shape[1]), 0)
    return jnp.where(rows == ids, 1.0, 0.0).astype(jnp.bfloat16)


def weighted_rows(table, take, put, weight, width):
    size = table.shape[1]
    groups = table.shape[0] // width
    shift = size.bit_length() - 1
    beside = functools.partial(jnp.concatenate, axis=1)
    picked = jnp.dot(
        table,
        beside([one_hot(ids & (size - 1), size) for ids in take]),
        preferred_element_type=jnp.float32,
    )
    take_group = beside([lax.shift_right_logical(ids, shift) for ids in take])
    put_group = beside([lax.shift_right_logical(ids, shift) for ids in put])
    row = picked[:width]
    for g in range(1, groups):
        row = jnp.where(take_group == g, picked[g * width : (g + 1) * width], row)
    row = beside(weight) * row
    placed = jnp.concatenate(
        [jnp.where(put_group == g, row, 0.0).astype(jnp.bfloat16) for g in range(groups)], axis=0
    )
    return placed, beside([one_hot(ids & (size - 1), size) for ids in put])


def vmem():
    return pl.BlockSpec(memory_space=pltpu.VMEM)


def put_copy(src, dst, send, recv, axis, peer):
    return pltpu.make_async_remote_copy(
        src_ref=src,
        dst_ref=dst,
        send_sem=send,
        recv_sem=recv,
        device_id={axis: peer},
        device_id_type=pl.DeviceIdType.MESH,
    )


def over_peers(axis, act, stride=1):
    count = lax.axis_size(axis)
    me = lax.axis_index(axis)

    def one(offset, carry):
        act(offset, lax.rem(me + stride * offset, count))
        return carry

    lax.fori_loop(1, count // stride, one, 0)


def signal(barrier, axis, peer):
    pl.semaphore_signal(
        barrier, inc=1, device_id={axis: peer}, device_id_type=pl.DeviceIdType.MESH
    )


def greet(*groups, near=()):
    barrier = pltpu.get_barrier_semaphore()
    for peer in near:
        signal(barrier, "cols", peer)
    for axis, stride in groups:
        over_peers(axis, lambda offset, peer, axis=axis: signal(barrier, axis, peer), stride)
    count = sum(lax.axis_size(axis) // stride - 1 for axis, stride in groups)
    return lambda: pl.semaphore_wait(barrier, count + len(near))


def lower_blocks(width, lanes):
    return [(i, j) for i in range(width // lanes) for j in range(i + 1)]


def rows_at(start, count):
    return pl.ds(pl.multiple_of(start, 8), count)


def gram_steps(
    total_ref,
    mine_ref,
    rows_ref,
    gram_ref,
    totals_ref,
    part_ref,
    half_ref,
    other_ref,
    got_ref,
    piece_ref,
    arrived_ref,
    shared_ref,
    own_ref,
    sum_ref,
    rows_sems,
    pair_sems,
    part_sems,
    piece_sems,
    shared_sems,
    gram_sems,
):
    data_at, col_at = lax.axis_index("dp"), lax.axis_index("cols")
    core, chip = lax.rem(col_at, 2), col_at // 2
    pair = col_at + 1 - 2 * core
    ndata, chunk, size = rows_ref.shape
    width = ndata * chunk
    lanes = part_ref.shape[1]
    half = half_ref.shape[0]
    share = half // ndata
    chips = piece_ref.shape[0]
    few = share // chips

    def rows_copy(offset, peer):
        return put_copy(
            total_ref.at[rows_at(peer * chunk, chunk), :],
            rows_ref.at[data_at],
            rows_sems.at[0, offset],
            rows_sems.at[1, offset],
            "dp",
            peer,
        )

    over_peers("dp", lambda offset, peer: rows_copy(offset, peer).start())
    rows_ref[data_at] = total_ref[rows_at(data_at * chunk, chunk), :]
    weight = mine_ref[:, :, 1, :]
    for at, term in ((0, weight), (1, (weight > 0.0).astype(jnp.float32))):
        term = jnp.sum(term, axis=0).reshape(-1, *totals_ref.shape[1:])
        sum_ref[0, at] = jnp.sum(term, axis=0)
    sums_copy = put_copy(
        sum_ref.at[0], sum_ref.at[1], pair_sems.at[0, 0], pair_sems.at[1, 0], "cols", pair
    )
    sums_copy.start()
    piece_ref[...] = jnp.zeros_like(piece_ref)
    over_peers("dp", lambda offset, peer: rows_copy(offset, peer).wait())
    rows = rows_ref[...].reshape(width, size)
    gram = dot_exact(rows, rows, ((1,), (1,)))
    for at, (i, j) in enumerate(lower_blocks(width, lanes)):
        part_ref[lanes * at : lanes * (at + 1), :] = gram[
            lanes * i : lanes * (i + 1), lanes * j : lanes * (j + 1)
        ]

    pair_copy = put_copy(
        part_ref.at[rows_at((1 - core) * half, half), :],
        other_ref,
        pair_sems.at[0, 1],
        pair_sems.at[1, 1],
        "cols",
        pair,
    )
    pair_copy.start()
    sums_copy.wait()
    shared_ref[chip, 1] = sum_ref[0, 0] + sum_ref[1, 0]
    shared_ref[chip, 2] = sum_ref[0, 1] + sum_ref[1, 1]
    pair_copy.wait()
    half_ref[...] = part_ref[rows_at(core * half, half), :] + other_ref[...]

    def part_copy(offset, peer):
        return put_copy(
            half_ref.at[rows_at(peer * share, share), :],
            got_ref.at[data_at],
            part_sems.at[0, offset],
            part_sems.at[1, offset],
            "dp",
            peer,
        )

    over_peers("dp", lambda offset, peer: part_copy(offset, peer).start())
    got_ref[data_at] = half_ref[rows_at(data_at * share, share), :]
    over_peers("dp", lambda offset, peer: part_copy(offset, peer).wait())
    summed = jnp.sum(got_ref[...], axis=0)
    for at in range(chips):
        piece_ref[at, :few] = summed[few * at : few * (at + 1)]

    def piece_copy(offset, peer):
        return put_copy(
            piece_ref.at[peer // 2],
            arrived_ref.at[chip],
            piece_sems.at[0, offset],
            piece_sems.at[1, offset],
            "cols",
            peer,
        )

    over_peers("cols", lambda offset, peer: piece_copy(offset, peer).start(), 2)
    arrived_ref[chip] = piece_ref[chip]
    over_peers("cols", lambda offset, peer: piece_copy(offset, peer).wait(), 2)
    shared_ref[chip, 0] = jnp.sum(arrived_ref[...], axis=0)

    def shared_copy(offset, peer):
        return put_copy(
            shared_ref.at[chip],
            shared_ref.at[chip],
            shared_sems.at[0, offset],
            shared_sems.at[1, offset],
            "cols",
            peer,
        )

    over_peers("cols", lambda offset, peer: shared_copy(offset, peer).start(), 2)
    over_peers("cols", lambda offset, peer: shared_copy(offset, peer).wait(), 2)
    for at in range(chips):
        own_ref[few * at : few * (at + 1), :] = shared_ref[at, 0, :few, :]
    own_rows = rows_at((core * ndata + data_at) * share, share)

    def gram_copy(offset, peer):
        return put_copy(
            own_ref,
            gram_ref.at[own_rows, :],
            gram_sems.at[0, offset],
            gram_sems.at[1, offset],
            "dp",
            peer,
        )

    over_peers("dp", lambda offset, peer: gram_copy(offset, peer).start())
    gram_ref[own_rows, :] = own_ref[...]
    totals_ref[0] = jnp.sum(shared_ref[:, 1], axis=0)
    totals_ref[1] = jnp.sum(shared_ref[:, 2], axis=0)
    over_peers("dp", lambda offset, peer: gram_copy(offset, peer).wait())
    own_half = gram_ref.at[rows_at(core * half, half), :]
    last_copy = put_copy(
        own_half, own_half, pair_sems.at[0, 2], pair_sems.at[1, 2], "cols", pair
    )
    last_copy.start()
    last_copy.wait()


def corner_inverse(tile, pivots=8):
    n = tile.shape[0]
    blocks = n // pivots

    def full(x):
        return jnp.broadcast_to(x, (pivots, n))

    work = [tile[pivots * i : pivots * (i + 1), :] for i in range(blocks)]
    lane = lax.broadcasted_iota(jnp.int32, (pivots, n), 1)
    sub = lax.broadcasted_iota(jnp.int32, (pivots, n), 0)
    done = []
    for at in range(blocks):
        start = at * pivots
        group = (lane >= start) & (lane < start + pivots)
        cols = [full(work[at][:, start + c : start + c + 1]) for c in range(pivots)]
        left = [[full(cols[c][r : r + 1, :]) for c in range(r + 1)] for r in range(pivots)]
        rows = [
            jnp.where(group, jnp.where(lane == start + r, 1.0, 0.0), full(work[at][r : r + 1, :]))
            for r in range(pivots)
        ]
        recip = [None] * pivots
        low = [[None] * pivots for _ in range(pivots)]
        for c in range(pivots):
            recip[c] = 1.0 / left[c][c]
            for r in range(c + 1, pivots):
                low[r][c] = left[r][c] * recip[c]
                for e in range(c + 1, r + 1):
                    left[r][e] = left[r][e] - low[r][c] * left[e][c]
        for r in range(pivots):
            for c in range(r):
                rows[r] = rows[r] - low[r][c] * rows[c]
        result = jnp.zeros((pivots, n), jnp.float32)
        for r in range(pivots):
            result = jnp.where(sub == r, rows[r] * lax.rsqrt(left[r][r]), result)
        done.append(jnp.where(lane <= sub + start, result, 0.0))
        back = [rows[r] * recip[r] for r in range(pivots)]
        for r in range(pivots - 1, -1, -1):
            for c in range(r):
                back[c] = back[c] - low[r][c] * back[r]
        for i in range(at + 1, blocks):
            rest = jnp.where(group, 0.0, work[i])
            for c in range(pivots):
                rest = rest - full(work[i][:, start + c : start + c + 1]) * back[c]
            work[i] = rest
    return jnp.concatenate(done, axis=0)


def factor_steps(gram_ref, rows_ref, work_ref, inverse_ref, ready):
    n = work_ref.shape[0]
    size = gram_ref.shape[1]
    for at, (i, j) in enumerate(lower_blocks(n, size)):
        work_ref[size * i : size * (i + 1), size * j : size * (j + 1)] = gram_ref[
            size * at : size * (at + 1), :
        ]
    for start in range(0, n, size):
        end = start + size
        corner = corner_inverse(work_ref[start:end, start:end])
        if start:
            inverse_ref[start:end, :start] = dot_exact(
                corner, inverse_ref[start:end, :start], ((1,), (0,))
            )
        inverse_ref[start:end, start:end] = corner
        if end < n:
            low = dot_exact(work_ref[end:, start:end], corner, ((1,), (1,)))
            work_ref[end:, end:] -= dot_exact(low, low, ((1,), (1,)))
            if start:
                inverse_ref[end:, :start] -= dot_exact(
                    low, inverse_ref[start:end, :start], ((1,), (0,))
                )
            inverse_ref[end:, start:end] = -dot_exact(low, corner, ((1,), (0,)))
        ready(start, end, dot_exact(inverse_ref[start:end, :end], rows_ref[:end, :], ((1,), (0,))))


class Ring:
    ARRIVALS = 15
    RING = (0, 1, 3, 4, 5, 7, 8, 11)
    CROSS = (1, 5, 9)

    def __init__(self, lead, all_ref, got_sems, ring_sems, pair_sems, cross_sems):
        self.lead = lead
        self.all_ref, self.got_sems = all_ref, got_sems
        self.ring_sems, self.pair_sems, self.cross_sems = ring_sems, pair_sems, cross_sems
        at = lax.axis_index("cols")
        self.length = lax.axis_size("cols") // 4
        assert self.length == 8
        self.z, quad = at // 4, lax.rem(at, 4)
        self.y, self.core = quad // 2, lax.rem(quad, 2)
        self.way = 1 - 2 * self.core
        self.own = at
        self.pair = self.device(0, 0, 1)
        self.across = self.device(0, 1, 0)
        self.after = self.device(-1, 0, 0)
        self.before = self.device(1, 0, 0)
        self.diagonal = self.device(0, 1, 1)

    def device(self, away, row, core, mirror=False):
        way = -self.way if mirror else self.way
        z = lax.rem(self.z - way * away + self.length, self.length)
        y = lax.rem(self.y + row, 2)
        core = lax.rem(self.core + core + (1 if mirror else 0), 2)
        return z * 4 + y * 2 + core

    def place(self, n):
        return n + n // 13

    def slot(self, m, mirror=False):
        turn = lax.rem(m, 4)
        away = m // 4 + 1 - (turn // 2 - turn // 3)
        return self.device(away, turn // 2, lax.rem((turn + 1) // 2, 2), mirror)

    def greet(self, *groups):
        return greet(*groups, near=(self.pair, self.across, self.after, self.before))

    def copy(self, slot, send, peer):
        part = self.all_ref.at[slot]
        return put_copy(part, part, send, self.got_sems.at[slot], "cols", peer)

    def arrived(self, slot):
        self.copy(slot, self.cross_sems.at[0], self.pair).wait_recv()

    def to_ring(self, slot, at):
        self.copy(slot, self.ring_sems.at[at], self.after).start()

    def to_pair(self, slot, at):
        self.copy(slot, self.pair_sems.at[at], self.pair).start()

    def to_across(self, slot, at):
        self.copy(slot, self.cross_sems.at[at], self.across).start()

    def hand_on(self, n):
        m = self.place(n)
        slot = self.slot(m)
        self.arrived(slot)
        turn, step = lax.rem(m, 4), m // 4 + 1

        @pl.when(((turn == 1) & (step < 3)) | ((turn != 1) & (turn != 2) & (step < 4)))
        def _():
            self.to_ring(slot, m + 3)

        @pl.when(turn == 1)
        def _():
            self.to_across(slot, m)

        @pl.when(m != 2)
        def _():
            self.to_pair(slot, n + 1)

    def begin(self, *between):
        first, second, third = between or [lambda: None] * 3
        self.to_pair(self.own, 0)
        self.to_ring(self.own, 0)
        self.to_across(self.own, 0)
        first()
        self.arrived(self.pair)
        self.to_ring(self.pair, 1)
        second()
        self.arrived(self.across)
        self.to_ring(self.across, 2)
        self.to_pair(self.across, 3)
        self.hand_on(0)
        third()

        def early(n, carry):
            self.hand_on(n)
            return carry

        lax.fori_loop(1, self.lead, early, 0)

    def run(self, work, also):
        work([self.own, self.pair])
        last = self.ARRIVALS - 1

        def one(n, carry):
            for at, act in also.items():
                pl.when(n == at)(act)

            @pl.when(n + self.lead <= last)
            def _():
                self.hand_on(n + self.lead)

            m = self.place(n)
            mirrored = self.slot(m, mirror=True)

            @pl.when(m != 2)
            def _():
                self.arrived(mirrored)

            work([self.slot(m), mirrored])
            return carry

        lax.fori_loop(0, self.ARRIVALS, one, 0)
        for at in [0, 1, 2, *(m + 3 for m in self.RING)]:
            self.copy(self.own, self.ring_sems.at[at], self.after).wait_send()
        for at in [0, *self.CROSS]:
            self.copy(self.own, self.cross_sems.at[at], self.across).wait_send()

        def sent(at, carry):
            self.copy(self.own, self.pair_sems.at[at], self.pair).wait_send()
            return carry

        lax.fori_loop(0, self.ARRIVALS + 1, sent, 0)


def ring_scratch(table):
    dma = pltpu.SemaphoreType.DMA
    ncols = lax.axis_size("cols")
    return [
        pltpu.VMEM((ncols, *table), jnp.bfloat16),
        dma((ncols,)),
        dma((Ring.RING[-1] + 4,)),
        dma((Ring.ARRIVALS + 1,)),
        dma((Ring.CROSS[-1] + 1,)),
    ]


def block_sums(all_ref, records_ref, slots, places, block, width, by_prefix):
    shift = block.bit_length() - 1
    rows = range(records_ref.shape[0])
    placed, spots = [], []
    for slot, place in zip(slots, places):
        packed = [records_ref[d, place, 0:1, :].astype(jnp.int32) for d in rows]
        weight = [records_ref[d, place, 1:2, :] for d in rows]
        prefix = [lax.shift_right_logical(ids, shift) for ids in packed]
        suffix = [ids & (block - 1) for ids in packed]
        take, put = (prefix, suffix) if by_prefix else (suffix, prefix)
        one, spot = weighted_rows(all_ref[slot], take, put, weight, width)
        placed.append(one)
        spots.append(spot)
    return lax.dot_general(
        jnp.concatenate(placed, axis=1),
        jnp.concatenate(spots, axis=1),
        (((1,), (1,)), ((), ())),
        preferred_element_type=jnp.float32,
    )


def sketch_kernel(block, width, own_ref, part_ref, mine_ref, rows_ref, gram_ref, totals_ref, *scratch):
    here_ref, total_ref, col_sems, here_sems, mine_sems, *scratch = scratch
    ring = Ring(2, *scratch[:5])
    data_at, col_at = lax.axis_index("dp"), lax.axis_index("cols")
    greet(("cols", 1), ("dp", 1))()

    ncols = lax.axis_size("cols")
    near = 12

    def place_at(slot, device):
        return lax.rem(slot - device // 4 * 4 + 4 + ncols, ncols)

    own_place = place_at(col_at, col_at)

    def peer_at(place):
        return lax.rem(col_at // 4 * 4 - 4 + place + ncols, ncols)

    def to_col(place):
        peer = peer_at(place)
        there = place_at(col_at, peer)
        return put_copy(
            own_ref.at[peer],
            here_ref.at[data_at, there],
            col_sems.at[0, place],
            col_sems.at[1, there],
            "cols",
            peer,
        )

    def from_col(place):
        return put_copy(
            own_ref.at[peer_at(place)],
            here_ref.at[data_at, place],
            col_sems.at[0, place],
            col_sems.at[1, place],
            "cols",
            peer_at(place),
        )

    def others(start, end, act):
        def one(place, carry):
            pl.when(place != own_place)(lambda: act(place))
            return carry

        lax.fori_loop(start, end, one, 0)

    def mine_to_data(offset, peer):
        return put_copy(
            own_ref,
            mine_ref.at[data_at],
            mine_sems.at[0, offset],
            mine_sems.at[1, offset],
            "dp",
            peer,
        )

    def here_to_data(group):
        places = pl.ds(0, near) if group == 0 else pl.ds(near, ncols - near)

        def make(offset, peer):
            return put_copy(
                here_ref.at[data_at, places],
                here_ref.at[data_at, places],
                here_sems.at[0, group, offset],
                here_sems.at[1, group, offset],
                "dp",
                peer,
            )

        return make

    def begin_data(group):
        over_peers("dp", lambda offset, peer: here_to_data(group)(offset, peer).start())

    def end_data(group):
        over_peers("dp", lambda offset, peer: here_to_data(group)(offset, peer).wait())

    def first():
        others(0, ncols, lambda place: to_col(place).start())
        here_ref[data_at, own_place] = own_ref[col_at]

    def second():
        others(0, near, lambda place: from_col(place).wait())
        begin_data(0)
        mine_ref[data_at] = own_ref[...]

    def third():
        others(near, ncols, lambda place: from_col(place).wait())
        begin_data(1)

    all_ref = scratch[0]
    all_ref[ring.own] = part_ref[...]
    ring.begin(first, second, third)
    total_ref[...] = jnp.zeros_like(total_ref)
    end_data(0)

    def work(slots):
        places = [place_at(slot, col_at) for slot in slots]
        total_ref[...] += block_sums(all_ref, here_ref, slots, places, block, width, False)

    def begin_mine():
        over_peers("dp", lambda offset, peer: mine_to_data(offset, peer).start())

    ring.run(work, {0: begin_mine, 4: lambda: end_data(1)})
    over_peers("dp", lambda offset, peer: mine_to_data(offset, peer).wait())
    gram_steps(total_ref, mine_ref, rows_ref, gram_ref, totals_ref, *scratch[5:])


def sketch_and_gram(own, part, block, width):
    ndata, ncols = lax.axis_size("dp"), lax.axis_size("cols")
    whole, size = part.shape
    chips = ncols // 2
    lanes = own.shape[-1]
    f32 = jnp.float32
    packed = len(lower_blocks(whole, lanes)) * lanes
    half = packed // 2
    share = half // ndata
    tile = (8, lanes)
    assert share % 8 == 0 and share % chips == 0 and share // chips <= 8
    dma = pltpu.SemaphoreType.DMA
    return pl.pallas_call(
        functools.partial(sketch_kernel, block, width),
        out_shape=(
            jax.ShapeDtypeStruct((ndata, *own.shape), f32),
            jax.ShapeDtypeStruct((ndata, width, size), f32),
            jax.ShapeDtypeStruct((packed, lanes), f32),
            jax.ShapeDtypeStruct((2, *tile), f32),
        ),
        in_specs=[vmem(), vmem()],
        out_specs=(vmem(), vmem(), vmem(), vmem()),
        scratch_shapes=[
            pltpu.VMEM((ndata, *own.shape), f32),
            pltpu.VMEM((whole, size), f32),
            dma((2, ncols)),
            dma((2, 2, ndata)),
            dma((2, ndata)),
            *ring_scratch(part.shape),
            pltpu.VMEM((packed, lanes), f32),
            pltpu.VMEM((half, lanes), f32),
            pltpu.VMEM((half, lanes), f32),
            pltpu.VMEM((ndata, share, lanes), f32),
            pltpu.VMEM((chips, *tile), f32),
            pltpu.VMEM((chips, *tile), f32),
            pltpu.VMEM((chips, 3, *tile), f32),
            pltpu.VMEM((share, lanes), f32),
            pltpu.VMEM((2, 2, *tile), f32),
            dma((2, ndata)),
            dma((2, 3)),
            dma((2, ndata)),
            dma((2, chips)),
            dma((2, chips)),
            dma((2, ndata)),
        ],
        compiler_params=pltpu.CompilerParams(
            collective_id=0, has_side_effects=True, vmem_limit_bytes=40 * 2**20
        ),
        name="sketch",
    )(own, part)


def project_kernel(
    scale,
    block,
    width,
    gram_ref,
    rows_ref,
    mine_ref,
    totals_ref,
    coef_ref,
    whole_ref,
    work_ref,
    inverse_ref,
    half_ref,
    basis_ref,
    total_ref,
    half_sems,
    basis_sems,
    own_sem,
    all_ref,
    *sems,
):
    ring = Ring(1, all_ref, *sems)
    greeted = ring.greet(("dp", 1))
    data_at, col_at = lax.axis_index("dp"), lax.axis_index("cols")
    size = basis_ref.shape[0]
    ndata = whole_ref.shape[0] // size
    own_rows = pl.ds(pl.multiple_of(data_at * width, width), width)

    def half_copy(peer, sender):
        return put_copy(
            half_ref.at[peer * width : (peer + 1) * width, :],
            all_ref.at[col_at, own_rows, :],
            half_sems.at[0, peer],
            half_sems.at[1, sender],
            "dp",
            peer,
        )

    def ready(start, end, q):
        half_ref[start:end, :] = q.astype(jnp.bfloat16)
        basis_ref[:, start:end] = q.T.astype(jnp.bfloat16)
        if start == 0:
            greeted()
        for peer in range(start // width, end // width):
            pl.when(peer != data_at)(lambda peer=peer: half_copy(peer, data_at).start())

    along = ndata // 2
    other = lax.rem(data_at + along, ndata)

    def basis_rows(owner):
        return whole_ref.at[pl.ds(pl.multiple_of(owner * size, size), size), :]

    def basis_copy(offset, rows, source, peer):
        return put_copy(
            source, rows, basis_sems.at[0, offset], basis_sems.at[1, offset], "dp", peer
        )

    def x_copy(offset, owner, source):
        peer = data_at // along * along + lax.rem(data_at + offset, along)
        at = offset if source is basis_ref else along + offset
        return basis_copy(at, basis_rows(owner), source, peer)

    def own_x_copy(offset):
        return x_copy(offset, data_at, basis_ref)

    def other_x_copy(offset):
        return x_copy(offset, other, basis_rows(other))

    own_copy = pltpu.make_async_copy(basis_ref, basis_rows(data_at), own_sem)
    other_copy = basis_copy(0, basis_rows(data_at), basis_ref, other)

    def begun():
        other_copy.start()
        for offset in range(1, along):
            own_x_copy(offset).start()
        own_copy.start()

    def later():
        other_copy.wait_recv()
        for offset in range(1, along):
            other_x_copy(offset).start()

    def work(slots):
        total_ref[...] += block_sums(all_ref, mine_ref, slots, slots, block, width, True)

    factor_steps(gram_ref, rows_ref, work_ref, inverse_ref, ready)
    all_ref[col_at, own_rows, :] = half_ref[own_rows, :]
    total_ref[...] = jnp.zeros_like(total_ref)
    for peer in range(ndata):
        pl.when(peer != data_at)(lambda peer=peer: half_copy(peer, peer).wait())
    ring.begin()
    ring.run(work, {0: begun, 6: later})
    factor = scale * jnp.sum(totals_ref[1]) / jnp.sum(totals_ref[0])
    for g in range(total_ref.shape[0] // width):
        coef_ref[:, g * size : (g + 1) * size] = factor * total_ref[g * width : (g + 1) * width, :]
    other_copy.wait_send()
    for offset in range(1, along):
        own_x_copy(offset).wait()
        other_x_copy(offset).wait()
    own_copy.wait()


def project(gram, rows, mine, totals, scale, block, width):
    ndata = lax.axis_size("dp")
    whole, size = rows.shape
    dma = pltpu.SemaphoreType.DMA
    return pl.pallas_call(
        functools.partial(project_kernel, scale, block, width),
        out_shape=(
            jax.ShapeDtypeStruct((width, block), jnp.float32),
            jax.ShapeDtypeStruct((size * ndata, whole), jnp.bfloat16),
        ),
        in_specs=[vmem(), vmem(), vmem(), vmem()],
        out_specs=(vmem(), pl.BlockSpec(memory_space=pl.ANY)),
        scratch_shapes=[
            pltpu.VMEM((whole, whole), jnp.float32),
            pltpu.VMEM((whole, whole), jnp.float32),
            pltpu.VMEM((whole, size), jnp.bfloat16),
            pltpu.VMEM((size, whole), jnp.bfloat16),
            pltpu.VMEM((whole, size), jnp.float32),
            dma((2, ndata)),
            dma((2, ndata)),
            dma,
            *ring_scratch((whole, size)),
        ],
        compiler_params=pltpu.CompilerParams(
            collective_id=1, has_side_effects=True, vmem_limit_bytes=40 * 2**20
        ),
        name="project",
    )(gram, rows, mine, totals)


def shards(prefix_ids, suffix_ids, weights, counts, omega):
    ncols = lax.axis_size("cols")
    ndata = lax.axis_size("dp")
    block, width = omega.shape
    slots = prefix_ids.shape[-1]
    chunk = width // ndata
    size = block // ndata
    data_at = lax.axis_index("dp")

    live = lax.broadcasted_iota(jnp.int32, (ncols, slots), 1) < counts.reshape(ncols, 1)
    live_weights = jnp.where(live, weights.reshape(ncols, slots), 0.0)
    prefix_local = prefix_ids.reshape(ncols, slots) & (block - 1)
    suffix_local = suffix_ids.reshape(ncols, slots) & (block - 1)
    packed = prefix_local * block + suffix_local
    own = jnp.stack([packed.astype(jnp.float32), live_weights], axis=1)
    part = lax.dynamic_slice_in_dim(omega, data_at * chunk, chunk, 1)
    part = part.reshape(ndata, size, chunk).swapaxes(1, 2).reshape(ndata * chunk, size)
    mine, rows, gram, totals = sketch_and_gram(own, part, block, chunk)
    scale = math.sqrt(block * ncols)
    rows = rows.reshape(width, size)
    coefficients, q_block = project(gram, rows, mine, totals, scale, block, chunk)
    basis = scale * q_block.astype(jnp.float32)
    return (basis, coefficients)


def solution(mesh):
    placed = (
        P("dp", "cols", None, None),
        P("dp", "cols", None, None),
        P("dp", "cols", None, None),
        P("dp", "cols", None),
        P("cols", None),
    )
    return jax.shard_map(
        shards,
        mesh=mesh,
        in_specs=placed,
        out_specs=(P("cols", None), P("dp", "cols")),
        check_vma=False,
    )
```

```python
import functools
import math

import jax
import jax.numpy as jnp
from jax import lax
from jax.experimental import pallas as pl
from jax.experimental.pallas import tpu as pltpu
from jax.sharding import PartitionSpec as P

HIGHEST = lax.Precision.HIGHEST


def dot_exact(a, b, dims):
    return lax.dot_general(
        a, b, (dims, ((), ())), precision=HIGHEST, preferred_element_type=jnp.float32
    )


def one_hot(ids, size):
    rows = lax.broadcasted_iota(jnp.int32, (size, ids.shape[1]), 0)
    return jnp.where(rows == ids, 1.0, 0.0).astype(jnp.bfloat16)


def weighted_rows(table, take, put, weight, width):
    size = table.shape[1]
    groups = table.shape[0] // width
    shift = size.bit_length() - 1
    beside = functools.partial(jnp.concatenate, axis=1)
    picked = jnp.dot(
        table,
        beside([one_hot(ids & (size - 1), size) for ids in take]),
        preferred_element_type=jnp.float32,
    )
    take_group = beside([lax.shift_right_logical(ids, shift) for ids in take])
    put_group = beside([lax.shift_right_logical(ids, shift) for ids in put])
    row = picked[:width]
    for g in range(1, groups):
        row = jnp.where(take_group == g, picked[g * width : (g + 1) * width], row)
    row = beside(weight) * row
    placed = jnp.concatenate(
        [jnp.where(put_group == g, row, 0.0).astype(jnp.bfloat16) for g in range(groups)], axis=0
    )
    return placed, beside([one_hot(ids & (size - 1), size) for ids in put])


def vmem():
    return pl.BlockSpec(memory_space=pltpu.VMEM)


def put_copy(src, dst, send, recv, axis, peer):
    return pltpu.make_async_remote_copy(
        src_ref=src,
        dst_ref=dst,
        send_sem=send,
        recv_sem=recv,
        device_id={axis: peer},
        device_id_type=pl.DeviceIdType.MESH,
    )


def over_peers(axis, act, stride=1):
    count = lax.axis_size(axis)
    me = lax.axis_index(axis)

    def one(offset, carry):
        act(offset, lax.rem(me + stride * offset, count))
        return carry

    lax.fori_loop(1, count // stride, one, 0)


def signal(barrier, axis, peer):
    pl.semaphore_signal(
        barrier, inc=1, device_id={axis: peer}, device_id_type=pl.DeviceIdType.MESH
    )


def greet(*groups, near=(), plane=()):
    barrier = pltpu.get_barrier_semaphore()
    for peer in near:
        signal(barrier, "cols", peer)
    for axis, stride in groups:
        over_peers(axis, lambda offset, peer, axis=axis: signal(barrier, axis, peer), stride)
    for device in plane:
        pl.semaphore_signal(
            barrier, inc=1, device_id=device, device_id_type=pl.DeviceIdType.MESH
        )
    count = sum(lax.axis_size(axis) // stride - 1 for axis, stride in groups)
    return lambda: pl.semaphore_wait(barrier, count + len(near) + len(plane))


def lower_blocks(width, lanes):
    return [(i, j) for i in range(width // lanes) for j in range(i + 1)]


def rows_at(start, count):
    return pl.ds(pl.multiple_of(start, 8), count)


def gram_steps(
    total_ref,
    mine_ref,
    rows_ref,
    gram_ref,
    totals_ref,
    part_ref,
    half_ref,
    other_ref,
    got_ref,
    plane_ref,
    own_ref,
    sum_ref,
    rows_sems,
    pair_sems,
    part_sems,
    plane_sems,
    gram_sems,
):
    data_at, col_at = lax.axis_index("dp"), lax.axis_index("cols")
    core, y, z = lax.rem(col_at, 2), lax.rem(col_at // 2, 2), col_at // 4
    pair = col_at + 1 - 2 * core
    across = col_at + 2 - 4 * y
    ndata, chunk, size = rows_ref.shape
    width = ndata * chunk
    lanes = part_ref.shape[1]
    half = half_ref.shape[0]
    share = own_ref.shape[0]
    spots = 2 * ndata
    spot = 2 * data_at + y

    def over_plane(act):
        def one(offset, carry):
            to = lax.rem(spot + offset, spots)
            act(offset, to, {"dp": to // 2, "cols": z * 4 + lax.rem(to, 2) * 2 + core})
            return carry

        lax.fori_loop(1, spots, one, 0)

    def copy_to(src, dst, sems, at, device):
        return pltpu.make_async_remote_copy(
            src_ref=src,
            dst_ref=dst,
            send_sem=sems.at[0, at],
            recv_sem=sems.at[1, at],
            device_id=device,
            device_id_type=pl.DeviceIdType.MESH,
        )

    def rows_copy(offset, peer):
        return put_copy(
            total_ref.at[rows_at(peer * chunk, chunk), :],
            rows_ref.at[data_at],
            rows_sems.at[0, offset],
            rows_sems.at[1, offset],
            "dp",
            peer,
        )

    over_peers("dp", lambda offset, peer: rows_copy(offset, peer).start())
    rows_ref[data_at] = total_ref[rows_at(data_at * chunk, chunk), :]
    weight = mine_ref[:, :, 1, :]
    for at, term in ((0, weight), (1, (weight > 0.0).astype(jnp.float32))):
        term = jnp.sum(term, axis=0).reshape(-1, *totals_ref.shape[1:])
        sum_ref[0, at] = jnp.sum(term, axis=0)
    sums_copy = put_copy(
        sum_ref.at[0], sum_ref.at[1], pair_sems.at[0, 0], pair_sems.at[1, 0], "cols", pair
    )
    sums_copy.start()
    over_peers("dp", lambda offset, peer: rows_copy(offset, peer).wait())
    rows = rows_ref[...].reshape(width, size)
    gram = dot_exact(rows, rows, ((1,), (1,)))
    for at, (i, j) in enumerate(lower_blocks(width, lanes)):
        part_ref[lanes * at : lanes * (at + 1), :] = gram[
            lanes * i : lanes * (i + 1), lanes * j : lanes * (j + 1)
        ]

    pair_copy = put_copy(
        part_ref.at[rows_at((1 - core) * half, half), :],
        other_ref,
        pair_sems.at[0, 1],
        pair_sems.at[1, 1],
        "cols",
        pair,
    )
    pair_copy.start()
    sums_copy.wait()
    sum_ref[0] = sum_ref[0] + sum_ref[1]
    sums_copy = put_copy(
        sum_ref.at[0], sum_ref.at[2], pair_sems.at[0, 3], pair_sems.at[1, 3], "cols", across
    )
    sums_copy.start()
    pair_copy.wait()
    half_ref[...] = part_ref[rows_at(core * half, half), :] + other_ref[...]

    def part_copy(offset, to, device):
        source = half_ref.at[rows_at(to * share, share), :]
        return copy_to(source, got_ref.at[spot], part_sems, offset, device)

    over_plane(lambda *at: part_copy(*at).start())
    got_ref[spot] = half_ref[rows_at(spot * share, share), :]
    sums_copy.wait()
    sums = sum_ref[0] + sum_ref[2]
    over_plane(lambda *at: part_copy(*at).wait())
    plane_ref[z, :share, :] = jnp.sum(got_ref[...], axis=0)
    plane_ref[z, share:, :] = sums.reshape(-1, lanes)

    def plane_copy(offset, peer):
        return put_copy(
            plane_ref.at[z],
            plane_ref.at[z],
            plane_sems.at[0, offset],
            plane_sems.at[1, offset],
            "cols",
            peer,
        )

    over_peers("cols", lambda offset, peer: plane_copy(offset, peer).start(), 4)
    over_peers("cols", lambda offset, peer: plane_copy(offset, peer).wait(), 4)
    own_ref[...] = jnp.sum(plane_ref[:, :share, :], axis=0)
    own_rows = rows_at((core * spots + spot) * share, share)

    def gram_copy(offset, to, device):
        return copy_to(own_ref, gram_ref.at[own_rows, :], gram_sems, offset, device)

    over_plane(lambda *at: gram_copy(*at).start())
    gram_ref[own_rows, :] = own_ref[...]
    totals_ref[...] = jnp.sum(plane_ref[:, share:, :], axis=0).reshape(totals_ref.shape)
    over_plane(lambda *at: gram_copy(*at).wait())
    own_half = gram_ref.at[rows_at(core * half, half), :]
    last_copy = put_copy(
        own_half, own_half, pair_sems.at[0, 2], pair_sems.at[1, 2], "cols", pair
    )
    last_copy.start()
    last_copy.wait()


def corner_inverse(tile, pivots=8):
    n = tile.shape[0]
    blocks = n // pivots

    def full(x):
        return jnp.broadcast_to(x, (pivots, n))

    work = [tile[pivots * i : pivots * (i + 1), :] for i in range(blocks)]
    lane = lax.broadcasted_iota(jnp.int32, (pivots, n), 1)
    sub = lax.broadcasted_iota(jnp.int32, (pivots, n), 0)
    done = []
    for at in range(blocks):
        start = at * pivots
        group = (lane >= start) & (lane < start + pivots)
        cols = [full(work[at][:, start + c : start + c + 1]) for c in range(pivots)]
        left = [[full(cols[c][r : r + 1, :]) for c in range(r + 1)] for r in range(pivots)]
        rows = [
            jnp.where(group, jnp.where(lane == start + r, 1.0, 0.0), full(work[at][r : r + 1, :]))
            for r in range(pivots)
        ]
        recip = [None] * pivots
        low = [[None] * pivots for _ in range(pivots)]
        for c in range(pivots):
            recip[c] = 1.0 / left[c][c]
            for r in range(c + 1, pivots):
                low[r][c] = left[r][c] * recip[c]
                for e in range(c + 1, r + 1):
                    left[r][e] = left[r][e] - (left[r][c] * left[e][c]) * recip[c]
        for r in range(pivots):
            for c in range(r):
                rows[r] = rows[r] - low[r][c] * rows[c]
        result = jnp.zeros((pivots, n), jnp.float32)
        for r in range(pivots):
            result = jnp.where(sub == r, rows[r] * lax.rsqrt(left[r][r]), result)
        done.append(jnp.where(lane <= sub + start, result, 0.0))
        back = [rows[r] * recip[r] for r in range(pivots)]
        for r in range(pivots - 1, -1, -1):
            for c in range(r):
                back[c] = back[c] - low[r][c] * back[r]
        for i in range(at + 1, blocks):
            rest = jnp.where(group, 0.0, work[i])
            for c in range(pivots):
                rest = rest - full(work[i][:, start + c : start + c + 1]) * back[c]
            work[i] = rest
    return jnp.concatenate(done, axis=0)


def factor_steps(gram_ref, rows_ref, work_ref, inverse_ref, ready):
    n = work_ref.shape[0]
    size = gram_ref.shape[1]
    for at, (i, j) in enumerate(lower_blocks(n, size)):
        work_ref[size * i : size * (i + 1), size * j : size * (j + 1)] = gram_ref[
            size * at : size * (at + 1), :
        ]
    for start in range(0, n, size):
        end = start + size
        corner = corner_inverse(work_ref[start:end, start:end])
        if start:
            inverse_ref[start:end, :start] = dot_exact(
                corner, inverse_ref[start:end, :start], ((1,), (0,))
            )
        inverse_ref[start:end, start:end] = corner
        if end < n:
            low = dot_exact(work_ref[end:, start:end], corner, ((1,), (1,)))
            work_ref[end:, end:] -= dot_exact(low, low, ((1,), (1,)))
            if start:
                inverse_ref[end:, :start] -= dot_exact(
                    low, inverse_ref[start:end, :start], ((1,), (0,))
                )
            inverse_ref[end:, start:end] = -dot_exact(low, corner, ((1,), (0,)))
        ready(start, end, dot_exact(inverse_ref[start:end, :end], rows_ref[:end, :], ((1,), (0,))))


class Ring:
    ARRIVALS = 15
    RING = (0, 1, 3, 4, 5, 7, 8, 11)
    CROSS = (1, 5, 9)

    def __init__(self, lead, all_ref, got_sems, ring_sems, pair_sems, cross_sems):
        self.lead = lead
        self.all_ref, self.got_sems = all_ref, got_sems
        self.ring_sems, self.pair_sems, self.cross_sems = ring_sems, pair_sems, cross_sems
        at = lax.axis_index("cols")
        self.length = lax.axis_size("cols") // 4
        assert self.length == 8
        self.z, quad = at // 4, lax.rem(at, 4)
        self.y, self.core = quad // 2, lax.rem(quad, 2)
        self.way = 1 - 2 * self.core
        self.own = at
        self.pair = self.device(0, 0, 1)
        self.across = self.device(0, 1, 0)
        self.after = self.device(-1, 0, 0)
        self.before = self.device(1, 0, 0)
        self.diagonal = self.device(0, 1, 1)

    def device(self, away, row, core, mirror=False):
        way = -self.way if mirror else self.way
        z = lax.rem(self.z - way * away + self.length, self.length)
        y = lax.rem(self.y + row, 2)
        core = lax.rem(self.core + core + (1 if mirror else 0), 2)
        return z * 4 + y * 2 + core

    def place(self, n):
        return n + n // 13

    def slot(self, m, mirror=False):
        turn = lax.rem(m, 4)
        away = m // 4 + 1 - (turn // 2 - turn // 3)
        return self.device(away, turn // 2, lax.rem((turn + 1) // 2, 2), mirror)

    def greet(self, *groups):
        return greet(*groups, near=(self.pair, self.across, self.after, self.before))

    def copy(self, slot, send, peer):
        part = self.all_ref.at[slot]
        return put_copy(part, part, send, self.got_sems.at[slot], "cols", peer)

    def arrived(self, slot):
        self.copy(slot, self.cross_sems.at[0], self.pair).wait_recv()

    def to_ring(self, slot, at):
        self.copy(slot, self.ring_sems.at[at], self.after).start()

    def to_pair(self, slot, at):
        self.copy(slot, self.pair_sems.at[at], self.pair).start()

    def to_across(self, slot, at):
        self.copy(slot, self.cross_sems.at[at], self.across).start()

    def hand_on(self, n):
        m = self.place(n)
        slot = self.slot(m)
        self.arrived(slot)
        turn, step = lax.rem(m, 4), m // 4 + 1

        @pl.when(((turn == 1) & (step < 3)) | ((turn != 1) & (turn != 2) & (step < 4)))
        def _():
            self.to_ring(slot, m + 3)

        @pl.when(turn == 1)
        def _():
            self.to_across(slot, m)

        @pl.when(m != 2)
        def _():
            self.to_pair(slot, n + 1)

    def begin(self, *between):
        first, second, third = between or [lambda: None] * 3
        self.to_pair(self.own, 0)
        self.to_ring(self.own, 0)
        self.to_across(self.own, 0)
        first()
        self.arrived(self.pair)
        self.to_ring(self.pair, 1)
        second()
        self.arrived(self.across)
        self.to_ring(self.across, 2)
        self.to_pair(self.across, 3)
        self.hand_on(0)
        third()

        def early(n, carry):
            self.hand_on(n)
            return carry

        lax.fori_loop(1, self.lead, early, 0)

    def run(self, work, also):
        work([self.own, self.pair])
        last = self.ARRIVALS - 1

        def one(n, carry):
            for at, act in also.items():
                pl.when(n == at)(act)

            @pl.when(n + self.lead <= last)
            def _():
                self.hand_on(n + self.lead)

            m = self.place(n)
            mirrored = self.slot(m, mirror=True)

            @pl.when(m != 2)
            def _():
                self.arrived(mirrored)

            work([self.slot(m), mirrored])
            return carry

        lax.fori_loop(0, self.ARRIVALS, one, 0)
        for at in [0, 1, 2, *(m + 3 for m in self.RING)]:
            self.copy(self.own, self.ring_sems.at[at], self.after).wait_send()
        for at in [0, *self.CROSS]:
            self.copy(self.own, self.cross_sems.at[at], self.across).wait_send()

        def sent(at, carry):
            self.copy(self.own, self.pair_sems.at[at], self.pair).wait_send()
            return carry

        lax.fori_loop(0, self.ARRIVALS + 1, sent, 0)


def ring_scratch(table):
    dma = pltpu.SemaphoreType.DMA
    ncols = lax.axis_size("cols")
    return [
        pltpu.VMEM((ncols, *table), jnp.bfloat16),
        dma((ncols,)),
        dma((Ring.RING[-1] + 4,)),
        dma((Ring.ARRIVALS + 1,)),
        dma((Ring.CROSS[-1] + 1,)),
    ]


def block_sums(all_ref, records_ref, slots, places, block, width, by_prefix):
    shift = block.bit_length() - 1
    rows = range(records_ref.shape[0])
    placed, spots = [], []
    for slot, place in zip(slots, places):
        packed = [records_ref[d, place, 0:1, :].astype(jnp.int32) for d in rows]
        weight = [records_ref[d, place, 1:2, :] for d in rows]
        prefix = [lax.shift_right_logical(ids, shift) for ids in packed]
        suffix = [ids & (block - 1) for ids in packed]
        take, put = (prefix, suffix) if by_prefix else (suffix, prefix)
        one, spot = weighted_rows(all_ref[slot], take, put, weight, width)
        placed.append(one)
        spots.append(spot)
    return lax.dot_general(
        jnp.concatenate(placed, axis=1),
        jnp.concatenate(spots, axis=1),
        (((1,), (1,)), ((), ())),
        preferred_element_type=jnp.float32,
    )


def sketch_kernel(block, width, own_ref, part_ref, mine_ref, rows_ref, gram_ref, totals_ref, *scratch):
    here_ref, total_ref, col_sems, here_sems, mine_sems, *scratch = scratch
    ring = Ring(2, *scratch[:5])
    data_at, col_at = lax.axis_index("dp"), lax.axis_index("cols")
    ndata = lax.axis_size("dp")
    across = [
        {"dp": lax.rem(data_at + offset, ndata), "cols": ring.across} for offset in range(1, ndata)
    ]
    greet(("cols", 1), ("dp", 1), plane=across)()

    ncols = lax.axis_size("cols")
    near = 12

    def place_at(slot, device):
        return lax.rem(slot - device // 4 * 4 + 4 + ncols, ncols)

    own_place = place_at(col_at, col_at)

    def peer_at(place):
        return lax.rem(col_at // 4 * 4 - 4 + place + ncols, ncols)

    def to_col(place):
        peer = peer_at(place)
        there = place_at(col_at, peer)
        return put_copy(
            own_ref.at[peer],
            here_ref.at[data_at, there],
            col_sems.at[0, place],
            col_sems.at[1, there],
            "cols",
            peer,
        )

    def from_col(place):
        return put_copy(
            own_ref.at[peer_at(place)],
            here_ref.at[data_at, place],
            col_sems.at[0, place],
            col_sems.at[1, place],
            "cols",
            peer_at(place),
        )

    def others(start, end, act):
        def one(place, carry):
            pl.when(place != own_place)(lambda: act(place))
            return carry

        lax.fori_loop(start, end, one, 0)

    def mine_to_data(offset, peer):
        return put_copy(
            own_ref,
            mine_ref.at[data_at],
            mine_sems.at[0, offset],
            mine_sems.at[1, offset],
            "dp",
            peer,
        )

    def here_to_data(group):
        places = pl.ds(0, near) if group == 0 else pl.ds(near, ncols - near)

        def make(offset, peer):
            return put_copy(
                here_ref.at[data_at, places],
                here_ref.at[data_at, places],
                here_sems.at[0, group, offset],
                here_sems.at[1, group, offset],
                "dp",
                peer,
            )

        return make

    def begin_data(group):
        over_peers("dp", lambda offset, peer: here_to_data(group)(offset, peer).start())

    def end_data(group):
        over_peers("dp", lambda offset, peer: here_to_data(group)(offset, peer).wait())

    def first():
        others(0, ncols, lambda place: to_col(place).start())
        here_ref[data_at, own_place] = own_ref[col_at]

    def second():
        others(0, near, lambda place: from_col(place).wait())
        begin_data(0)
        mine_ref[data_at] = own_ref[...]

    def third():
        others(near, ncols, lambda place: from_col(place).wait())
        begin_data(1)

    all_ref = scratch[0]
    all_ref[ring.own] = part_ref[...]
    ring.begin(first, second, third)
    total_ref[...] = jnp.zeros_like(total_ref)
    end_data(0)

    def work(slots):
        places = [place_at(slot, col_at) for slot in slots]
        total_ref[...] += block_sums(all_ref, here_ref, slots, places, block, width, False)

    def begin_mine():
        over_peers("dp", lambda offset, peer: mine_to_data(offset, peer).start())

    ring.run(work, {0: begin_mine, 4: lambda: end_data(1)})
    over_peers("dp", lambda offset, peer: mine_to_data(offset, peer).wait())
    gram_steps(total_ref, mine_ref, rows_ref, gram_ref, totals_ref, *scratch[5:])


def sketch_and_gram(own, part, block, width):
    ndata, ncols = lax.axis_size("dp"), lax.axis_size("cols")
    whole, size = part.shape
    lanes = own.shape[-1]
    f32 = jnp.float32
    packed = len(lower_blocks(whole, lanes)) * lanes
    half = packed // 2
    share = half // (2 * ndata)
    tile = (8, lanes)
    assert share % 8 == 0
    dma = pltpu.SemaphoreType.DMA
    return pl.pallas_call(
        functools.partial(sketch_kernel, block, width),
        out_shape=(
            jax.ShapeDtypeStruct((ndata, *own.shape), f32),
            jax.ShapeDtypeStruct((ndata, width, size), f32),
            jax.ShapeDtypeStruct((packed, lanes), f32),
            jax.ShapeDtypeStruct((2, *tile), f32),
        ),
        in_specs=[vmem(), vmem()],
        out_specs=(vmem(), vmem(), vmem(), vmem()),
        scratch_shapes=[
            pltpu.VMEM((ndata, *own.shape), f32),
            pltpu.VMEM((whole, size), f32),
            dma((2, ncols)),
            dma((2, 2, ndata)),
            dma((2, ndata)),
            *ring_scratch(part.shape),
            pltpu.VMEM((packed, lanes), f32),
            pltpu.VMEM((half, lanes), f32),
            pltpu.VMEM((half, lanes), f32),
            pltpu.VMEM((2 * ndata, share, lanes), f32),
            pltpu.VMEM((ncols // 4, share + 2 * tile[0], lanes), f32),
            pltpu.VMEM((share, lanes), f32),
            pltpu.VMEM((3, 2, *tile), f32),
            dma((2, ndata)),
            dma((2, 4)),
            dma((2, 2 * ndata)),
            dma((2, ncols // 4)),
            dma((2, 2 * ndata)),
        ],
        compiler_params=pltpu.CompilerParams(
            collective_id=0, has_side_effects=True, vmem_limit_bytes=40 * 2**20
        ),
        name="sketch",
    )(own, part)


def project_kernel(
    scale,
    block,
    width,
    gram_ref,
    rows_ref,
    mine_ref,
    totals_ref,
    coef_ref,
    whole_ref,
    work_ref,
    inverse_ref,
    half_ref,
    basis_ref,
    total_ref,
    half_sems,
    basis_sems,
    own_sem,
    all_ref,
    *sems,
):
    ring = Ring(1, all_ref, *sems)
    greeted = ring.greet(("dp", 1))
    data_at, col_at = lax.axis_index("dp"), lax.axis_index("cols")
    size = basis_ref.shape[0]
    ndata = whole_ref.shape[0] // size
    own_rows = pl.ds(pl.multiple_of(data_at * width, width), width)

    def half_copy(peer, sender):
        return put_copy(
            half_ref.at[peer * width : (peer + 1) * width, :],
            all_ref.at[col_at, own_rows, :],
            half_sems.at[0, peer],
            half_sems.at[1, sender],
            "dp",
            peer,
        )

    def ready(start, end, q):
        half_ref[start:end, :] = q.astype(jnp.bfloat16)
        basis_ref[:, start:end] = q.T.astype(jnp.bfloat16)
        if start == 0:
            greeted()
        for peer in range(start // width, end // width):
            pl.when(peer != data_at)(lambda peer=peer: half_copy(peer, data_at).start())

    along = ndata // 2
    other = lax.rem(data_at + along, ndata)

    def basis_rows(owner):
        return whole_ref.at[pl.ds(pl.multiple_of(owner * size, size), size), :]

    def basis_copy(offset, rows, source, peer):
        return put_copy(
            source, rows, basis_sems.at[0, offset], basis_sems.at[1, offset], "dp", peer
        )

    def x_copy(offset, owner, source):
        peer = data_at // along * along + lax.rem(data_at + offset, along)
        at = offset if source is basis_ref else along + offset
        return basis_copy(at, basis_rows(owner), source, peer)

    def own_x_copy(offset):
        return x_copy(offset, data_at, basis_ref)

    def other_x_copy(offset):
        return x_copy(offset, other, basis_rows(other))

    own_copy = pltpu.make_async_copy(basis_ref, basis_rows(data_at), own_sem)
    other_copy = basis_copy(0, basis_rows(data_at), basis_ref, other)

    def begun():
        other_copy.start()
        for offset in range(1, along):
            own_x_copy(offset).start()
        own_copy.start()

    def later():
        other_copy.wait_recv()
        for offset in range(1, along):
            other_x_copy(offset).start()

    def work(slots):
        total_ref[...] += block_sums(all_ref, mine_ref, slots, slots, block, width, True)

    factor_steps(gram_ref, rows_ref, work_ref, inverse_ref, ready)
    all_ref[col_at, own_rows, :] = half_ref[own_rows, :]
    total_ref[...] = jnp.zeros_like(total_ref)
    for peer in range(ndata):
        pl.when(peer != data_at)(lambda peer=peer: half_copy(peer, peer).wait())
    ring.begin()
    ring.run(work, {0: begun, 6: later})
    factor = scale * jnp.sum(totals_ref[1]) / jnp.sum(totals_ref[0])
    for g in range(total_ref.shape[0] // width):
        coef_ref[:, g * size : (g + 1) * size] = factor * total_ref[g * width : (g + 1) * width, :]
    other_copy.wait_send()
    for offset in range(1, along):
        own_x_copy(offset).wait()
        other_x_copy(offset).wait()
    own_copy.wait()


def project(gram, rows, mine, totals, scale, block, width):
    ndata = lax.axis_size("dp")
    whole, size = rows.shape
    dma = pltpu.SemaphoreType.DMA
    return pl.pallas_call(
        functools.partial(project_kernel, scale, block, width),
        out_shape=(
            jax.ShapeDtypeStruct((width, block), jnp.float32),
            jax.ShapeDtypeStruct((size * ndata, whole), jnp.bfloat16),
        ),
        in_specs=[vmem(), vmem(), vmem(), vmem()],
        out_specs=(vmem(), pl.BlockSpec(memory_space=pl.ANY)),
        scratch_shapes=[
            pltpu.VMEM((whole, whole), jnp.float32),
            pltpu.VMEM((whole, whole), jnp.float32),
            pltpu.VMEM((whole, size), jnp.bfloat16),
            pltpu.VMEM((size, whole), jnp.bfloat16),
            pltpu.VMEM((whole, size), jnp.float32),
            dma((2, ndata)),
            dma((2, ndata)),
            dma,
            *ring_scratch((whole, size)),
        ],
        compiler_params=pltpu.CompilerParams(
            collective_id=1, has_side_effects=True, vmem_limit_bytes=40 * 2**20
        ),
        name="project",
    )(gram, rows, mine, totals)


def shards(prefix_ids, suffix_ids, weights, counts, omega):
    ncols = lax.axis_size("cols")
    ndata = lax.axis_size("dp")
    block, width = omega.shape
    slots = prefix_ids.shape[-1]
    chunk = width // ndata
    size = block // ndata
    data_at = lax.axis_index("dp")

    live = lax.broadcasted_iota(jnp.int32, (ncols, slots), 1) < counts.reshape(ncols, 1)
    live_weights = jnp.where(live, weights.reshape(ncols, slots), 0.0)
    prefix_local = prefix_ids.reshape(ncols, slots) & (block - 1)
    suffix_local = suffix_ids.reshape(ncols, slots) & (block - 1)
    packed = prefix_local * block + suffix_local
    own = jnp.stack([packed.astype(jnp.float32), live_weights], axis=1)
    part = lax.dynamic_slice_in_dim(omega, data_at * chunk, chunk, 1)
    part = part.reshape(ndata, size, chunk).swapaxes(1, 2).reshape(ndata * chunk, size)
    mine, rows, gram, totals = sketch_and_gram(own, part, block, chunk)
    scale = math.sqrt(block * ncols)
    rows = rows.reshape(width, size)
    coefficients, q_block = project(gram, rows, mine, totals, scale, block, chunk)
    basis = scale * q_block.astype(jnp.float32)
    return (basis, coefficients)


def solution(mesh):
    placed = (
        P("dp", "cols", None, None),
        P("dp", "cols", None, None),
        P("dp", "cols", None, None),
        P("dp", "cols", None),
        P("cols", None),
    )
    return jax.shard_map(
        shards,
        mesh=mesh,
        in_specs=placed,
        out_specs=(P("cols", None), P("dp", "cols")),
        check_vma=False,
    )
```

```python
import functools
import math

import jax
import jax.numpy as jnp
from jax import lax
from jax.experimental import pallas as pl
from jax.experimental.pallas import tpu as pltpu
from jax.sharding import PartitionSpec as P

HIGHEST = lax.Precision.HIGHEST


def dot_exact(a, b, dims):
    return lax.dot_general(
        a, b, (dims, ((), ())), precision=HIGHEST, preferred_element_type=jnp.float32
    )


def one_hot(ids, size):
    rows = lax.broadcasted_iota(jnp.int32, (size, ids.shape[1]), 0)
    return jnp.where(rows == ids, 1.0, 0.0).astype(jnp.bfloat16)


def weighted_rows(table, take, put, weight, width):
    size = table.shape[1]
    groups = table.shape[0] // width
    shift = size.bit_length() - 1
    beside = functools.partial(jnp.concatenate, axis=1)
    picked = jnp.dot(
        table,
        beside([one_hot(ids & (size - 1), size) for ids in take]),
        preferred_element_type=jnp.float32,
    )
    take_group = beside([lax.shift_right_logical(ids, shift) for ids in take])
    put_group = beside([lax.shift_right_logical(ids, shift) for ids in put])
    row = picked[:width]
    for g in range(1, groups):
        row = jnp.where(take_group == g, picked[g * width : (g + 1) * width], row)
    row = beside(weight) * row
    placed = jnp.concatenate(
        [jnp.where(put_group == g, row, 0.0).astype(jnp.bfloat16) for g in range(groups)], axis=0
    )
    return placed, beside([one_hot(ids & (size - 1), size) for ids in put])


def vmem():
    return pl.BlockSpec(memory_space=pltpu.VMEM)


def put_copy(src, dst, send, recv, axis, peer):
    return pltpu.make_async_remote_copy(
        src_ref=src,
        dst_ref=dst,
        send_sem=send,
        recv_sem=recv,
        device_id={axis: peer},
        device_id_type=pl.DeviceIdType.MESH,
    )


def over_peers(axis, act, stride=1):
    count = lax.axis_size(axis)
    me = lax.axis_index(axis)

    def one(offset, carry):
        act(offset, lax.rem(me + stride * offset, count))
        return carry

    lax.fori_loop(1, count // stride, one, 0)


def signal(barrier, axis, peer):
    pl.semaphore_signal(
        barrier, inc=1, device_id={axis: peer}, device_id_type=pl.DeviceIdType.MESH
    )


def greet(*groups, near=(), plane=()):
    barrier = pltpu.get_barrier_semaphore()
    for peer in near:
        signal(barrier, "cols", peer)
    for axis, stride in groups:
        over_peers(axis, lambda offset, peer, axis=axis: signal(barrier, axis, peer), stride)
    for device in plane:
        pl.semaphore_signal(
            barrier, inc=1, device_id=device, device_id_type=pl.DeviceIdType.MESH
        )
    count = sum(lax.axis_size(axis) // stride - 1 for axis, stride in groups)
    return lambda: pl.semaphore_wait(barrier, count + len(near) + len(plane))


def lower_blocks(width, lanes):
    return [(i, j) for i in range(width // lanes) for j in range(i + 1)]


def rows_at(start, count):
    return pl.ds(pl.multiple_of(start, 8), count)


def gram_steps(
    total_ref,
    mine_ref,
    rows_ref,
    gram_ref,
    totals_ref,
    part_ref,
    half_ref,
    other_ref,
    got_ref,
    plane_ref,
    own_ref,
    sum_ref,
    rows_sems,
    pair_sems,
    part_sems,
    plane_sems,
    gram_sems,
):
    data_at, col_at = lax.axis_index("dp"), lax.axis_index("cols")
    core, y, z = lax.rem(col_at, 2), lax.rem(col_at // 2, 2), col_at // 4
    pair = col_at + 1 - 2 * core
    across = col_at + 2 - 4 * y
    ndata, chunk, size = rows_ref.shape
    width = ndata * chunk
    lanes = part_ref.shape[1]
    half = half_ref.shape[0]
    share = own_ref.shape[0]
    spots = 2 * ndata
    spot = 2 * data_at + y

    def over_plane(act):
        def one(offset, carry):
            to = lax.rem(spot + offset, spots)
            act(offset, to, {"dp": to // 2, "cols": z * 4 + lax.rem(to, 2) * 2 + core})
            return carry

        lax.fori_loop(1, spots, one, 0)

    def copy_to(src, dst, sems, at, device):
        return pltpu.make_async_remote_copy(
            src_ref=src,
            dst_ref=dst,
            send_sem=sems.at[0, at],
            recv_sem=sems.at[1, at],
            device_id=device,
            device_id_type=pl.DeviceIdType.MESH,
        )

    def rows_copy(offset, peer):
        return put_copy(
            total_ref.at[rows_at(peer * chunk, chunk), :],
            rows_ref.at[data_at],
            rows_sems.at[0, offset],
            rows_sems.at[1, offset],
            "dp",
            peer,
        )

    over_peers("dp", lambda offset, peer: rows_copy(offset, peer).start())
    rows_ref[data_at] = total_ref[rows_at(data_at * chunk, chunk), :]
    weight = mine_ref[:, :, 1, :]
    for at, term in ((0, weight), (1, (weight > 0.0).astype(jnp.float32))):
        term = jnp.sum(term, axis=0).reshape(-1, *totals_ref.shape[1:])
        sum_ref[0, at] = jnp.sum(term, axis=0)
    sums_copy = put_copy(
        sum_ref.at[0], sum_ref.at[1], pair_sems.at[0, 0], pair_sems.at[1, 0], "cols", pair
    )
    sums_copy.start()
    over_peers("dp", lambda offset, peer: rows_copy(offset, peer).wait())
    rows = rows_ref[...].reshape(width, size)
    gram = dot_exact(rows, rows, ((1,), (1,)))
    for at, (i, j) in enumerate(lower_blocks(width, lanes)):
        part_ref[lanes * at : lanes * (at + 1), :] = gram[
            lanes * i : lanes * (i + 1), lanes * j : lanes * (j + 1)
        ]

    pair_copy = put_copy(
        part_ref.at[rows_at((1 - core) * half, half), :],
        other_ref,
        pair_sems.at[0, 1],
        pair_sems.at[1, 1],
        "cols",
        pair,
    )
    pair_copy.start()
    sums_copy.wait()
    sum_ref[0] = sum_ref[0] + sum_ref[1]
    sums_copy = put_copy(
        sum_ref.at[0], sum_ref.at[2], pair_sems.at[0, 3], pair_sems.at[1, 3], "cols", across
    )
    sums_copy.start()
    pair_copy.wait()
    half_ref[...] = part_ref[rows_at(core * half, half), :] + other_ref[...]

    def part_copy(offset, to, device):
        source = half_ref.at[rows_at(to * share, share), :]
        return copy_to(source, got_ref.at[spot], part_sems, offset, device)

    over_plane(lambda *at: part_copy(*at).start())
    got_ref[spot] = half_ref[rows_at(spot * share, share), :]
    sums_copy.wait()
    sums = sum_ref[0] + sum_ref[2]
    over_plane(lambda *at: part_copy(*at).wait())
    plane_ref[z, :share, :] = jnp.sum(got_ref[...], axis=0)
    plane_ref[z, share:, :] = sums.reshape(-1, lanes)

    def plane_copy(offset, peer):
        return put_copy(
            plane_ref.at[z],
            plane_ref.at[z],
            plane_sems.at[0, offset],
            plane_sems.at[1, offset],
            "cols",
            peer,
        )

    over_peers("cols", lambda offset, peer: plane_copy(offset, peer).start(), 4)
    over_peers("cols", lambda offset, peer: plane_copy(offset, peer).wait(), 4)
    own_ref[...] = jnp.sum(plane_ref[:, :share, :], axis=0)
    own_rows = rows_at((core * spots + spot) * share, share)

    def gram_copy(offset, to, device):
        return copy_to(own_ref, gram_ref.at[own_rows, :], gram_sems, offset, device)

    over_plane(lambda *at: gram_copy(*at).start())
    gram_ref[own_rows, :] = own_ref[...]
    totals_ref[...] = jnp.sum(plane_ref[:, share:, :], axis=0).reshape(totals_ref.shape)
    over_plane(lambda *at: gram_copy(*at).wait())
    own_half = gram_ref.at[rows_at(core * half, half), :]
    last_copy = put_copy(
        own_half, own_half, pair_sems.at[0, 2], pair_sems.at[1, 2], "cols", pair
    )
    last_copy.start()
    last_copy.wait()


def corner_inverse(tile, pivots=8):
    n = tile.shape[0]
    blocks = n // pivots

    def full(x):
        return jnp.broadcast_to(x, (pivots, n))

    work = [tile[pivots * i : pivots * (i + 1), :] for i in range(blocks)]
    lane = lax.broadcasted_iota(jnp.int32, (pivots, n), 1)
    sub = lax.broadcasted_iota(jnp.int32, (pivots, n), 0)
    done = []
    for at in range(blocks):
        start = at * pivots
        group = (lane >= start) & (lane < start + pivots)
        cols = [full(work[at][:, start + c : start + c + 1]) for c in range(pivots)]
        left = [[full(cols[c][r : r + 1, :]) for c in range(r + 1)] for r in range(pivots)]
        rows = [
            jnp.where(group, jnp.where(lane == start + r, 1.0, 0.0), full(work[at][r : r + 1, :]))
            for r in range(pivots)
        ]
        recip = [None] * pivots
        low = [[None] * pivots for _ in range(pivots)]
        for c in range(pivots):
            recip[c] = 1.0 / left[c][c]
            for r in range(c + 1, pivots):
                low[r][c] = left[r][c] * recip[c]
                for e in range(c + 1, r + 1):
                    left[r][e] = left[r][e] - (left[r][c] * left[e][c]) * recip[c]
        for r in range(pivots):
            for c in range(r):
                rows[r] = rows[r] - low[r][c] * rows[c]
        result = jnp.zeros((pivots, n), jnp.float32)
        for r in range(pivots):
            result = jnp.where(sub == r, rows[r] * lax.rsqrt(left[r][r]), result)
        done.append(jnp.where(lane <= sub + start, result, 0.0))
        if at + 1 == blocks:
            break
        back = [rows[r] * recip[r] for r in range(pivots)]

        def columns(i):
            return [full(work[i][:, start + c : start + c + 1]) for c in range(pivots)]

        ahead = columns(at + 1)
        for r in range(pivots):
            for c in range(r):
                ahead[r] = ahead[r] - low[r][c] * ahead[c]
        terms = [ahead[c] * back[c] for c in range(pivots)]
        while len(terms) > 1:
            terms = [terms[c] + terms[c + 1] for c in range(0, len(terms), 2)]
        following = jnp.where(group, 0.0, work[at + 1]) - terms[0]
        for r in range(pivots - 1, -1, -1):
            for c in range(r):
                back[c] = back[c] - low[r][c] * back[r]
        for i in range(at + 2, blocks):
            later = columns(i)
            rest = jnp.where(group, 0.0, work[i])
            for c in range(pivots):
                rest = rest - later[c] * back[c]
            work[i] = rest
        work[at + 1] = following
    return jnp.concatenate(done, axis=0)


def factor_steps(gram_ref, rows_ref, work_ref, inverse_ref, ready):
    n = work_ref.shape[0]
    size = gram_ref.shape[1]
    for at, (i, j) in enumerate(lower_blocks(n, size)):
        work_ref[size * i : size * (i + 1), size * j : size * (j + 1)] = gram_ref[
            size * at : size * (at + 1), :
        ]
    for start in range(0, n, size):
        end = start + size
        corner = corner_inverse(work_ref[start:end, start:end])
        if start:
            inverse_ref[start:end, :start] = dot_exact(
                corner, inverse_ref[start:end, :start], ((1,), (0,))
            )
        inverse_ref[start:end, start:end] = corner
        if end < n:
            low = dot_exact(work_ref[end:, start:end], corner, ((1,), (1,)))
            work_ref[end:, end:] -= dot_exact(low, low, ((1,), (1,)))
            if start:
                inverse_ref[end:, :start] -= dot_exact(
                    low, inverse_ref[start:end, :start], ((1,), (0,))
                )
            inverse_ref[end:, start:end] = -dot_exact(low, corner, ((1,), (0,)))
        ready(start, end, dot_exact(inverse_ref[start:end, :end], rows_ref[:end, :], ((1,), (0,))))


class Ring:
    ARRIVALS = 15
    RING = (0, 1, 3, 4, 5, 7, 8, 11)
    CROSS = (1, 5, 9)

    def __init__(self, lead, all_ref, got_sems, ring_sems, pair_sems, cross_sems):
        self.lead = lead
        self.all_ref, self.got_sems = all_ref, got_sems
        self.ring_sems, self.pair_sems, self.cross_sems = ring_sems, pair_sems, cross_sems
        at = lax.axis_index("cols")
        self.length = lax.axis_size("cols") // 4
        assert self.length == 8
        self.z, quad = at // 4, lax.rem(at, 4)
        self.y, self.core = quad // 2, lax.rem(quad, 2)
        self.way = 1 - 2 * self.core
        self.own = at
        self.pair = self.device(0, 0, 1)
        self.across = self.device(0, 1, 0)
        self.after = self.device(-1, 0, 0)
        self.before = self.device(1, 0, 0)
        self.diagonal = self.device(0, 1, 1)

    def device(self, away, row, core, mirror=False):
        way = -self.way if mirror else self.way
        z = lax.rem(self.z - way * away + self.length, self.length)
        y = lax.rem(self.y + row, 2)
        core = lax.rem(self.core + core + (1 if mirror else 0), 2)
        return z * 4 + y * 2 + core

    def place(self, n):
        return n + n // 13

    def slot(self, m, mirror=False):
        turn = lax.rem(m, 4)
        away = m // 4 + 1 - (turn // 2 - turn // 3)
        return self.device(away, turn // 2, lax.rem((turn + 1) // 2, 2), mirror)

    def greet(self, *groups):
        return greet(*groups, near=(self.pair, self.across, self.after, self.before))

    def copy(self, slot, send, peer):
        part = self.all_ref.at[slot]
        return put_copy(part, part, send, self.got_sems.at[slot], "cols", peer)

    def arrived(self, slot):
        self.copy(slot, self.cross_sems.at[0], self.pair).wait_recv()

    def to_ring(self, slot, at):
        self.copy(slot, self.ring_sems.at[at], self.after).start()

    def to_pair(self, slot, at):
        self.copy(slot, self.pair_sems.at[at], self.pair).start()

    def to_across(self, slot, at):
        self.copy(slot, self.cross_sems.at[at], self.across).start()

    def hand_on(self, n):
        m = self.place(n)
        slot = self.slot(m)
        self.arrived(slot)
        turn, step = lax.rem(m, 4), m // 4 + 1

        @pl.when(((turn == 1) & (step < 3)) | ((turn != 1) & (turn != 2) & (step < 4)))
        def _():
            self.to_ring(slot, m + 3)

        @pl.when(turn == 1)
        def _():
            self.to_across(slot, m)

        @pl.when(m != 2)
        def _():
            self.to_pair(slot, n + 1)

    def begin(self, *between):
        first, second, third = between or [lambda: None] * 3
        self.to_pair(self.own, 0)
        self.to_ring(self.own, 0)
        self.to_across(self.own, 0)
        first()
        self.arrived(self.pair)
        self.to_ring(self.pair, 1)
        second()
        self.arrived(self.across)
        self.to_ring(self.across, 2)
        self.to_pair(self.across, 3)
        self.hand_on(0)
        third()

        def early(n, carry):
            self.hand_on(n)
            return carry

        lax.fori_loop(1, self.lead, early, 0)

    def run(self, work, also):
        work([self.own, self.pair])
        last = self.ARRIVALS - 1

        def one(n, carry):
            for at, act in also.items():
                pl.when(n == at)(act)

            @pl.when(n + self.lead <= last)
            def _():
                self.hand_on(n + self.lead)

            m = self.place(n)
            mirrored = self.slot(m, mirror=True)

            @pl.when(m != 2)
            def _():
                self.arrived(mirrored)

            work([self.slot(m), mirrored])
            return carry

        lax.fori_loop(0, self.ARRIVALS, one, 0)
        for at in [0, 1, 2, *(m + 3 for m in self.RING)]:
            self.copy(self.own, self.ring_sems.at[at], self.after).wait_send()
        for at in [0, *self.CROSS]:
            self.copy(self.own, self.cross_sems.at[at], self.across).wait_send()

        def sent(at, carry):
            self.copy(self.own, self.pair_sems.at[at], self.pair).wait_send()
            return carry

        lax.fori_loop(0, self.ARRIVALS + 1, sent, 0)


def ring_scratch(table):
    dma = pltpu.SemaphoreType.DMA
    ncols = lax.axis_size("cols")
    return [
        pltpu.VMEM((ncols, *table), jnp.bfloat16),
        dma((ncols,)),
        dma((Ring.RING[-1] + 4,)),
        dma((Ring.ARRIVALS + 1,)),
        dma((Ring.CROSS[-1] + 1,)),
    ]


def block_sums(all_ref, records_ref, slots, places, block, width, by_prefix):
    shift = block.bit_length() - 1
    rows = range(records_ref.shape[0])
    placed, spots = [], []
    for slot, place in zip(slots, places):
        packed = [records_ref[d, place, 0:1, :].astype(jnp.int32) for d in rows]
        weight = [records_ref[d, place, 1:2, :] for d in rows]
        prefix = [lax.shift_right_logical(ids, shift) for ids in packed]
        suffix = [ids & (block - 1) for ids in packed]
        take, put = (prefix, suffix) if by_prefix else (suffix, prefix)
        one, spot = weighted_rows(all_ref[slot], take, put, weight, width)
        placed.append(one)
        spots.append(spot)
    return lax.dot_general(
        jnp.concatenate(placed, axis=1),
        jnp.concatenate(spots, axis=1),
        (((1,), (1,)), ((), ())),
        preferred_element_type=jnp.float32,
    )


def sketch_kernel(block, width, own_ref, part_ref, mine_ref, rows_ref, gram_ref, totals_ref, *scratch):
    here_ref, total_ref, col_sems, here_sems, mine_sems, *scratch = scratch
    ring = Ring(2, *scratch[:5])
    data_at, col_at = lax.axis_index("dp"), lax.axis_index("cols")
    ndata = lax.axis_size("dp")
    across = [
        {"dp": lax.rem(data_at + offset, ndata), "cols": ring.across} for offset in range(1, ndata)
    ]
    greet(("cols", 1), ("dp", 1), plane=across)()

    ncols = lax.axis_size("cols")
    near = 12

    def place_at(slot, device):
        return lax.rem(slot - device // 4 * 4 + 4 + ncols, ncols)

    own_place = place_at(col_at, col_at)

    def peer_at(place):
        return lax.rem(col_at // 4 * 4 - 4 + place + ncols, ncols)

    def to_col(place):
        peer = peer_at(place)
        there = place_at(col_at, peer)
        return put_copy(
            own_ref.at[peer],
            here_ref.at[data_at, there],
            col_sems.at[0, place],
            col_sems.at[1, there],
            "cols",
            peer,
        )

    def from_col(place):
        return put_copy(
            own_ref.at[peer_at(place)],
            here_ref.at[data_at, place],
            col_sems.at[0, place],
            col_sems.at[1, place],
            "cols",
            peer_at(place),
        )

    def others(start, end, act):
        def one(place, carry):
            pl.when(place != own_place)(lambda: act(place))
            return carry

        lax.fori_loop(start, end, one, 0)

    def mine_to_data(offset, peer):
        return put_copy(
            own_ref,
            mine_ref.at[data_at],
            mine_sems.at[0, offset],
            mine_sems.at[1, offset],
            "dp",
            peer,
        )

    def here_to_data(group):
        places = pl.ds(0, near) if group == 0 else pl.ds(near, ncols - near)

        def make(offset, peer):
            return put_copy(
                here_ref.at[data_at, places],
                here_ref.at[data_at, places],
                here_sems.at[0, group, offset],
                here_sems.at[1, group, offset],
                "dp",
                peer,
            )

        return make

    def begin_data(group):
        over_peers("dp", lambda offset, peer: here_to_data(group)(offset, peer).start())

    def end_data(group):
        over_peers("dp", lambda offset, peer: here_to_data(group)(offset, peer).wait())

    def first():
        others(0, ncols, lambda place: to_col(place).start())
        here_ref[data_at, own_place] = own_ref[col_at]

    def second():
        others(0, near, lambda place: from_col(place).wait())
        begin_data(0)
        mine_ref[data_at] = own_ref[...]

    def third():
        others(near, ncols, lambda place: from_col(place).wait())
        begin_data(1)

    all_ref = scratch[0]
    all_ref[ring.own] = part_ref[...]
    ring.begin(first, second, third)
    total_ref[...] = jnp.zeros_like(total_ref)
    end_data(0)

    def work(slots):
        places = [place_at(slot, col_at) for slot in slots]
        total_ref[...] += block_sums(all_ref, here_ref, slots, places, block, width, False)

    def begin_mine():
        over_peers("dp", lambda offset, peer: mine_to_data(offset, peer).start())

    ring.run(work, {0: begin_mine, 4: lambda: end_data(1)})
    over_peers("dp", lambda offset, peer: mine_to_data(offset, peer).wait())
    gram_steps(total_ref, mine_ref, rows_ref, gram_ref, totals_ref, *scratch[5:])


def sketch_and_gram(own, part, block, width):
    ndata, ncols = lax.axis_size("dp"), lax.axis_size("cols")
    whole, size = part.shape
    lanes = own.shape[-1]
    f32 = jnp.float32
    packed = len(lower_blocks(whole, lanes)) * lanes
    half = packed // 2
    share = half // (2 * ndata)
    tile = (8, lanes)
    assert share % 8 == 0
    dma = pltpu.SemaphoreType.DMA
    return pl.pallas_call(
        functools.partial(sketch_kernel, block, width),
        out_shape=(
            jax.ShapeDtypeStruct((ndata, *own.shape), f32),
            jax.ShapeDtypeStruct((ndata, width, size), f32),
            jax.ShapeDtypeStruct((packed, lanes), f32),
            jax.ShapeDtypeStruct((2, *tile), f32),
        ),
        in_specs=[vmem(), vmem()],
        out_specs=(vmem(), vmem(), vmem(), vmem()),
        scratch_shapes=[
            pltpu.VMEM((ndata, *own.shape), f32),
            pltpu.VMEM((whole, size), f32),
            dma((2, ncols)),
            dma((2, 2, ndata)),
            dma((2, ndata)),
            *ring_scratch(part.shape),
            pltpu.VMEM((packed, lanes), f32),
            pltpu.VMEM((half, lanes), f32),
            pltpu.VMEM((half, lanes), f32),
            pltpu.VMEM((2 * ndata, share, lanes), f32),
            pltpu.VMEM((ncols // 4, share + 2 * tile[0], lanes), f32),
            pltpu.VMEM((share, lanes), f32),
            pltpu.VMEM((3, 2, *tile), f32),
            dma((2, ndata)),
            dma((2, 4)),
            dma((2, 2 * ndata)),
            dma((2, ncols // 4)),
            dma((2, 2 * ndata)),
        ],
        compiler_params=pltpu.CompilerParams(
            collective_id=0, has_side_effects=True, vmem_limit_bytes=40 * 2**20
        ),
        name="sketch",
    )(own, part)


def project_kernel(
    scale,
    block,
    width,
    gram_ref,
    rows_ref,
    mine_ref,
    totals_ref,
    coef_ref,
    whole_ref,
    work_ref,
    inverse_ref,
    half_ref,
    basis_ref,
    total_ref,
    half_sems,
    basis_sems,
    own_sem,
    all_ref,
    *sems,
):
    ring = Ring(1, all_ref, *sems)
    greeted = ring.greet(("dp", 1))
    data_at, col_at = lax.axis_index("dp"), lax.axis_index("cols")
    size = basis_ref.shape[0]
    ndata = whole_ref.shape[0] // size
    own_rows = pl.ds(pl.multiple_of(data_at * width, width), width)

    def half_copy(peer, sender):
        return put_copy(
            half_ref.at[peer * width : (peer + 1) * width, :],
            all_ref.at[col_at, own_rows, :],
            half_sems.at[0, peer],
            half_sems.at[1, sender],
            "dp",
            peer,
        )

    def ready(start, end, q):
        half_ref[start:end, :] = q.astype(jnp.bfloat16)
        basis_ref[:, start:end] = q.T.astype(jnp.bfloat16)
        if start == 0:
            greeted()
        for peer in range(start // width, end // width):
            pl.when(peer != data_at)(lambda peer=peer: half_copy(peer, data_at).start())

    along = ndata // 2
    other = lax.rem(data_at + along, ndata)

    def basis_rows(owner):
        return whole_ref.at[pl.ds(pl.multiple_of(owner * size, size), size), :]

    def basis_copy(offset, rows, source, peer):
        return put_copy(
            source, rows, basis_sems.at[0, offset], basis_sems.at[1, offset], "dp", peer
        )

    def x_copy(offset, owner, source):
        peer = data_at // along * along + lax.rem(data_at + offset, along)
        at = offset if source is basis_ref else along + offset
        return basis_copy(at, basis_rows(owner), source, peer)

    def own_x_copy(offset):
        return x_copy(offset, data_at, basis_ref)

    def other_x_copy(offset):
        return x_copy(offset, other, basis_rows(other))

    own_copy = pltpu.make_async_copy(basis_ref, basis_rows(data_at), own_sem)
    other_copy = basis_copy(0, basis_rows(data_at), basis_ref, other)

    def begun():
        other_copy.start()
        for offset in range(1, along):
            own_x_copy(offset).start()
        own_copy.start()

    def later():
        other_copy.wait_recv()
        for offset in range(1, along):
            other_x_copy(offset).start()

    def work(slots):
        total_ref[...] += block_sums(all_ref, mine_ref, slots, slots, block, width, True)

    factor_steps(gram_ref, rows_ref, work_ref, inverse_ref, ready)
    all_ref[col_at, own_rows, :] = half_ref[own_rows, :]
    total_ref[...] = jnp.zeros_like(total_ref)
    for peer in range(ndata):
        pl.when(peer != data_at)(lambda peer=peer: half_copy(peer, peer).wait())
    ring.begin()
    ring.run(work, {0: begun, 6: later})
    factor = scale * jnp.sum(totals_ref[1]) / jnp.sum(totals_ref[0])
    for g in range(total_ref.shape[0] // width):
        coef_ref[:, g * size : (g + 1) * size] = factor * total_ref[g * width : (g + 1) * width, :]
    other_copy.wait_send()
    for offset in range(1, along):
        own_x_copy(offset).wait()
        other_x_copy(offset).wait()
    own_copy.wait()


def project(gram, rows, mine, totals, scale, block, width):
    ndata = lax.axis_size("dp")
    whole, size = rows.shape
    dma = pltpu.SemaphoreType.DMA
    return pl.pallas_call(
        functools.partial(project_kernel, scale, block, width),
        out_shape=(
            jax.ShapeDtypeStruct((width, block), jnp.float32),
            jax.ShapeDtypeStruct((size * ndata, whole), jnp.bfloat16),
        ),
        in_specs=[vmem(), vmem(), vmem(), vmem()],
        out_specs=(vmem(), pl.BlockSpec(memory_space=pl.ANY)),
        scratch_shapes=[
            pltpu.VMEM((whole, whole), jnp.float32),
            pltpu.VMEM((whole, whole), jnp.float32),
            pltpu.VMEM((whole, size), jnp.bfloat16),
            pltpu.VMEM((size, whole), jnp.bfloat16),
            pltpu.VMEM((whole, size), jnp.float32),
            dma((2, ndata)),
            dma((2, ndata)),
            dma,
            *ring_scratch((whole, size)),
        ],
        compiler_params=pltpu.CompilerParams(
            collective_id=1, has_side_effects=True, vmem_limit_bytes=40 * 2**20
        ),
        name="project",
    )(gram, rows, mine, totals)


def shards(prefix_ids, suffix_ids, weights, counts, omega):
    ncols = lax.axis_size("cols")
    ndata = lax.axis_size("dp")
    block, width = omega.shape
    slots = prefix_ids.shape[-1]
    chunk = width // ndata
    size = block // ndata
    data_at = lax.axis_index("dp")

    live = lax.broadcasted_iota(jnp.int32, (ncols, slots), 1) < counts.reshape(ncols, 1)
    live_weights = jnp.where(live, weights.reshape(ncols, slots), 0.0)
    prefix_local = prefix_ids.reshape(ncols, slots) & (block - 1)
    suffix_local = suffix_ids.reshape(ncols, slots) & (block - 1)
    packed = prefix_local * block + suffix_local
    own = jnp.stack([packed.astype(jnp.float32), live_weights], axis=1)
    part = lax.dynamic_slice_in_dim(omega, data_at * chunk, chunk, 1)
    part = part.reshape(ndata, size, chunk).swapaxes(1, 2).reshape(ndata * chunk, size)
    mine, rows, gram, totals = sketch_and_gram(own, part, block, chunk)
    scale = math.sqrt(block * ncols)
    rows = rows.reshape(width, size)
    coefficients, q_block = project(gram, rows, mine, totals, scale, block, chunk)
    basis = scale * q_block.astype(jnp.float32)
    return (basis, coefficients)


def solution(mesh):
    placed = (
        P("dp", "cols", None, None),
        P("dp", "cols", None, None),
        P("dp", "cols", None, None),
        P("dp", "cols", None),
        P("cols", None),
    )
    return jax.shard_map(
        shards,
        mesh=mesh,
        in_specs=placed,
        out_specs=(P("cols", None), P("dp", "cols")),
        check_vma=False,
    )
```

```python
import functools
import math

import jax
import jax.numpy as jnp
from jax import lax
from jax.experimental import pallas as pl
from jax.experimental.pallas import tpu as pltpu
from jax.sharding import PartitionSpec as P

HIGHEST = lax.Precision.HIGHEST


def dot_exact(a, b, dims):
    return lax.dot_general(
        a, b, (dims, ((), ())), precision=HIGHEST, preferred_element_type=jnp.float32
    )


def one_hot(ids, size):
    rows = lax.broadcasted_iota(jnp.int32, (size, ids.shape[1]), 0)
    return jnp.where(rows == ids, 1.0, 0.0).astype(jnp.bfloat16)


def weighted_rows(table, take, put, weight, width):
    size = table.shape[1]
    groups = table.shape[0] // width
    shift = size.bit_length() - 1
    beside = functools.partial(jnp.concatenate, axis=1)
    picked = jnp.dot(
        table,
        beside([one_hot(ids & (size - 1), size) for ids in take]),
        preferred_element_type=jnp.float32,
    )
    take_group = beside([lax.shift_right_logical(ids, shift) for ids in take])
    put_group = beside([lax.shift_right_logical(ids, shift) for ids in put])
    row = picked[:width]
    for g in range(1, groups):
        row = jnp.where(take_group == g, picked[g * width : (g + 1) * width], row)
    row = beside(weight) * row
    placed = jnp.concatenate(
        [jnp.where(put_group == g, row, 0.0).astype(jnp.bfloat16) for g in range(groups)], axis=0
    )
    return placed, beside([one_hot(ids & (size - 1), size) for ids in put])


def vmem():
    return pl.BlockSpec(memory_space=pltpu.VMEM)


def put_copy(src, dst, send, recv, axis, peer):
    return pltpu.make_async_remote_copy(
        src_ref=src,
        dst_ref=dst,
        send_sem=send,
        recv_sem=recv,
        device_id={axis: peer},
        device_id_type=pl.DeviceIdType.MESH,
    )


def over_peers(axis, act, stride=1):
    count = lax.axis_size(axis)
    me = lax.axis_index(axis)

    def one(offset, carry):
        act(offset, lax.rem(me + stride * offset, count))
        return carry

    lax.fori_loop(1, count // stride, one, 0)


def signal(barrier, axis, peer):
    pl.semaphore_signal(
        barrier, inc=1, device_id={axis: peer}, device_id_type=pl.DeviceIdType.MESH
    )


def greet(*groups, near=(), plane=()):
    barrier = pltpu.get_barrier_semaphore()
    for peer in near:
        signal(barrier, "cols", peer)
    for axis, stride in groups:
        over_peers(axis, lambda offset, peer, axis=axis: signal(barrier, axis, peer), stride)
    for device in plane:
        pl.semaphore_signal(
            barrier, inc=1, device_id=device, device_id_type=pl.DeviceIdType.MESH
        )
    count = sum(lax.axis_size(axis) // stride - 1 for axis, stride in groups)
    return lambda: pl.semaphore_wait(barrier, count + len(near) + len(plane))


def lower_blocks(width, lanes):
    return [(i, j) for i in range(width // lanes) for j in range(i + 1)]


def rows_at(start, count):
    return pl.ds(pl.multiple_of(start, 8), count)


def gram_steps(
    total_ref,
    mine_ref,
    rows_ref,
    gram_ref,
    totals_ref,
    part_ref,
    half_ref,
    other_ref,
    got_ref,
    plane_ref,
    own_ref,
    sum_ref,
    rows_sems,
    pair_sems,
    part_sems,
    plane_sems,
    gram_sems,
):
    data_at, col_at = lax.axis_index("dp"), lax.axis_index("cols")
    core, y, z = lax.rem(col_at, 2), lax.rem(col_at // 2, 2), col_at // 4
    pair = col_at + 1 - 2 * core
    across = col_at + 2 - 4 * y
    ndata, chunk, size = rows_ref.shape
    width = ndata * chunk
    lanes = part_ref.shape[1]
    half = half_ref.shape[0]
    share = own_ref.shape[0]
    spots = 2 * ndata
    spot = 2 * data_at + y

    def over_plane(act):
        def one(offset, carry):
            to = lax.rem(spot + offset, spots)
            act(offset, to, {"dp": to // 2, "cols": z * 4 + lax.rem(to, 2) * 2 + core})
            return carry

        lax.fori_loop(1, spots, one, 0)

    def copy_to(src, dst, sems, at, device):
        return pltpu.make_async_remote_copy(
            src_ref=src,
            dst_ref=dst,
            send_sem=sems.at[0, at],
            recv_sem=sems.at[1, at],
            device_id=device,
            device_id_type=pl.DeviceIdType.MESH,
        )

    def rows_copy(offset, peer):
        return put_copy(
            total_ref.at[rows_at(peer * chunk, chunk), :],
            rows_ref.at[data_at],
            rows_sems.at[0, offset],
            rows_sems.at[1, offset],
            "dp",
            peer,
        )

    over_peers("dp", lambda offset, peer: rows_copy(offset, peer).start())
    rows_ref[data_at] = total_ref[rows_at(data_at * chunk, chunk), :]
    weight = mine_ref[:, :, 1, :]
    for at, term in ((0, weight), (1, (weight > 0.0).astype(jnp.float32))):
        term = jnp.sum(term, axis=0).reshape(-1, *totals_ref.shape[1:])
        sum_ref[0, at] = jnp.sum(term, axis=0)
    sums_copy = put_copy(
        sum_ref.at[0], sum_ref.at[1], pair_sems.at[0, 0], pair_sems.at[1, 0], "cols", pair
    )
    sums_copy.start()
    over_peers("dp", lambda offset, peer: rows_copy(offset, peer).wait())
    rows = rows_ref[...].reshape(width, size)
    gram = dot_exact(rows, rows, ((1,), (1,)))
    for at, (i, j) in enumerate(lower_blocks(width, lanes)):
        part_ref[lanes * at : lanes * (at + 1), :] = gram[
            lanes * i : lanes * (i + 1), lanes * j : lanes * (j + 1)
        ]

    pair_copy = put_copy(
        part_ref.at[rows_at((1 - core) * half, half), :],
        other_ref,
        pair_sems.at[0, 1],
        pair_sems.at[1, 1],
        "cols",
        pair,
    )
    pair_copy.start()
    sums_copy.wait()
    sum_ref[0] = sum_ref[0] + sum_ref[1]
    sums_copy = put_copy(
        sum_ref.at[0], sum_ref.at[2], pair_sems.at[0, 3], pair_sems.at[1, 3], "cols", across
    )
    sums_copy.start()
    pair_copy.wait()
    half_ref[...] = part_ref[rows_at(core * half, half), :] + other_ref[...]

    def part_copy(offset, to, device):
        source = half_ref.at[rows_at(to * share, share), :]
        return copy_to(source, got_ref.at[spot], part_sems, offset, device)

    over_plane(lambda *at: part_copy(*at).start())
    got_ref[spot] = half_ref[rows_at(spot * share, share), :]
    sums_copy.wait()
    sums = sum_ref[0] + sum_ref[2]
    over_plane(lambda *at: part_copy(*at).wait())
    plane_ref[z, :share, :] = jnp.sum(got_ref[...], axis=0)
    plane_ref[z, share:, :] = sums.reshape(-1, lanes)

    def plane_copy(offset, peer):
        return put_copy(
            plane_ref.at[z],
            plane_ref.at[z],
            plane_sems.at[0, offset],
            plane_sems.at[1, offset],
            "cols",
            peer,
        )

    over_peers("cols", lambda offset, peer: plane_copy(offset, peer).start(), 4)
    over_peers("cols", lambda offset, peer: plane_copy(offset, peer).wait(), 4)
    own_ref[...] = jnp.sum(plane_ref[:, :share, :], axis=0)
    own_rows = rows_at((core * spots + spot) * share, share)

    def gram_copy(offset, to, device):
        return copy_to(own_ref, gram_ref.at[own_rows, :], gram_sems, offset, device)

    over_plane(lambda *at: gram_copy(*at).start())
    gram_ref[own_rows, :] = own_ref[...]
    totals_ref[...] = jnp.sum(plane_ref[:, share:, :], axis=0).reshape(totals_ref.shape)
    over_plane(lambda *at: gram_copy(*at).wait())
    own_half = gram_ref.at[rows_at(core * half, half), :]
    last_copy = put_copy(
        own_half, own_half, pair_sems.at[0, 2], pair_sems.at[1, 2], "cols", pair
    )
    last_copy.start()
    last_copy.wait()


def corner_inverse(tile, pivots=8):
    n = tile.shape[0]
    blocks = n // pivots

    def full(x):
        return jnp.broadcast_to(x, (pivots, n))

    work = [tile[pivots * i : pivots * (i + 1), :] for i in range(blocks)]
    lane = lax.broadcasted_iota(jnp.int32, (pivots, n), 1)
    sub = lax.broadcasted_iota(jnp.int32, (pivots, n), 0)
    done = []
    for at in range(blocks):
        start = at * pivots
        group = (lane >= start) & (lane < start + pivots)
        cols = [full(work[at][:, start + c : start + c + 1]) for c in range(pivots)]
        left = [[full(cols[c][r : r + 1, :]) for c in range(r + 1)] for r in range(pivots)]
        rows = [
            jnp.where(group, jnp.where(lane == start + r, 1.0, 0.0), full(work[at][r : r + 1, :]))
            for r in range(pivots)
        ]
        recip = [None] * pivots
        low = [[None] * pivots for _ in range(pivots)]
        for c in range(pivots):
            recip[c] = 1.0 / left[c][c]
            for r in range(c + 1, pivots):
                low[r][c] = left[r][c] * recip[c]
                for e in range(c + 1, r + 1):
                    left[r][e] = left[r][e] - (left[r][c] * left[e][c]) * recip[c]
        for r in range(pivots):
            for c in range(r):
                rows[r] = rows[r] - low[r][c] * rows[c]
        result = jnp.zeros((pivots, n), jnp.float32)
        for r in range(pivots):
            result = jnp.where(sub == r, rows[r] * lax.rsqrt(left[r][r]), result)
        done.append(jnp.where(lane <= sub + start, result, 0.0))
        if at + 1 == blocks:
            break
        back = [rows[r] * recip[r] for r in range(pivots)]

        def columns(i):
            return [full(work[i][:, start + c : start + c + 1]) for c in range(pivots)]

        ahead = columns(at + 1)
        for r in range(pivots):
            for c in range(r):
                ahead[r] = ahead[r] - low[r][c] * ahead[c]
        terms = [ahead[c] * back[c] for c in range(pivots)]
        while len(terms) > 1:
            terms = [terms[c] + terms[c + 1] for c in range(0, len(terms), 2)]
        following = jnp.where(group, 0.0, work[at + 1]) - terms[0]
        for r in range(pivots - 1, -1, -1):
            for c in range(r):
                back[c] = back[c] - low[r][c] * back[r]
        for i in range(at + 2, blocks):
            later = columns(i)
            rest = jnp.where(group, 0.0, work[i])
            for c in range(pivots):
                rest = rest - later[c] * back[c]
            work[i] = rest
        work[at + 1] = following
    return jnp.concatenate(done, axis=0)


def factor_steps(gram_ref, rows_ref, work_ref, inverse_ref, ready):
    n = work_ref.shape[0]
    size = gram_ref.shape[1]
    for at, (i, j) in enumerate(lower_blocks(n, size)):
        work_ref[size * i : size * (i + 1), size * j : size * (j + 1)] = gram_ref[
            size * at : size * (at + 1), :
        ]
    for start in range(0, n, size):
        end = start + size
        corner = corner_inverse(work_ref[start:end, start:end])
        if start:
            inverse_ref[start:end, :start] = dot_exact(
                corner, inverse_ref[start:end, :start], ((1,), (0,))
            )
        inverse_ref[start:end, start:end] = corner
        if end < n:
            low = dot_exact(work_ref[end:, start:end], corner, ((1,), (1,)))
            work_ref[end:, end:] -= dot_exact(low, low, ((1,), (1,)))
            if start:
                inverse_ref[end:, :start] -= dot_exact(
                    low, inverse_ref[start:end, :start], ((1,), (0,))
                )
            inverse_ref[end:, start:end] = -dot_exact(low, corner, ((1,), (0,)))
        ready(start, end, dot_exact(inverse_ref[start:end, :end], rows_ref[:end, :], ((1,), (0,))))


class Ring:
    ARRIVALS = 15
    RING = (0, 1, 3, 4, 5, 7, 8, 11)
    CROSS = (1, 5, 9)

    def __init__(self, lead, all_ref, got_sems, ring_sems, pair_sems, cross_sems):
        self.lead = lead
        self.all_ref, self.got_sems = all_ref, got_sems
        self.ring_sems, self.pair_sems, self.cross_sems = ring_sems, pair_sems, cross_sems
        at = lax.axis_index("cols")
        self.length = lax.axis_size("cols") // 4
        assert self.length == 8
        self.z, quad = at // 4, lax.rem(at, 4)
        self.y, self.core = quad // 2, lax.rem(quad, 2)
        self.way = 1 - 2 * self.core
        self.own = at
        self.pair = self.device(0, 0, 1)
        self.across = self.device(0, 1, 0)
        self.after = self.device(-1, 0, 0)
        self.before = self.device(1, 0, 0)
        self.diagonal = self.device(0, 1, 1)

    def device(self, away, row, core, mirror=False):
        way = -self.way if mirror else self.way
        z = lax.rem(self.z - way * away + self.length, self.length)
        y = lax.rem(self.y + row, 2)
        core = lax.rem(self.core + core + (1 if mirror else 0), 2)
        return z * 4 + y * 2 + core

    def place(self, n):
        return n + n // 13

    def slot(self, m, mirror=False):
        turn = lax.rem(m, 4)
        away = m // 4 + 1 - (turn // 2 - turn // 3)
        return self.device(away, turn // 2, lax.rem((turn + 1) // 2, 2), mirror)

    def greet(self, *groups):
        return greet(*groups, near=(self.pair, self.across, self.after, self.before))

    def copy(self, slot, send, peer):
        part = self.all_ref.at[slot]
        return put_copy(part, part, send, self.got_sems.at[slot], "cols", peer)

    def arrived(self, slot):
        self.copy(slot, self.cross_sems.at[0], self.pair).wait_recv()

    def to_ring(self, slot, at):
        self.copy(slot, self.ring_sems.at[at], self.after).start()

    def to_pair(self, slot, at):
        self.copy(slot, self.pair_sems.at[at], self.pair).start()

    def to_across(self, slot, at):
        self.copy(slot, self.cross_sems.at[at], self.across).start()

    def hand_on(self, n):
        m = self.place(n)
        slot = self.slot(m)
        self.arrived(slot)
        turn, step = lax.rem(m, 4), m // 4 + 1

        @pl.when(((turn == 1) & (step < 3)) | ((turn != 1) & (turn != 2) & (step < 4)))
        def _():
            self.to_ring(slot, m + 3)

        @pl.when(turn == 1)
        def _():
            self.to_across(slot, m)

        @pl.when(m != 2)
        def _():
            self.to_pair(slot, n + 1)

    def begin(self, *between):
        first, second, third = between or [lambda: None] * 3
        self.to_pair(self.own, 0)
        self.to_ring(self.own, 0)
        self.to_across(self.own, 0)
        first()
        self.arrived(self.pair)
        self.to_ring(self.pair, 1)
        second()
        self.arrived(self.across)
        self.to_ring(self.across, 2)
        self.to_pair(self.across, 3)
        self.hand_on(0)
        third()

        def early(n, carry):
            self.hand_on(n)
            return carry

        lax.fori_loop(1, self.lead, early, 0)

    def run(self, work, also):
        work([self.own, self.pair])
        last = self.ARRIVALS - 1

        def one(n, carry):
            for at, act in also.items():
                pl.when(n == at)(act)

            @pl.when(n + self.lead <= last)
            def _():
                self.hand_on(n + self.lead)

            m = self.place(n)
            mirrored = self.slot(m, mirror=True)

            @pl.when(m != 2)
            def _():
                self.arrived(mirrored)

            work([self.slot(m), mirrored])
            return carry

        lax.fori_loop(0, self.ARRIVALS, one, 0)
        for at in [0, 1, 2, *(m + 3 for m in self.RING)]:
            self.copy(self.own, self.ring_sems.at[at], self.after).wait_send()
        for at in [0, *self.CROSS]:
            self.copy(self.own, self.cross_sems.at[at], self.across).wait_send()

        def sent(at, carry):
            self.copy(self.own, self.pair_sems.at[at], self.pair).wait_send()
            return carry

        lax.fori_loop(0, self.ARRIVALS + 1, sent, 0)


def ring_scratch(table):
    dma = pltpu.SemaphoreType.DMA
    ncols = lax.axis_size("cols")
    return [
        pltpu.VMEM((ncols, *table), jnp.bfloat16),
        dma((ncols,)),
        dma((Ring.RING[-1] + 4,)),
        dma((Ring.ARRIVALS + 1,)),
        dma((Ring.CROSS[-1] + 1,)),
    ]


def block_sums(all_ref, records_ref, slots, places, block, width, by_prefix):
    shift = block.bit_length() - 1
    rows = range(records_ref.shape[0])
    placed, spots = [], []
    for slot, place in zip(slots, places):
        packed = [records_ref[d, place, 0:1, :].astype(jnp.int32) for d in rows]
        weight = [records_ref[d, place, 1:2, :] for d in rows]
        prefix = [lax.shift_right_logical(ids, shift) for ids in packed]
        suffix = [ids & (block - 1) for ids in packed]
        take, put = (prefix, suffix) if by_prefix else (suffix, prefix)
        one, spot = weighted_rows(all_ref[slot], take, put, weight, width)
        placed.append(one)
        spots.append(spot)
    return lax.dot_general(
        jnp.concatenate(placed, axis=1),
        jnp.concatenate(spots, axis=1),
        (((1,), (1,)), ((), ())),
        preferred_element_type=jnp.float32,
    )


def sketch_kernel(block, width, own_ref, part_ref, mine_ref, rows_ref, gram_ref, totals_ref, *scratch):
    here_ref, total_ref, col_sems, here_sems, mine_sems, *scratch = scratch
    ring = Ring(2, *scratch[:5])
    data_at, col_at = lax.axis_index("dp"), lax.axis_index("cols")
    ndata = lax.axis_size("dp")
    across = [
        {"dp": lax.rem(data_at + offset, ndata), "cols": ring.across} for offset in range(1, ndata)
    ]
    greet(("cols", 1), ("dp", 1), plane=across)()

    ncols = lax.axis_size("cols")
    near = 12

    def place_at(slot, device):
        return lax.rem(slot - device // 4 * 4 + 4 + ncols, ncols)

    own_place = place_at(col_at, col_at)

    def peer_at(place):
        return lax.rem(col_at // 4 * 4 - 4 + place + ncols, ncols)

    def to_col(place):
        peer = peer_at(place)
        there = place_at(col_at, peer)
        return put_copy(
            own_ref.at[peer],
            here_ref.at[data_at, there],
            col_sems.at[0, place],
            col_sems.at[1, there],
            "cols",
            peer,
        )

    def from_col(place):
        return put_copy(
            own_ref.at[peer_at(place)],
            here_ref.at[data_at, place],
            col_sems.at[0, place],
            col_sems.at[1, place],
            "cols",
            peer_at(place),
        )

    def others(start, end, act):
        def one(place, carry):
            pl.when(place != own_place)(lambda: act(place))
            return carry

        lax.fori_loop(start, end, one, 0)

    def mine_to_data(offset, peer):
        return put_copy(
            own_ref,
            mine_ref.at[data_at],
            mine_sems.at[0, offset],
            mine_sems.at[1, offset],
            "dp",
            peer,
        )

    def here_to_data(group):
        places = pl.ds(0, near) if group == 0 else pl.ds(near, ncols - near)

        def make(offset, peer):
            return put_copy(
                here_ref.at[data_at, places],
                here_ref.at[data_at, places],
                here_sems.at[0, group, offset],
                here_sems.at[1, group, offset],
                "dp",
                peer,
            )

        return make

    def begin_data(group):
        over_peers("dp", lambda offset, peer: here_to_data(group)(offset, peer).start())

    def end_data(group):
        over_peers("dp", lambda offset, peer: here_to_data(group)(offset, peer).wait())

    def first():
        others(0, ncols, lambda place: to_col(place).start())
        here_ref[data_at, own_place] = own_ref[col_at]

    def second():
        others(0, near, lambda place: from_col(place).wait())
        begin_data(0)
        mine_ref[data_at] = own_ref[...]

    def third():
        others(near, ncols, lambda place: from_col(place).wait())
        begin_data(1)

    all_ref = scratch[0]
    all_ref[ring.own] = part_ref[...]
    ring.begin(first, second, third)
    total_ref[...] = jnp.zeros_like(total_ref)
    end_data(0)

    def work(slots):
        places = [place_at(slot, col_at) for slot in slots]
        total_ref[...] += block_sums(all_ref, here_ref, slots, places, block, width, False)

    def begin_mine():
        over_peers("dp", lambda offset, peer: mine_to_data(offset, peer).start())

    ring.run(work, {0: begin_mine, 4: lambda: end_data(1)})
    over_peers("dp", lambda offset, peer: mine_to_data(offset, peer).wait())
    gram_steps(total_ref, mine_ref, rows_ref, gram_ref, totals_ref, *scratch[5:])


def sketch_and_gram(own, part, block, width):
    ndata, ncols = lax.axis_size("dp"), lax.axis_size("cols")
    whole, size = part.shape
    lanes = own.shape[-1]
    f32 = jnp.float32
    packed = len(lower_blocks(whole, lanes)) * lanes
    half = packed // 2
    share = half // (2 * ndata)
    tile = (8, lanes)
    assert share % 8 == 0
    dma = pltpu.SemaphoreType.DMA
    return pl.pallas_call(
        functools.partial(sketch_kernel, block, width),
        out_shape=(
            jax.ShapeDtypeStruct((ndata, *own.shape), f32),
            jax.ShapeDtypeStruct((ndata, width, size), f32),
            jax.ShapeDtypeStruct((packed, lanes), f32),
            jax.ShapeDtypeStruct((2, *tile), f32),
        ),
        in_specs=[vmem(), vmem()],
        out_specs=(vmem(), vmem(), vmem(), vmem()),
        scratch_shapes=[
            pltpu.VMEM((ndata, *own.shape), f32),
            pltpu.VMEM((whole, size), f32),
            dma((2, ncols)),
            dma((2, 2, ndata)),
            dma((2, ndata)),
            *ring_scratch(part.shape),
            pltpu.VMEM((packed, lanes), f32),
            pltpu.VMEM((half, lanes), f32),
            pltpu.VMEM((half, lanes), f32),
            pltpu.VMEM((2 * ndata, share, lanes), f32),
            pltpu.VMEM((ncols // 4, share + 2 * tile[0], lanes), f32),
            pltpu.VMEM((share, lanes), f32),
            pltpu.VMEM((3, 2, *tile), f32),
            dma((2, ndata)),
            dma((2, 4)),
            dma((2, 2 * ndata)),
            dma((2, ncols // 4)),
            dma((2, 2 * ndata)),
        ],
        compiler_params=pltpu.CompilerParams(
            collective_id=0, has_side_effects=True, vmem_limit_bytes=40 * 2**20
        ),
        name="sketch",
    )(own, part)


def project_kernel(
    scale,
    block,
    width,
    gram_ref,
    rows_ref,
    mine_ref,
    totals_ref,
    coef_ref,
    whole_ref,
    work_ref,
    inverse_ref,
    half_ref,
    basis_ref,
    total_ref,
    half_sems,
    basis_sems,
    own_sem,
    all_ref,
    *sems,
):
    ring = Ring(1, all_ref, *sems)
    greeted = ring.greet(("dp", 1))
    data_at, col_at = lax.axis_index("dp"), lax.axis_index("cols")
    size = basis_ref.shape[0]
    ndata = whole_ref.shape[0] // size
    own_rows = pl.ds(pl.multiple_of(data_at * width, width), width)

    def half_copy(peer, sender):
        return put_copy(
            half_ref.at[peer * width : (peer + 1) * width, :],
            all_ref.at[col_at, own_rows, :],
            half_sems.at[0, peer],
            half_sems.at[1, sender],
            "dp",
            peer,
        )

    def ready(start, end, q):
        half_ref[start:end, :] = q.astype(jnp.bfloat16)
        if start == 0:
            greeted()
        for peer in range(start // width, end // width):
            pl.when(peer != data_at)(lambda peer=peer: half_copy(peer, data_at).start())
        basis_ref[:, start:end] = q.T.astype(jnp.bfloat16)

    along = ndata // 2
    other = lax.rem(data_at + along, ndata)

    def basis_rows(owner):
        return whole_ref.at[pl.ds(pl.multiple_of(owner * size, size), size), :]

    def basis_copy(offset, rows, source, peer):
        return put_copy(
            source, rows, basis_sems.at[0, offset], basis_sems.at[1, offset], "dp", peer
        )

    def x_copy(offset, owner, source):
        peer = data_at // along * along + lax.rem(data_at + offset, along)
        at = offset if source is basis_ref else along + offset
        return basis_copy(at, basis_rows(owner), source, peer)

    def own_x_copy(offset):
        return x_copy(offset, data_at, basis_ref)

    def other_x_copy(offset):
        return x_copy(offset, other, basis_rows(other))

    own_copy = pltpu.make_async_copy(basis_ref, basis_rows(data_at), own_sem)
    other_copy = basis_copy(0, basis_rows(data_at), basis_ref, other)

    def begun():
        other_copy.start()
        for offset in range(1, along):
            own_x_copy(offset).start()
        own_copy.start()

    def later():
        other_copy.wait_recv()
        for offset in range(1, along):
            other_x_copy(offset).start()

    def work(slots):
        total_ref[...] += block_sums(all_ref, mine_ref, slots, slots, block, width, True)

    total_ref[...] = jnp.zeros_like(total_ref)
    factor_steps(gram_ref, rows_ref, work_ref, inverse_ref, ready)
    all_ref[col_at, own_rows, :] = half_ref[own_rows, :]
    for peer in range(ndata):
        pl.when(peer != data_at)(lambda peer=peer: half_copy(peer, peer).wait())
    ring.begin()
    ring.run(work, {0: begun, 6: later})
    factor = scale * jnp.sum(totals_ref[1]) / jnp.sum(totals_ref[0])
    for g in range(total_ref.shape[0] // width):
        coef_ref[:, g * size : (g + 1) * size] = factor * total_ref[g * width : (g + 1) * width, :]
    other_copy.wait_send()
    for offset in range(1, along):
        own_x_copy(offset).wait()
        other_x_copy(offset).wait()
    own_copy.wait()


def project(gram, rows, mine, totals, scale, block, width):
    ndata = lax.axis_size("dp")
    whole, size = rows.shape
    dma = pltpu.SemaphoreType.DMA
    return pl.pallas_call(
        functools.partial(project_kernel, scale, block, width),
        out_shape=(
            jax.ShapeDtypeStruct((width, block), jnp.float32),
            jax.ShapeDtypeStruct((size * ndata, whole), jnp.bfloat16),
        ),
        in_specs=[vmem(), vmem(), vmem(), vmem()],
        out_specs=(vmem(), pl.BlockSpec(memory_space=pl.ANY)),
        scratch_shapes=[
            pltpu.VMEM((whole, whole), jnp.float32),
            pltpu.VMEM((whole, whole), jnp.float32),
            pltpu.VMEM((whole, size), jnp.bfloat16),
            pltpu.VMEM((size, whole), jnp.bfloat16),
            pltpu.VMEM((whole, size), jnp.float32),
            dma((2, ndata)),
            dma((2, ndata)),
            dma,
            *ring_scratch((whole, size)),
        ],
        compiler_params=pltpu.CompilerParams(
            collective_id=1, has_side_effects=True, vmem_limit_bytes=40 * 2**20
        ),
        name="project",
    )(gram, rows, mine, totals)


def shards(prefix_ids, suffix_ids, weights, counts, omega):
    ncols = lax.axis_size("cols")
    ndata = lax.axis_size("dp")
    block, width = omega.shape
    slots = prefix_ids.shape[-1]
    chunk = width // ndata
    size = block // ndata
    data_at = lax.axis_index("dp")

    live = lax.broadcasted_iota(jnp.int32, (ncols, slots), 1) < counts.reshape(ncols, 1)
    live_weights = jnp.where(live, weights.reshape(ncols, slots), 0.0)
    prefix_local = prefix_ids.reshape(ncols, slots) & (block - 1)
    suffix_local = suffix_ids.reshape(ncols, slots) & (block - 1)
    packed = prefix_local * block + suffix_local
    own = jnp.stack([packed.astype(jnp.float32), live_weights], axis=1)
    part = lax.dynamic_slice_in_dim(omega, data_at * chunk, chunk, 1)
    part = part.reshape(ndata, size, chunk).swapaxes(1, 2).reshape(ndata * chunk, size)
    mine, rows, gram, totals = sketch_and_gram(own, part, block, chunk)
    scale = math.sqrt(block * ncols)
    rows = rows.reshape(width, size)
    coefficients, q_block = project(gram, rows, mine, totals, scale, block, chunk)
    basis = scale * q_block.astype(jnp.float32)
    return (basis, coefficients)


def solution(mesh):
    placed = (
        P("dp", "cols", None, None),
        P("dp", "cols", None, None),
        P("dp", "cols", None, None),
        P("dp", "cols", None),
        P("cols", None),
    )
    return jax.shard_map(
        shards,
        mesh=mesh,
        in_specs=placed,
        out_specs=(P("cols", None), P("dp", "cols")),
        check_vma=False,
    )
```
